32 devices in a mesh: tok: 32 (over z, y, x, core).
Axes of the slice: x: 2, y: 2, z: 4, core: 2. Of those that a mesh axis runs over, the one named last changes fastest.
Arguments:
- tokens: bfloat16 [32768, 768], P('tok'), may hold values from -6 to 6
- doc_lengths: int32 [33], replicated, may hold values from 1 to 2047, as said below
- first_gain: bfloat16 [768], P('tok'), may hold values from 0.5 to 1.5
- qkv_weight: bfloat16 [768, 2304], P('tok'), may hold values from -0.21875 to 0.21875
- attn_weight: bfloat16 [768, 768], P('tok'), may hold values from -0.625 to 0.625
- second_gain: bfloat16 [768], P('tok'), may hold values from 0.5 to 1.5
- feed_in_weight: bfloat16 [768, 2304], P('tok'), may hold values from -0.21875 to 0.21875
- feed_out_weight: bfloat16 [1152, 768], P(None, 'tok'), may hold values from -0.1875 to 0.1875
- cotangent: bfloat16 [32768, 768], P('tok'), may hold values from -6 to 6
Outputs:
- block_output: bfloat16 [32768, 768], P('tok')
- input_grad: float32 [32768, 768], P('tok')
- first_gain_grad: float32 [768], P('tok')
- qkv_grad: float32 [768, 2304], P('tok')
- attn_grad: float32 [768, 768], P('tok')
- second_gain_grad: float32 [768], P('tok')
- feed_in_grad: float32 [768, 2304], P('tok')
- feed_out_grad: float32 [1152, 768], P(None, 'tok')
The draws below stay inside these ranges and needn't reach their ends.
Inputs may be any that keep to these rules, and one draw needn't show every extreme that they name: Counting the cumulative sums of doc_lengths from 0, the i-th of the first 32 lies in the interval (i * 1024, (i + 1) * 1024], every length is positive, and the last sum equals 32768.
All inputs are finite; a program needn't handle non-finite values.
Results may differ from the reference program's by a relative error of at most 0.015.
Values may be sent and summed in bfloat16 or wider, within the bound.
No kernel may reach another device: no remote copies, remote signals or barrier semaphores. Data moves between devices by JAX's collectives and lax.ppermute only.
A program may use at most 192 MiB of HBM per device.

```python
import jax
import jax.numpy as jnp
from jax import lax

D = 768
FF = 1152
HEADS = 12
HEAD_DIM = 64
HALF = 64
TOK_DEV = 1024
TOKENS = 32768
NDOCS = 33


def draw_doc_lengths(key, part):
    key = jax.random.fold_in(key, 11)
    device_count = NDOCS - 1
    pick_key, lower_key, upper_key, wide_key, place_key = jax.random.split(key, 5)
    selector = jax.random.randint(pick_key, (device_count,), 0, 4, dtype=jnp.int32)
    near_lower = jax.random.randint(lower_key, (device_count,), 1, HALF + 1, dtype=jnp.int32)
    near_upper = jax.random.randint(upper_key, (device_count,), TOK_DEV - HALF, TOK_DEV + 1, dtype=jnp.int32)
    anywhere = jax.random.randint(wide_key, (device_count,), 1, TOK_DEV + 1, dtype=jnp.int32)
    reach = jnp.where(selector == 0, near_lower, jnp.where(selector == 1, near_upper, anywhere)).astype(jnp.int32)
    first_forced = jax.random.randint(place_key, (), 0, device_count - 4, dtype=jnp.int32)
    index = jnp.arange(device_count, dtype=jnp.int32)
    reach = jnp.where(index == first_forced, TOK_DEV, reach)
    reach = jnp.where(index == first_forced + 1, 1, reach)
    reach = jnp.where(index == first_forced + 2, 1, reach)
    reach = jnp.where(index == first_forced + 3, TOK_DEV, reach)
    reach = jnp.where(index == device_count - 1, jnp.minimum(reach, TOK_DEV - 1), reach).astype(jnp.int32)
    doc_ends = (index * TOK_DEV + reach).astype(jnp.int32)
    doc_ends = jnp.concatenate([doc_ends, jnp.full((1,), TOKENS, dtype=jnp.int32)])
    doc_starts = jnp.concatenate([jnp.zeros((1,), jnp.int32), doc_ends[:-1]])
    return (doc_ends - doc_starts).astype(jnp.int32)


def raised(entries, rng, source, target, shards_of, factor):
    def block_of(axis_at):
        return (jnp.arange(entries.shape[axis_at]) // (entries.shape[axis_at] // shards_of)).reshape((-1,) + (1,) * (entries.ndim - 1 - axis_at))

    first = jax.random.permutation(rng, shards_of)[block_of(target)]
    other_side = (block_of(target) + shards_of // 2) % shards_of
    return jnp.where((block_of(source) == first) | (block_of(source) == other_side), factor * entries, entries)


def levels(key, extent, shards, low, largest):
    level, own = 1.0, jax.random.fold_in(key, 6)
    for dim, parts in shards:
        draws = jnp.exp(jax.random.uniform(jax.random.fold_in(own, dim), (parts,), jnp.float32, low / len(shards), largest / len(shards)))
        level = level * jnp.repeat(draws, extent[dim] // parts).reshape([-1 if axis == dim else 1 for axis in range(len(extent))])
    return level


def bell_draw(rng, dims, width, most, shards=(), held_as=jnp.bfloat16):
    factor_of = levels(rng, dims, shards, -0.22, 0.18) if shards else 1.0
    drawn = jax.random.normal(rng, dims, jnp.float32) * width * factor_of
    return jnp.minimum(jnp.maximum(drawn, -most), most).astype(held_as)


def noise_with(key, extent, width, bound, cuts, heavy, kind=jnp.bfloat16):
    values = width * jax.random.normal(key, extent, jnp.float32)
    if cuts:
        values = values * levels(key, extent, cuts, -0.22, 0.18)
    return jnp.clip(raised(values, jax.random.fold_in(key, 3), *heavy), -bound, bound).astype(kind)


def setup_inputs(seed: int = 0) -> dict:
    key_list = jax.random.split(jax.random.key(seed), 10)
    tokens = bell_draw(key_list[0], (TOKENS, D), 1.0, 6.0, ((0, 32),))
    doc_lengths = draw_doc_lengths(jax.random.fold_in(key_list[9], 71), 0)
    first_gain = jnp.clip(1.0 + 0.1 * jax.random.normal(key_list[2], (D,), jnp.float32), 0.5, 1.5).astype(jnp.bfloat16)
    qkv_weight = bell_draw(key_list[3], (D, 3 * D), D ** -0.5, 0.21875, ((0, 32),))
    attn_weight = bell_draw(key_list[4], (D, D), (D // 8) ** -0.5, 0.625, ((0, 32),))
    second_gain = jnp.clip(1.0 + 0.1 * jax.random.normal(key_list[5], (D,), jnp.float32), 0.5, 1.5).astype(jnp.bfloat16)
    feed_in_weight = bell_draw(key_list[6], (D, 2 * FF), D ** -0.5, 0.21875, ((0, 32),))
    feed_out_weight = bell_draw(key_list[7], (FF, D), FF ** -0.5, 0.1875, ((1, 32),))
    cotangent = noise_with(key_list[8], (TOKENS, D), 1.0, 6.0, ((0, 32),), (0, 1, 32, 2.75))
    return dict(tokens=tokens, doc_lengths=doc_lengths, first_gain=first_gain, qkv_weight=qkv_weight, attn_weight=attn_weight, second_gain=second_gain, feed_in_weight=feed_in_weight, feed_out_weight=feed_out_weight, cotangent=cotangent)


@jax.custom_vjp
def low(v):
    return lax.optimization_barrier(v.astype(jnp.bfloat16)).astype(jnp.float32)

@jax.custom_vjp
def low_back(v):
    return v

def low_keep(v):
    return (low(v), None)

def low_pass(kept, grad):
    return (grad,)

def back_keep(v):
    return (v, None)

def back_low(kept, grad):
    return (low(grad),)
low.defvjp(low_keep, low_pass)
low_back.defvjp(back_keep, back_low)

def layer_norm(values, gains):
    row_mean = lax.optimization_barrier(jnp.mean(values, axis=-1, keepdims=True))
    centered = values - row_mean
    variance = lax.optimization_barrier(jnp.mean(centered * centered, axis=-1, keepdims=True))
    return centered * lax.rsqrt(variance + 1e-05) * gains

def rotary_tables(offsets, head_size):
    frequency = 10000.0 ** (-jnp.arange(0, head_size, 2, dtype=jnp.float32) / head_size)
    angles = offsets.astype(jnp.float32)[:, None] * frequency[None, :]
    angles = jnp.concatenate([angles, angles], axis=-1)
    return (jnp.cos(angles), jnp.sin(angles))

def rotate(values, cosine_table, sine_table):
    half_size = values.shape[-1] // 2
    turned = jnp.concatenate([-values[..., half_size:], values[..., :half_size]], axis=-1)
    return values * cosine_table[:, None, :] + turned * sine_table[:, None, :]

def doc_tables(doc_lengths, positions):
    doc_ends = jnp.cumsum(doc_lengths).astype(jnp.int32)
    token_total = doc_ends[-1]
    passed = doc_ends[None, :] <= positions[:, None]
    segment = lax.optimization_barrier(jnp.sum(passed.astype(jnp.int32), axis=1)).astype(jnp.int32)
    inside = (positions >= 0) & (positions < token_total)
    segment = jnp.where(inside, segment, -1).astype(jnp.int32)
    doc_start = lax.optimization_barrier(jnp.max(jnp.where(passed, doc_ends[None, :], 0), axis=1)).astype(jnp.int32)
    return (segment, (positions - doc_start).astype(jnp.int32))

def matmul(left, right):
    return jnp.dot(left, right, precision=lax.Precision.HIGHEST, preferred_element_type=jnp.float32)

def reference(tokens, doc_lengths, first_gain, qkv_weight, attn_weight, second_gain, feed_in_weight, feed_out_weight, cotangent):
    block_size = min(512, TOK_DEV)
    block_count = TOKENS // block_size
    span_size = block_size + 2 * HALF
    positions = jnp.arange(-HALF, TOKENS + HALF, dtype=jnp.int32)
    segment, offsets = doc_tables(doc_lengths, positions)
    cosine_table, sine_table = rotary_tables(offsets[HALF:HALF + TOKENS], HEAD_DIM)
    row_ids = jnp.arange(block_size, dtype=jnp.int32)[:, None]
    col_ids = jnp.arange(span_size, dtype=jnp.int32)[None, :]
    in_window = jnp.abs(col_ids - HALF - row_ids) <= HALF

    def forward(inputs, gain_one, weight_qkv, weight_attn, gain_two, weight_in, weight_down):
        normed = low(layer_norm(inputs, gain_one))
        merged = low_back(matmul(normed, weight_qkv))
        queries = low(rotate(merged[:, :D].reshape(TOKENS, HEADS, HEAD_DIM), cosine_table, sine_table))
        key_rows = low(rotate(merged[:, D:2 * D].reshape(TOKENS, HEADS, HEAD_DIM), cosine_table, sine_table))
        value_rows = low(merged[:, 2 * D:].reshape(TOKENS, HEADS, HEAD_DIM))
        key_padded = jnp.pad(key_rows, ((HALF, HALF), (0, 0), (0, 0)))
        value_padded = jnp.pad(value_rows, ((HALF, HALF), (0, 0), (0, 0)))

        def attend(block_index):
            first_row = (block_index * block_size).astype(jnp.int32)
            query_block = lax.dynamic_slice_in_dim(queries, first_row, block_size, 0)
            key_block = lax.dynamic_slice_in_dim(key_padded, first_row, span_size, 0)
            value_block = lax.dynamic_slice_in_dim(value_padded, first_row, span_size, 0)
            query_seg = lax.dynamic_slice_in_dim(segment, first_row + HALF, block_size, 0)
            key_seg = lax.dynamic_slice_in_dim(segment, first_row, span_size, 0)
            allowed = in_window & (query_seg[:, None] == key_seg[None, :])
            scores = low_back(jnp.einsum('qhd,khd->hqk', query_block, key_block, precision=lax.Precision.HIGHEST)) * 0.125
            scores = jnp.where(allowed[None], scores, -1e+30)
            weights_block = low(jax.nn.softmax(scores, axis=-1))
            return jnp.einsum('hqk,khd->qhd', weights_block, value_block, precision=lax.Precision.HIGHEST).reshape(block_size, D)
        mixed = lax.map(jax.checkpoint(attend), jnp.arange(block_count, dtype=jnp.int32)).reshape(TOKENS, D)
        attended = low(low_back(mixed))
        residual = inputs + low_back(matmul(attended, weight_attn))
        normed_two = low(layer_norm(residual, gain_two))
        both_halves = low_back(matmul(normed_two, weight_in))
        hidden = low(jax.nn.gelu(both_halves[:, :FF], approximate=False) * both_halves[:, FF:])
        return residual + low_back(matmul(hidden, weight_down))
    result, pullback = jax.vjp(forward, tokens.astype(jnp.float32), first_gain.astype(jnp.float32), qkv_weight.astype(jnp.float32), attn_weight.astype(jnp.float32), second_gain.astype(jnp.float32), feed_in_weight.astype(jnp.float32), feed_out_weight.astype(jnp.float32))
    grads_all = pullback(cotangent.astype(jnp.float32))
    return (result.astype(jnp.bfloat16), grads_all[0], grads_all[1], grads_all[2], grads_all[3], grads_all[4], grads_all[5], grads_all[6])
```

```python
import jax
import jax.numpy as jnp
from jax import lax
from jax.experimental import pallas as pl
from jax.experimental.pallas import tpu as pltpu
from jax.sharding import PartitionSpec as P

D = 768
FF = 1152
HEADS = 12
HEAD_DIM = 64
HALF = 64
PAIRS = HEADS // 2
BLOCK = 128
SPAN = BLOCK + 2 * HALF
LANES = 128
QKV_HALF = 3 * D // 2
FF_HALF = 2 * FF
MIB = 1024 * 1024
BF = jnp.bfloat16
F32 = jnp.float32


def dot(left, right, left_dim=1, right_dim=0):
    return lax.dot_general(
        left, right, (((left_dim,), (right_dim,)), ((), ())), preferred_element_type=F32
    )


def params(mib):
    return pltpu.CompilerParams(vmem_limit_bytes=mib * MIB)


def whole(shape):
    return pl.BlockSpec(shape, lambda *_: (0,) * len(shape))


def rows(shape):
    return pl.BlockSpec(shape, lambda i: (i,) + (0,) * (len(shape) - 1))


SMEM = pl.BlockSpec(memory_space=pltpu.SMEM)
ANY = pl.BlockSpec(memory_space=pl.ANY)


def lane_ids(shape):
    return lax.broadcasted_iota(jnp.int32, shape, len(shape) - 1)


def swap_halves(values):
    low = (lane_ids(values.shape) & (HEAD_DIM - 1)) < HEAD_DIM // 2
    return jnp.where(
        low, pltpu.roll(values, LANES - HEAD_DIM // 2, 1), pltpu.roll(values, HEAD_DIM // 2, 1)
    )


def normalized(values):
    centered = values - jnp.mean(values, axis=-1, keepdims=True)
    scale = lax.rsqrt(jnp.mean(centered * centered, axis=-1, keepdims=True) + 1e-05)
    return centered * scale, scale


def norm_back(grad, unit, scale, gains):
    grad_unit = grad * gains
    return scale * (
        grad_unit
        - jnp.mean(grad_unit, axis=-1, keepdims=True)
        - unit * jnp.mean(grad_unit * unit, axis=-1, keepdims=True)
    )


def qkv_kernel(x_ref, gain_ref, w_ref, cos_ref, sin_ref, normed_ref, qkv_ref):
    unit, _ = normalized(x_ref[...].astype(F32))
    normed = (unit * gain_ref[...]).astype(BF)
    normed_ref[...] = normed
    cosine = cos_ref[...]
    sine = sin_ref[...]
    for half in range(2):
        merged = dot(normed, w_ref[half, :, :QKV_HALF])
        for tile in range(QKV_HALF // LANES):
            first = half * QKV_HALF + tile * LANES
            part = merged[:, tile * LANES : (tile + 1) * LANES]
            if first < 2 * D:
                part = part * cosine + swap_halves(part) * sine
            qkv_ref[:, first : first + LANES] = part.astype(BF)


def project_qkv(tokens, gain, weights, cosine, sine):
    count = tokens.shape[0]
    size = min(256, count)
    return pl.pallas_call(
        qkv_kernel,
        grid=(count // size,),
        in_specs=[
            rows((size, D)),
            whole((1, D)),
            whole(weights.shape),
            rows((size, LANES)),
            rows((size, LANES)),
        ],
        out_specs=[rows((size, D)), rows((size, 3 * D))],
        out_shape=[
            jax.ShapeDtypeStruct((count, D), BF),
            jax.ShapeDtypeStruct((count, 3 * D), BF),
        ],
        compiler_params=params(40),
        cost_estimate=pl.CostEstimate(
            flops=2 * count * D * 3 * D, bytes_accessed=count * D * 10 + 6 * D * D, transcendentals=0
        ),
        name="qkv",
    )(tokens, gain, weights, cosine, sine)


def window_bias(marks_ref, block):
    shape = (SPAN, 2 * BLOCK)
    first = marks_ref[3] + block * BLOCK
    key = lax.broadcasted_iota(jnp.int32, shape, 0)
    query = lax.broadcasted_iota(jnp.int32, (1, 2 * BLOCK), 1) & (BLOCK - 1)
    place = first + query
    lowest = query
    highest = query + 2 * HALF
    for index in range(3):
        mark = marks_ref[index]
        edge = mark - first + HALF
        past = place >= mark
        lowest = jnp.where(past, jnp.maximum(lowest, edge), lowest)
        highest = jnp.where(past, highest, jnp.minimum(highest, edge - 1))
    return jnp.where((key >= lowest) & (key <= highest), 0.0, -1e30).astype(F32)


def stacked(pair):
    low = lane_ids(pair.shape) < HEAD_DIM
    zero = jnp.zeros_like(pair)
    return jnp.concatenate([jnp.where(low, pair, zero), jnp.where(low, zero, pair)], axis=0)


def unstacked(both):
    low = lane_ids((BLOCK, LANES)) < HEAD_DIM
    return jnp.where(low, both[:BLOCK], both[BLOCK:])


def fill_span(qkv_ref, lower_ref, upper_ref, span_ref, sems):
    count = qkv_ref.shape[0]
    copies = [
        pltpu.make_async_copy(
            qkv_ref.at[:, pl.ds(D, 2 * D)], span_ref.at[pl.ds(HALF, count)], sems.at[0]
        ),
        pltpu.make_async_copy(lower_ref, span_ref.at[pl.ds(0, HALF)], sems.at[1]),
        pltpu.make_async_copy(upper_ref, span_ref.at[pl.ds(HALF + count, HALF)], sems.at[2]),
    ]
    for copy in copies:
        copy.start()
    for copy in copies:
        copy.wait()


def attend_kernel(marks_ref, query_ref, qkv_ref, lower_ref, upper_ref, out_ref, log_ref, span_ref, sems):
    block = pl.program_id(0)

    @pl.when(block == 0)
    def _():
        fill_span(qkv_ref, lower_ref, upper_ref, span_ref, sems)

    bias = window_bias(marks_ref, block)
    window = pl.ds(pl.multiple_of(block * BLOCK, BLOCK), SPAN)
    for pair in range(PAIRS):
        lanes = slice(pair * LANES, (pair + 1) * LANES)
        query = stacked(query_ref[:, lanes] * BF(0.125))
        keys = span_ref[window, lanes]
        values = span_ref[window, D + pair * LANES : D + (pair + 1) * LANES]
        scores = dot(keys, query, 1, 1) + bias
        peak = jnp.max(scores, axis=0, keepdims=True)
        expo = jnp.exp(scores - peak)
        total = jnp.sum(expo, axis=0, keepdims=True)
        weights = (expo * (1.0 / total)).astype(BF)
        out_ref[:, lanes] = unstacked(dot(weights, values, 0, 0)).astype(BF)
        log_ref[0, pair : pair + 1, :] = peak + jnp.log(total)


def attend(marks, qkv, lower, upper):
    count = qkv.shape[0]
    blocks = count // BLOCK
    return pl.pallas_call(
        attend_kernel,
        grid=(blocks,),
        in_specs=[SMEM, rows((BLOCK, D)), ANY, ANY, ANY],
        out_specs=[rows((BLOCK, D)), rows((1, 8, 2 * BLOCK))],
        out_shape=[
            jax.ShapeDtypeStruct((count, D), BF),
            jax.ShapeDtypeStruct((blocks, 8, 2 * BLOCK), F32),
        ],
        scratch_shapes=[
            pltpu.VMEM((count + 2 * HALF, 2 * D), BF),
            pltpu.SemaphoreType.DMA((3,)),
        ],
        compiler_params=params(32),
        cost_estimate=pl.CostEstimate(
            flops=4 * count * SPAN * D * 2, bytes_accessed=count * D * 10, transcendentals=0
        ),
        name="attend",
    )(marks, qkv, qkv, lower, upper)


FF_PARTS = tuple((first, min(256, FF - first)) for first in range(0, FF, 256))


def middle_kernel(
    x_ref,
    mixed_ref,
    cot_ref,
    gain_ref,
    w_ref,
    result_ref,
    normed_ref,
    both_ref,
    hidden_ref,
    low_ref,
    mixed_grad_ref,
    grad_ref,
):
    gain = gain_ref[...]
    cot = cot_ref[...]
    weight_attn = w_ref[1, :, FF : FF + D]
    residual = x_ref[...].astype(F32) + dot(mixed_ref[...], weight_attn)
    unit, scale = normalized(residual)
    normed = (unit * gain).astype(BF)
    normed_ref[...] = normed
    result = residual
    grad_normed = None
    for first, size in FF_PARTS:
        gate_cols = slice(first, first + size)
        up_cols = slice(FF + first, FF + first + size)
        gate = dot(normed, w_ref[0, :, gate_cols])
        up = dot(normed, w_ref[0, :, up_cols])
        grad_hidden = dot(cot, w_ref[1, :, gate_cols])
        share = 0.5 + 0.5 * lax.erf(gate * 0.7071067811865476)
        active = gate * share
        slope = share + gate * (jnp.exp(-0.5 * gate * gate) * 0.3989422804014327)
        hidden = (active * up).astype(BF)
        hidden_ref[:, gate_cols] = hidden
        grad_gate = (grad_hidden * up * slope).astype(BF)
        grad_up = (grad_hidden * active).astype(BF)
        both_ref[:, gate_cols] = grad_gate
        both_ref[:, up_cols] = grad_up
        result = result + dot(hidden, w_ref[1, :, gate_cols], 1, 1)
        piece = dot(grad_gate, w_ref[0, :, gate_cols], 1, 1) + dot(
            grad_up, w_ref[0, :, up_cols], 1, 1
        )
        grad_normed = piece if grad_normed is None else grad_normed + piece
    result_ref[...] = result.astype(BF)
    grad = cot.astype(F32) + norm_back(grad_normed, unit, scale, gain)
    grad_ref[...] = grad
    low = grad.astype(BF)
    low_ref[...] = low
    mixed_grad_ref[...] = dot(low, weight_attn, 1, 1).astype(BF)


def middle(tokens, mixed, cotangent, gain, weights):
    count = tokens.shape[0]
    size = min(256, count)
    wide = [(D, BF), (D, BF), (2 * FF, BF), (FF, BF), (D, BF), (D, BF), (D, F32)]
    return pl.pallas_call(
        middle_kernel,
        grid=(count // size,),
        in_specs=[
            rows((size, D)),
            rows((size, D)),
            rows((size, D)),
            whole((1, D)),
            whole(weights.shape),
        ],
        out_specs=[rows((size, width)) for width, _ in wide],
        out_shape=[jax.ShapeDtypeStruct((count, width), kind) for width, kind in wide],
        compiler_params=params(56),
        cost_estimate=pl.CostEstimate(
            flops=4 * count * D * (D + 3 * FF), bytes_accessed=count * D * 30, transcendentals=0
        ),
        name="middle",
    )(tokens, mixed, cotangent, gain, weights)


def attend_back_kernel(
    marks_ref,
    query_ref,
    mixed_grad_ref,
    log_ref,
    cos_ref,
    sin_ref,
    qkv_ref,
    lower_ref,
    upper_ref,
    grad_ref,
    edge_ref,
    away_ref,
    span_ref,
    sum_ref,
    sems,
):
    block = pl.program_id(0)
    count = qkv_ref.shape[0]

    @pl.when(block == 0)
    def _():
        fill_span(qkv_ref, lower_ref, upper_ref, span_ref, sems)
        sum_ref[0:BLOCK, :] = jnp.zeros((BLOCK, 2 * D), F32)

    bias = window_bias(marks_ref, block)
    start = pl.multiple_of(block * BLOCK, BLOCK)
    window = pl.ds(start, SPAN)
    older = pl.ds(start, BLOCK)
    newer = pl.ds(start + BLOCK, BLOCK)
    cosine = cos_ref[older, :]
    sine = sin_ref[older, :]
    for pair in range(PAIRS):
        lanes = slice(pair * LANES, (pair + 1) * LANES)
        value_lanes = slice(D + pair * LANES, D + (pair + 1) * LANES)
        query = stacked(query_ref[:, lanes] * BF(0.125))
        keys = span_ref[window, lanes]
        values = span_ref[window, value_lanes]
        out_grad = stacked(mixed_grad_ref[:, lanes])
        scores = dot(keys, query, 1, 1) + bias
        weights = jnp.exp(scores - log_ref[0, pair : pair + 1, :])
        weight_grad = dot(values, out_grad, 1, 1)
        score_grad = weights * (
            weight_grad - jnp.sum(weights * weight_grad, axis=0, keepdims=True)
        )
        score_grad = score_grad.astype(BF)
        key_grad = dot(score_grad, query)
        value_grad = dot(weights.astype(BF), out_grad)
        sum_ref[older, lanes] += key_grad[:BLOCK]
        sum_ref[newer, lanes] = key_grad[BLOCK:]
        sum_ref[older, value_lanes] += value_grad[:BLOCK]
        sum_ref[newer, value_lanes] = value_grad[BLOCK:]
        query_grad = unstacked(dot(score_grad, keys, 0, 0)) * 0.125
        query_grad = query_grad * cosine - swap_halves(query_grad) * sine
        grad_ref[older, lanes] = query_grad.astype(BF)

    @pl.when(block > 0)
    def _():
        own = pl.ds(pl.multiple_of(start - HALF, HALF), BLOCK)
        own_cosine = cos_ref[own, :]
        own_sine = sin_ref[own, :]
        for pair in range(PAIRS):
            lanes = slice(pair * LANES, (pair + 1) * LANES)
            done = sum_ref[older, lanes]
            done = done * own_cosine - swap_halves(done) * own_sine
            grad_ref[own, D + pair * LANES : D + (pair + 1) * LANES] = done.astype(BF)
        grad_ref[own, 2 * D :] = sum_ref[older, D:].astype(BF)

    @pl.when(block == pl.num_programs(0) - 1)
    def _():
        away_ref[0:HALF, :] = sum_ref[0:HALF, :].astype(BF)
        away_ref[HALF:, :] = sum_ref[count + HALF :, :].astype(BF)
        edge_ref[0:HALF, :] = sum_ref[HALF : 2 * HALF, :]
        edge_ref[HALF:, :] = sum_ref[count : count + HALF, :]


def attend_back(marks, qkv, mixed_grad, logs, cosine, sine, lower, upper):
    count = qkv.shape[0]
    return pl.pallas_call(
        attend_back_kernel,
        grid=(count // BLOCK,),
        in_specs=[
            SMEM,
            rows((BLOCK, D)),
            rows((BLOCK, D)),
            rows((1, 8, 2 * BLOCK)),
            whole((count, LANES)),
            whole((count, LANES)),
            ANY,
            ANY,
            ANY,
        ],
        out_specs=[whole((count, 3 * D)), whole((2 * HALF, 2 * D)), whole((2 * HALF, 2 * D))],
        out_shape=[
            jax.ShapeDtypeStruct((count, 3 * D), BF),
            jax.ShapeDtypeStruct((2 * HALF, 2 * D), F32),
            jax.ShapeDtypeStruct((2 * HALF, 2 * D), BF),
        ],
        scratch_shapes=[
            pltpu.VMEM((count + 2 * HALF, 2 * D), BF),
            pltpu.VMEM((count + 2 * HALF, 2 * D), F32),
            pltpu.SemaphoreType.DMA((3,)),
        ],
        compiler_params=params(48),
        cost_estimate=pl.CostEstimate(
            flops=10 * count * SPAN * D * 2, bytes_accessed=count * D * 20, transcendentals=0
        ),
        name="attend_back",
    )(marks, qkv, mixed_grad, logs, cosine, sine, qkv, lower, upper)


def patch_kernel(edge_ref, near_ref, cos_ref, sin_ref, _, out_ref):
    part = pl.program_id(1)
    total = edge_ref[...] + near_ref[...].astype(F32)

    @pl.when(part == 0)
    def _():
        cosine = cos_ref[...]
        sine = sin_ref[...]
        for pair in range(PAIRS):
            lanes = slice(pair * LANES, (pair + 1) * LANES)
            done = total[:, lanes]
            out_ref[:, lanes] = (done * cosine - swap_halves(done) * sine).astype(BF)

    @pl.when(part == 1)
    def _():
        out_ref[...] = total.astype(BF)


def patch(edge, near, cosine, sine, grads):
    last = grads.shape[0] // HALF - 1
    return pl.pallas_call(
        patch_kernel,
        grid=(2, 2),
        in_specs=[
            pl.BlockSpec((HALF, D), lambda side, part: (side, part)),
            pl.BlockSpec((HALF, D), lambda side, part: (side, part)),
            pl.BlockSpec((HALF, LANES), lambda side, part: (side * last, 0)),
            pl.BlockSpec((HALF, LANES), lambda side, part: (side * last, 0)),
            ANY,
        ],
        out_specs=pl.BlockSpec((HALF, D), lambda side, part: (side * last, 1 + part)),
        out_shape=jax.ShapeDtypeStruct(grads.shape, BF),
        input_output_aliases={4: 0},
        compiler_params=params(16),
        cost_estimate=pl.CostEstimate(flops=0, bytes_accessed=HALF * D * 24, transcendentals=0),
        name="patch",
    )(edge, near, cosine, sine, grads)


def input_grad_kernel(x_ref, gain_ref, w_ref, dqkv_ref, grad_ref, out_ref):
    unit, scale = normalized(x_ref[...].astype(F32))
    grad_normed = dot(dqkv_ref[:, :QKV_HALF], w_ref[0, :, :QKV_HALF], 1, 1) + dot(
        dqkv_ref[:, QKV_HALF:], w_ref[1, :, :QKV_HALF], 1, 1
    )
    out_ref[...] = grad_ref[...] + norm_back(grad_normed, unit, scale, gain_ref[...])


def input_grad(tokens, gain, weights, dqkv, grad):
    count = tokens.shape[0]
    size = min(256, count)
    return pl.pallas_call(
        input_grad_kernel,
        grid=(count // size,),
        in_specs=[
            rows((size, D)),
            whole((1, D)),
            whole(weights.shape),
            rows((size, 3 * D)),
            rows((size, D)),
        ],
        out_specs=rows((size, D)),
        out_shape=jax.ShapeDtypeStruct((count, D), F32),
        compiler_params=params(40),
        cost_estimate=pl.CostEstimate(
            flops=2 * count * D * 3 * D, bytes_accessed=count * D * 16, transcendentals=0
        ),
        name="input_grad",
    )(tokens, gain, weights, dqkv, grad)


CHIP_ROWS = 48
TILE = 384


def store_slots(slots_ref, out_ref, product):
    step = CHIP_ROWS
    for index in range(D // step):
        place = pl.multiple_of(slots_ref[1 + index] * step, 16)
        out_ref[pl.ds(place, step), :] = product[index * step : (index + 1) * step].astype(BF)


def qkv_weight_kernel(slots_ref, normed_ref, grad_ref, out_ref, turned_ref):
    @pl.when(pl.program_id(0) == 0)
    def _():
        turned_ref[...] = normed_ref[...].T

    store_slots(slots_ref, out_ref, dot(turned_ref[...], grad_ref[...]))


def qkv_weight_grad(slots, normed, dqkv):
    count = normed.shape[0]
    tiles = QKV_HALF // TILE
    return pl.pallas_call(
        qkv_weight_kernel,
        grid_spec=pltpu.PrefetchScalarGridSpec(
            num_scalar_prefetch=1,
            grid=(tiles,),
            in_specs=[
                pl.BlockSpec((count, D), lambda t, s: (0, 0)),
                pl.BlockSpec((count, TILE), lambda t, s: (0, s[0] * tiles + t)),
            ],
            out_specs=pl.BlockSpec((D, TILE), lambda t, s: (0, t)),
            scratch_shapes=[pltpu.VMEM((D, count), BF)],
        ),
        out_shape=jax.ShapeDtypeStruct((D, QKV_HALF), BF),
        compiler_params=params(32),
        cost_estimate=pl.CostEstimate(
            flops=2 * count * D * QKV_HALF, bytes_accessed=count * D * 8, transcendentals=0
        ),
        name="qkv_weight_grad",
    )(slots, normed, dqkv)


def ff_weight_kernel(slots_ref, normed_ref, cot_ref, mixed_ref, both_ref, hidden_ref, low_ref, out_ref, turned_ref):
    step = pl.program_id(0)
    second = slots_ref[0] == 1

    @pl.when((step == 0) & ~second)
    def _():
        turned_ref[...] = normed_ref[...].T

    @pl.when((step == 0) & second)
    def _():
        turned_ref[...] = cot_ref[...].T

    @pl.when((step == 3) & second)
    def _():
        turned_ref[...] = mixed_ref[...].T

    @pl.when(~second)
    def _():
        store_slots(slots_ref, out_ref, dot(turned_ref[...], both_ref[...]))

    @pl.when(second & (step < 3))
    def _():
        store_slots(slots_ref, out_ref, dot(turned_ref[...], hidden_ref[...]))

    @pl.when(second & (step >= 3) & (step < 5))
    def _():
        store_slots(slots_ref, out_ref, dot(turned_ref[...], low_ref[...]))

    @pl.when(second & (step == 5))
    def _():
        out_ref[...] = jnp.zeros_like(out_ref)


def ff_weight_grad(slots, normed, cot, mixed, both, hidden, low):
    count = normed.shape[0]
    full = pl.BlockSpec((count, D), lambda t, s: (0, 0))
    return pl.pallas_call(
        ff_weight_kernel,
        grid_spec=pltpu.PrefetchScalarGridSpec(
            num_scalar_prefetch=1,
            grid=(FF_HALF // TILE,),
            in_specs=[
                full,
                full,
                full,
                pl.BlockSpec((count, TILE), lambda t, s: (0, jnp.where(s[0] == 0, t, 0))),
                pl.BlockSpec((count, TILE), lambda t, s: (0, jnp.where(s[0] == 0, 0, jnp.minimum(t, 2)))),
                pl.BlockSpec(
                    (count, TILE), lambda t, s: (0, jnp.where(s[0] == 0, 0, jnp.clip(t - 3, 0, 1)))
                ),
            ],
            out_specs=pl.BlockSpec((D, TILE), lambda t, s: (0, t)),
            scratch_shapes=[pltpu.VMEM((D, count), BF)],
        ),
        out_shape=jax.ShapeDtypeStruct((D, FF_HALF), BF),
        compiler_params=params(40),
        cost_estimate=pl.CostEstimate(
            flops=2 * count * D * FF_HALF, bytes_accessed=count * D * 12, transcendentals=0
        ),
        name="ff_weight_grad",
    )(slots, normed, cot, mixed, both, hidden, low)


def doc_marks(doc_lengths, row_count):
    me = lax.axis_index("tok")
    ends = jnp.cumsum(doc_lengths).astype(jnp.int32)
    before = jnp.where(me > 0, ends[jnp.maximum(me - 1, 0)], 0)
    return jnp.stack([before, ends[me], ends[me + 1], me * row_count]).astype(jnp.int32)


def rotary_tables(marks, row_count):
    place = marks[3] + jnp.arange(row_count, dtype=jnp.int32)
    offset = place - jnp.where(place >= marks[1], marks[1], marks[0])
    frequency = 10000.0 ** (-jnp.arange(0, HEAD_DIM, 2, dtype=F32) / HEAD_DIM)
    angles = offset.astype(F32)[:, None] * frequency[None, :]
    cosine = jnp.cos(angles)
    sine = jnp.sin(angles)
    return (
        jnp.concatenate([cosine] * 4, axis=1),
        jnp.concatenate([-sine, sine, -sine, sine], axis=1),
    )


def passed_along(value, steps):
    count = lax.axis_size("tok")
    first, last = (max(0, -steps), min(count, count - steps))
    return lax.ppermute(value, "tok", [(at, at + steps) for at in range(first, last)])


def gathered(shard):
    full = lax.all_gather(shard, "tok", axis=0, tiled=True)
    half = full.shape[1] // 2
    return jnp.stack([full[:, :half], full[:, half:]])


def scattered(first, second):
    full = jnp.concatenate([first, second], axis=1)
    return lax.psum_scatter(full.astype(F32), "tok", scatter_dimension=0, tiled=True)


def on_device(
    tokens,
    doc_lengths,
    first_gain,
    qkv_weight,
    attn_weight,
    second_gain,
    feed_in_weight,
    feed_out_weight,
    cotangent,
):
    row_count = tokens.shape[0]
    share = first_gain.shape[0]

    def spread(gain):
        return jnp.broadcast_to(gain[:, None], (share, LANES))

    shard_one = jnp.concatenate(
        [
            qkv_weight[:, :QKV_HALF],
            spread(first_gain),
            qkv_weight[:, QKV_HALF:],
            spread(second_gain),
        ],
        axis=1,
    )
    shard_two = jnp.concatenate(
        [
            feed_in_weight,
            feed_out_weight.T,
            attn_weight,
            jnp.zeros((share, FF_HALF - FF - D), BF),
        ],
        axis=1,
    )
    marks = doc_marks(doc_lengths, row_count)
    cosine, sine = rotary_tables(marks, row_count)
    weights_one = gathered(shard_one)
    weights_two = gathered(shard_two)
    gain_one = weights_one[0, :, QKV_HALF].astype(F32)[None]
    gain_two = weights_one[1, :, QKV_HALF].astype(F32)[None]
    normed, qkv = project_qkv(tokens, gain_one, weights_one, cosine, sine)
    lower = passed_along(qkv[row_count - HALF :, D:], 1)
    upper = passed_along(qkv[:HALF, D:], -1)
    mixed, logs = attend(marks, qkv, lower, upper)
    result, normed_two, both, hidden, low, mixed_grad, grad = middle(
        tokens, mixed, cotangent, gain_two, weights_two
    )
    slots = jnp.arange(D // CHIP_ROWS, dtype=jnp.int32)

    def order(half):
        return jnp.concatenate([jnp.full((1,), half, jnp.int32), slots])

    grads_ff = [
        ff_weight_grad(order(half), normed_two, cotangent, mixed, both, hidden, low)
        for half in range(2)
    ]
    dqkv, edge, away = attend_back(marks, qkv, mixed_grad, logs, cosine, sine, lower, upper)
    from_upper = passed_along(away[:HALF], -1)
    from_lower = passed_along(away[HALF:], 1)
    dqkv = patch(edge, jnp.concatenate([from_lower, from_upper], axis=0), cosine, sine, dqkv)
    grads_qkv = [qkv_weight_grad(order(half), normed, dqkv) for half in range(2)]
    grad_in = input_grad(tokens, gain_one, weights_one, dqkv, grad)
    sum_ff = scattered(*grads_ff)
    sum_qkv = scattered(*grads_qkv)
    sent_in = sum_ff[:, : 2 * FF]
    sent_down = sum_ff[:, 2 * FF : 3 * FF].T
    sent_attn = sum_ff[:, 3 * FF : 3 * FF + D]

    def gain_grad(summed, weight, gain):
        return jnp.sum(summed * weight.astype(F32), axis=1) / gain.astype(F32)

    return (
        result,
        grad_in,
        gain_grad(sum_qkv, qkv_weight, first_gain),
        sum_qkv,
        sent_attn,
        gain_grad(sent_in, feed_in_weight, second_gain),
        sent_in,
        sent_down,
    )


def solution(mesh):
    in_specs = (
        P("tok", None),
        P(),
        P("tok"),
        P("tok", None),
        P("tok", None),
        P("tok"),
        P("tok", None),
        P(None, "tok"),
        P("tok", None),
    )
    out_specs = (
        P("tok", None),
        P("tok", None),
        P("tok"),
        P("tok", None),
        P("tok", None),
        P("tok"),
        P("tok", None),
        P(None, "tok"),
    )
    return jax.shard_map(
        on_device, mesh=mesh, in_specs=in_specs, out_specs=out_specs, check_vma=False
    )
```

```python
import jax
import jax.numpy as jnp
from jax import lax
from jax.experimental import pallas as pl
from jax.experimental.pallas import tpu as pltpu
from jax.sharding import PartitionSpec as P

D = 768
FF = 1152
HEADS = 12
HEAD_DIM = 64
HALF = 64
PAIRS = HEADS // 2
BLOCK = 128
SPAN = BLOCK + 2 * HALF
LANES = 128
QKV_HALF = 3 * D // 2
FF_HALF = 2 * FF
MIB = 1024 * 1024
BF = jnp.bfloat16
F32 = jnp.float32


def dot(left, right, left_dim=1, right_dim=0):
    return lax.dot_general(
        left, right, (((left_dim,), (right_dim,)), ((), ())), preferred_element_type=F32
    )


def params(mib):
    return pltpu.CompilerParams(vmem_limit_bytes=mib * MIB)


def whole(shape):
    return pl.BlockSpec(shape, lambda *_: (0,) * len(shape))


def rows(shape):
    return pl.BlockSpec(shape, lambda i: (i,) + (0,) * (len(shape) - 1))


SMEM = pl.BlockSpec(memory_space=pltpu.SMEM)
ANY = pl.BlockSpec(memory_space=pl.ANY)


def lane_ids(shape):
    return lax.broadcasted_iota(jnp.int32, shape, len(shape) - 1)


def swap_halves(values):
    low = (lane_ids(values.shape) & (HEAD_DIM - 1)) < HEAD_DIM // 2
    return jnp.where(
        low, pltpu.roll(values, LANES - HEAD_DIM // 2, 1), pltpu.roll(values, HEAD_DIM // 2, 1)
    )


def normalized(values):
    centered = values - jnp.mean(values, axis=-1, keepdims=True)
    scale = lax.rsqrt(jnp.mean(centered * centered, axis=-1, keepdims=True) + 1e-05)
    return centered * scale, scale


def norm_back(grad, unit, scale, gains):
    grad_unit = grad * gains
    return scale * (
        grad_unit
        - jnp.mean(grad_unit, axis=-1, keepdims=True)
        - unit * jnp.mean(grad_unit * unit, axis=-1, keepdims=True)
    )


def qkv_kernel(x_ref, gain_ref, w_ref, cos_ref, sin_ref, normed_ref, qkv_ref):
    unit, _ = normalized(x_ref[...].astype(F32))
    normed = (unit * gain_ref[...]).astype(BF)
    normed_ref[...] = normed
    cosine = cos_ref[...]
    sine = sin_ref[...]
    for half in range(2):
        merged = dot(normed, w_ref[half, :, :QKV_HALF])
        for tile in range(QKV_HALF // LANES):
            first = half * QKV_HALF + tile * LANES
            part = merged[:, tile * LANES : (tile + 1) * LANES]
            if first < 2 * D:
                part = part * cosine + swap_halves(part) * sine
            qkv_ref[:, first : first + LANES] = part.astype(BF)


def project_qkv(tokens, gain, weights, cosine, sine):
    count = tokens.shape[0]
    size = min(256, count)
    return pl.pallas_call(
        qkv_kernel,
        grid=(count // size,),
        in_specs=[
            rows((size, D)),
            whole((1, D)),
            whole(weights.shape),
            rows((size, LANES)),
            rows((size, LANES)),
        ],
        out_specs=[rows((size, D)), rows((size, 3 * D))],
        out_shape=[
            jax.ShapeDtypeStruct((count, D), BF),
            jax.ShapeDtypeStruct((count, 3 * D), BF),
        ],
        compiler_params=params(40),
        cost_estimate=pl.CostEstimate(
            flops=2 * count * D * 3 * D, bytes_accessed=count * D * 10 + 6 * D * D, transcendentals=0
        ),
        name="qkv",
    )(tokens, gain, weights, cosine, sine)


def window_bias(marks_ref, block):
    shape = (SPAN, 2 * BLOCK)
    first = marks_ref[3] + block * BLOCK
    key = lax.broadcasted_iota(jnp.int32, shape, 0)
    query = lax.broadcasted_iota(jnp.int32, (1, 2 * BLOCK), 1) & (BLOCK - 1)
    place = first + query
    lowest = query
    highest = query + 2 * HALF
    for index in range(3):
        mark = marks_ref[index]
        edge = mark - first + HALF
        past = place >= mark
        lowest = jnp.where(past, jnp.maximum(lowest, edge), lowest)
        highest = jnp.where(past, highest, jnp.minimum(highest, edge - 1))
    return jnp.where((key >= lowest) & (key <= highest), 0.0, -1e30).astype(F32)


def stacked(pair):
    low = lane_ids(pair.shape) < HEAD_DIM
    zero = jnp.zeros_like(pair)
    return jnp.concatenate([jnp.where(low, pair, zero), jnp.where(low, zero, pair)], axis=0)


def unstacked(both):
    low = lane_ids((BLOCK, LANES)) < HEAD_DIM
    return jnp.where(low, both[:BLOCK], both[BLOCK:])


def fill_span(qkv_ref, lower_ref, upper_ref, span_ref, sems):
    count = qkv_ref.shape[0]
    copies = [
        pltpu.make_async_copy(
            qkv_ref.at[:, pl.ds(D, 2 * D)], span_ref.at[pl.ds(HALF, count)], sems.at[0]
        ),
        pltpu.make_async_copy(lower_ref, span_ref.at[pl.ds(0, HALF)], sems.at[1]),
        pltpu.make_async_copy(upper_ref, span_ref.at[pl.ds(HALF + count, HALF)], sems.at[2]),
    ]
    for copy in copies:
        copy.start()
    for copy in copies:
        copy.wait()


def attend_kernel(marks_ref, query_ref, qkv_ref, lower_ref, upper_ref, out_ref, log_ref, span_ref, sems):
    block = pl.program_id(0)

    @pl.when(block == 0)
    def _():
        fill_span(qkv_ref, lower_ref, upper_ref, span_ref, sems)

    bias = window_bias(marks_ref, block)
    window = pl.ds(pl.multiple_of(block * BLOCK, BLOCK), SPAN)
    for pair in range(PAIRS):
        lanes = slice(pair * LANES, (pair + 1) * LANES)
        query = stacked(query_ref[:, lanes] * BF(0.125))
        keys = span_ref[window, lanes]
        values = span_ref[window, D + pair * LANES : D + (pair + 1) * LANES]
        scores = dot(keys, query, 1, 1) + bias
        peak = jnp.max(scores, axis=0, keepdims=True)
        expo = jnp.exp(scores - peak)
        total = jnp.sum(expo, axis=0, keepdims=True)
        weights = (expo * (1.0 / total)).astype(BF)
        out_ref[:, lanes] = unstacked(dot(weights, values, 0, 0)).astype(BF)
        log_ref[0, pair : pair + 1, :] = peak + jnp.log(total)


def attend(marks, qkv, lower, upper):
    count = qkv.shape[0]
    blocks = count // BLOCK
    return pl.pallas_call(
        attend_kernel,
        grid=(blocks,),
        in_specs=[SMEM, rows((BLOCK, D)), ANY, ANY, ANY],
        out_specs=[rows((BLOCK, D)), rows((1, 8, 2 * BLOCK))],
        out_shape=[
            jax.ShapeDtypeStruct((count, D), BF),
            jax.ShapeDtypeStruct((blocks, 8, 2 * BLOCK), F32),
        ],
        scratch_shapes=[
            pltpu.VMEM((count + 2 * HALF, 2 * D), BF),
            pltpu.SemaphoreType.DMA((3,)),
        ],
        compiler_params=params(32),
        cost_estimate=pl.CostEstimate(
            flops=4 * count * SPAN * D * 2, bytes_accessed=count * D * 10, transcendentals=0
        ),
        name="attend",
    )(marks, qkv, qkv, lower, upper)


FF_PARTS = tuple((first, min(256, FF - first)) for first in range(0, FF, 256))


def middle_kernel(
    x_ref,
    mixed_ref,
    cot_ref,
    gain_ref,
    w_ref,
    result_ref,
    normed_ref,
    both_ref,
    hidden_ref,
    low_ref,
    mixed_grad_ref,
    grad_ref,
):
    gain = gain_ref[...]
    cot = cot_ref[...]
    weight_attn = w_ref[1, :, FF : FF + D]
    residual = x_ref[...].astype(F32) + dot(mixed_ref[...], weight_attn)
    unit, scale = normalized(residual)
    normed = (unit * gain).astype(BF)
    normed_ref[...] = normed
    result = residual
    grad_normed = None
    for first, size in FF_PARTS:
        gate_cols = slice(first, first + size)
        up_cols = slice(FF + first, FF + first + size)
        gate = dot(normed, w_ref[0, :, gate_cols])
        up = dot(normed, w_ref[0, :, up_cols])
        grad_hidden = dot(cot, w_ref[1, :, gate_cols])
        share = 0.5 + 0.5 * lax.erf(gate * 0.7071067811865476)
        active = gate * share
        slope = share + gate * (jnp.exp(-0.5 * gate * gate) * 0.3989422804014327)
        hidden = (active * up).astype(BF)
        hidden_ref[:, gate_cols] = hidden
        grad_gate = (grad_hidden * up * slope).astype(BF)
        grad_up = (grad_hidden * active).astype(BF)
        both_ref[:, gate_cols] = grad_gate
        both_ref[:, up_cols] = grad_up
        result = result + dot(hidden, w_ref[1, :, gate_cols], 1, 1)
        piece = dot(grad_gate, w_ref[0, :, gate_cols], 1, 1) + dot(
            grad_up, w_ref[0, :, up_cols], 1, 1
        )
        grad_normed = piece if grad_normed is None else grad_normed + piece
    result_ref[...] = result.astype(BF)
    grad = cot.astype(F32) + norm_back(grad_normed, unit, scale, gain)
    grad_ref[...] = grad
    low = grad.astype(BF)
    low_ref[...] = low
    mixed_grad_ref[...] = dot(low, weight_attn, 1, 1).astype(BF)


def middle(tokens, mixed, cotangent, gain, weights):
    count = tokens.shape[0]
    size = min(256, count)
    wide = [(D, BF), (D, BF), (2 * FF, BF), (FF, BF), (D, BF), (D, BF), (D, F32)]
    return pl.pallas_call(
        middle_kernel,
        grid=(count // size,),
        in_specs=[
            rows((size, D)),
            rows((size, D)),
            rows((size, D)),
            whole((1, D)),
            whole(weights.shape),
        ],
        out_specs=[rows((size, width)) for width, _ in wide],
        out_shape=[jax.ShapeDtypeStruct((count, width), kind) for width, kind in wide],
        compiler_params=params(56),
        cost_estimate=pl.CostEstimate(
            flops=4 * count * D * (D + 3 * FF), bytes_accessed=count * D * 30, transcendentals=0
        ),
        name="middle",
    )(tokens, mixed, cotangent, gain, weights)


def attend_back_kernel(
    marks_ref,
    query_ref,
    mixed_grad_ref,
    log_ref,
    cos_ref,
    sin_ref,
    qkv_ref,
    lower_ref,
    upper_ref,
    grad_ref,
    edge_ref,
    away_ref,
    span_ref,
    sum_ref,
    sems,
):
    block = pl.program_id(0)
    count = qkv_ref.shape[0]

    @pl.when(block == 0)
    def _():
        fill_span(qkv_ref, lower_ref, upper_ref, span_ref, sems)
        sum_ref[0:BLOCK, :] = jnp.zeros((BLOCK, 2 * D), F32)

    bias = window_bias(marks_ref, block)
    start = pl.multiple_of(block * BLOCK, BLOCK)
    window = pl.ds(start, SPAN)
    older = pl.ds(start, BLOCK)
    newer = pl.ds(start + BLOCK, BLOCK)
    cosine = cos_ref[older, :]
    sine = sin_ref[older, :]
    for pair in range(PAIRS):
        lanes = slice(pair * LANES, (pair + 1) * LANES)
        value_lanes = slice(D + pair * LANES, D + (pair + 1) * LANES)
        query = stacked(query_ref[:, lanes] * BF(0.125))
        keys = span_ref[window, lanes]
        values = span_ref[window, value_lanes]
        out_grad = stacked(mixed_grad_ref[:, lanes])
        scores = dot(keys, query, 1, 1) + bias
        weights = jnp.exp(scores - log_ref[0, pair : pair + 1, :])
        weight_grad = dot(values, out_grad, 1, 1)
        score_grad = weights * (
            weight_grad - jnp.sum(weights * weight_grad, axis=0, keepdims=True)
        )
        score_grad = score_grad.astype(BF)
        key_grad = dot(score_grad, query)
        value_grad = dot(weights.astype(BF), out_grad)
        sum_ref[older, lanes] += key_grad[:BLOCK]
        sum_ref[newer, lanes] = key_grad[BLOCK:]
        sum_ref[older, value_lanes] += value_grad[:BLOCK]
        sum_ref[newer, value_lanes] = value_grad[BLOCK:]
        query_grad = unstacked(dot(score_grad, keys, 0, 0)) * 0.125
        query_grad = query_grad * cosine - swap_halves(query_grad) * sine
        grad_ref[older, lanes] = query_grad.astype(BF)

    @pl.when(block > 0)
    def _():
        own = pl.ds(pl.multiple_of(start - HALF, HALF), BLOCK)
        own_cosine = cos_ref[own, :]
        own_sine = sin_ref[own, :]
        for pair in range(PAIRS):
            lanes = slice(pair * LANES, (pair + 1) * LANES)
            done = sum_ref[older, lanes]
            done = done * own_cosine - swap_halves(done) * own_sine
            grad_ref[own, D + pair * LANES : D + (pair + 1) * LANES] = done.astype(BF)
        grad_ref[own, 2 * D :] = sum_ref[older, D:].astype(BF)

    @pl.when(block == pl.num_programs(0) - 1)
    def _():
        away_ref[0:HALF, :] = sum_ref[0:HALF, :].astype(BF)
        away_ref[HALF:, :] = sum_ref[count + HALF :, :].astype(BF)
        edge_ref[0:HALF, :] = sum_ref[HALF : 2 * HALF, :]
        edge_ref[HALF:, :] = sum_ref[count : count + HALF, :]


def attend_back(marks, qkv, mixed_grad, logs, cosine, sine, lower, upper):
    count = qkv.shape[0]
    return pl.pallas_call(
        attend_back_kernel,
        grid=(count // BLOCK,),
        in_specs=[
            SMEM,
            rows((BLOCK, D)),
            rows((BLOCK, D)),
            rows((1, 8, 2 * BLOCK)),
            whole((count, LANES)),
            whole((count, LANES)),
            ANY,
            ANY,
            ANY,
        ],
        out_specs=[whole((count, 3 * D)), whole((2 * HALF, 2 * D)), whole((2 * HALF, 2 * D))],
        out_shape=[
            jax.ShapeDtypeStruct((count, 3 * D), BF),
            jax.ShapeDtypeStruct((2 * HALF, 2 * D), F32),
            jax.ShapeDtypeStruct((2 * HALF, 2 * D), BF),
        ],
        scratch_shapes=[
            pltpu.VMEM((count + 2 * HALF, 2 * D), BF),
            pltpu.VMEM((count + 2 * HALF, 2 * D), F32),
            pltpu.SemaphoreType.DMA((3,)),
        ],
        compiler_params=params(48),
        cost_estimate=pl.CostEstimate(
            flops=10 * count * SPAN * D * 2, bytes_accessed=count * D * 20, transcendentals=0
        ),
        name="attend_back",
    )(marks, qkv, mixed_grad, logs, cosine, sine, qkv, lower, upper)


def patch_kernel(edge_ref, near_ref, cos_ref, sin_ref, _, out_ref):
    part = pl.program_id(1)
    total = edge_ref[...] + near_ref[...].astype(F32)

    @pl.when(part == 0)
    def _():
        cosine = cos_ref[...]
        sine = sin_ref[...]
        for pair in range(PAIRS):
            lanes = slice(pair * LANES, (pair + 1) * LANES)
            done = total[:, lanes]
            out_ref[:, lanes] = (done * cosine - swap_halves(done) * sine).astype(BF)

    @pl.when(part == 1)
    def _():
        out_ref[...] = total.astype(BF)


def patch(edge, near, cosine, sine, grads):
    last = grads.shape[0] // HALF - 1
    return pl.pallas_call(
        patch_kernel,
        grid=(2, 2),
        in_specs=[
            pl.BlockSpec((HALF, D), lambda side, part: (side, part)),
            pl.BlockSpec((HALF, D), lambda side, part: (side, part)),
            pl.BlockSpec((HALF, LANES), lambda side, part: (side * last, 0)),
            pl.BlockSpec((HALF, LANES), lambda side, part: (side * last, 0)),
            ANY,
        ],
        out_specs=pl.BlockSpec((HALF, D), lambda side, part: (side * last, 1 + part)),
        out_shape=jax.ShapeDtypeStruct(grads.shape, BF),
        input_output_aliases={4: 0},
        compiler_params=params(16),
        cost_estimate=pl.CostEstimate(flops=0, bytes_accessed=HALF * D * 24, transcendentals=0),
        name="patch",
    )(edge, near, cosine, sine, grads)


def input_grad_kernel(x_ref, gain_ref, w_ref, dqkv_ref, grad_ref, out_ref):
    unit, scale = normalized(x_ref[...].astype(F32))
    grad_normed = dot(dqkv_ref[:, :QKV_HALF], w_ref[0, :, :QKV_HALF], 1, 1) + dot(
        dqkv_ref[:, QKV_HALF:], w_ref[1, :, :QKV_HALF], 1, 1
    )
    out_ref[...] = grad_ref[...] + norm_back(grad_normed, unit, scale, gain_ref[...])


def input_grad(tokens, gain, weights, dqkv, grad):
    count = tokens.shape[0]
    size = min(256, count)
    return pl.pallas_call(
        input_grad_kernel,
        grid=(count // size,),
        in_specs=[
            rows((size, D)),
            whole((1, D)),
            whole(weights.shape),
            rows((size, 3 * D)),
            rows((size, D)),
        ],
        out_specs=rows((size, D)),
        out_shape=jax.ShapeDtypeStruct((count, D), F32),
        compiler_params=params(40),
        cost_estimate=pl.CostEstimate(
            flops=2 * count * D * 3 * D, bytes_accessed=count * D * 16, transcendentals=0
        ),
        name="input_grad",
    )(tokens, gain, weights, dqkv, grad)


CHIP_ROWS = 48
TILE = 384


def store_slots(slots_ref, out_ref, product):
    step = CHIP_ROWS
    for index in range(D // step):
        place = pl.multiple_of(slots_ref[1 + index] * step, 16)
        out_ref[pl.ds(place, step), :] = product[index * step : (index + 1) * step].astype(BF)


def qkv_weight_kernel(slots_ref, normed_ref, grad_ref, out_ref, turned_ref):
    @pl.when(pl.program_id(0) == 0)
    def _():
        turned_ref[...] = normed_ref[...].T

    store_slots(slots_ref, out_ref, dot(turned_ref[...], grad_ref[...]))


def qkv_weight_grad(slots, normed, dqkv):
    count = normed.shape[0]
    tiles = QKV_HALF // TILE
    return pl.pallas_call(
        qkv_weight_kernel,
        grid_spec=pltpu.PrefetchScalarGridSpec(
            num_scalar_prefetch=1,
            grid=(tiles,),
            in_specs=[
                pl.BlockSpec((count, D), lambda t, s: (0, 0)),
                pl.BlockSpec((count, TILE), lambda t, s: (0, s[0] * tiles + t)),
            ],
            out_specs=pl.BlockSpec((D, TILE), lambda t, s: (0, t)),
            scratch_shapes=[pltpu.VMEM((D, count), BF)],
        ),
        out_shape=jax.ShapeDtypeStruct((D, QKV_HALF), BF),
        compiler_params=params(32),
        cost_estimate=pl.CostEstimate(
            flops=2 * count * D * QKV_HALF, bytes_accessed=count * D * 8, transcendentals=0
        ),
        name="qkv_weight_grad",
    )(slots, normed, dqkv)


def ff_weight_kernel(slots_ref, normed_ref, cot_ref, mixed_ref, both_ref, hidden_ref, low_ref, out_ref, turned_ref):
    step = pl.program_id(0)
    second = slots_ref[0] == 1

    @pl.when((step == 0) & ~second)
    def _():
        turned_ref[...] = normed_ref[...].T

    @pl.when((step == 0) & second)
    def _():
        turned_ref[...] = cot_ref[...].T

    @pl.when((step == 3) & second)
    def _():
        turned_ref[...] = mixed_ref[...].T

    @pl.when(~second)
    def _():
        store_slots(slots_ref, out_ref, dot(turned_ref[...], both_ref[...]))

    @pl.when(second & (step < 3))
    def _():
        store_slots(slots_ref, out_ref, dot(turned_ref[...], hidden_ref[...]))

    @pl.when(second & (step >= 3) & (step < 5))
    def _():
        store_slots(slots_ref, out_ref, dot(turned_ref[...], low_ref[...]))

    @pl.when(second & (step == 5))
    def _():
        out_ref[...] = jnp.zeros_like(out_ref)


def ff_weight_grad(slots, normed, cot, mixed, both, hidden, low):
    count = normed.shape[0]
    full = pl.BlockSpec((count, D), lambda t, s: (0, 0))
    return pl.pallas_call(
        ff_weight_kernel,
        grid_spec=pltpu.PrefetchScalarGridSpec(
            num_scalar_prefetch=1,
            grid=(FF_HALF // TILE,),
            in_specs=[
                full,
                full,
                full,
                pl.BlockSpec((count, TILE), lambda t, s: (0, jnp.where(s[0] == 0, t, 0))),
                pl.BlockSpec((count, TILE), lambda t, s: (0, jnp.where(s[0] == 0, 0, jnp.minimum(t, 2)))),
                pl.BlockSpec(
                    (count, TILE), lambda t, s: (0, jnp.where(s[0] == 0, 0, jnp.clip(t - 3, 0, 1)))
                ),
            ],
            out_specs=pl.BlockSpec((D, TILE), lambda t, s: (0, t)),
            scratch_shapes=[pltpu.VMEM((D, count), BF)],
        ),
        out_shape=jax.ShapeDtypeStruct((D, FF_HALF), BF),
        compiler_params=params(40),
        cost_estimate=pl.CostEstimate(
            flops=2 * count * D * FF_HALF, bytes_accessed=count * D * 12, transcendentals=0
        ),
        name="ff_weight_grad",
    )(slots, normed, cot, mixed, both, hidden, low)


def doc_marks(doc_lengths, row_count):
    me = lax.axis_index("tok")
    ends = jnp.cumsum(doc_lengths).astype(jnp.int32)
    before = jnp.where(me > 0, ends[jnp.maximum(me - 1, 0)], 0)
    return jnp.stack([before, ends[me], ends[me + 1], me * row_count]).astype(jnp.int32)


def rotary_tables(marks, row_count):
    place = marks[3] + jnp.arange(row_count, dtype=jnp.int32)
    offset = place - jnp.where(place >= marks[1], marks[1], marks[0])
    frequency = 10000.0 ** (-jnp.arange(0, HEAD_DIM, 2, dtype=F32) / HEAD_DIM)
    angles = offset.astype(F32)[:, None] * frequency[None, :]
    cosine = jnp.cos(angles)
    sine = jnp.sin(angles)
    return (
        jnp.concatenate([cosine] * 4, axis=1),
        jnp.concatenate([-sine, sine, -sine, sine], axis=1),
    )


def passed_along(value, steps):
    count = lax.axis_size("tok")
    first, last = (max(0, -steps), min(count, count - steps))
    return lax.ppermute(value, "tok", [(at, at + steps) for at in range(first, last)])


STAGED_DEVICES = 32


def staged():
    return lax.axis_size("tok") == STAGED_DEVICES


def exchange(value, by_core):
    pairs = [(at, at ^ by_core[at & 1]) for at in range(lax.axis_size("tok"))]
    return lax.ppermute(value, "tok", pairs)


CORE = (1, 1)
DEEP = tuple((step << 3, step << 3) for step in range(4))
NEAR = (2, 4)
FAR = (4, 2)


def slot_codes(core):
    slot = jnp.arange(16, dtype=jnp.int32)
    depth, near, far = (slot & 3, (slot >> 2) & 1, slot >> 3)
    return (depth << 2) | jnp.where(core == 0, (far << 1) | near, (near << 1) | far)


def chip_slots(chip, core):
    code = jnp.arange(16, dtype=jnp.int32) ^ chip
    depth, second, first = (code >> 2, (code >> 1) & 1, code & 1)
    return depth | jnp.where(core == 0, (second << 3) | (first << 2), (first << 3) | (second << 2))


def assemble_kernel(places_ref, held_ref, far_ref, other_held_ref, other_far_ref, out_ref, sems):
    core = places_ref[32]
    copies = []
    for index, source in enumerate((held_ref, far_ref, other_held_ref, other_far_ref)):
        half = core if index < 2 else 1 - core
        for slot in range(8):
            at = index * 8 + slot
            place = pl.multiple_of(places_ref[at] * CHIP_ROWS, 16)
            copies.append(
                pltpu.make_async_copy(
                    source.at[pl.ds(slot * CHIP_ROWS, CHIP_ROWS)],
                    out_ref.at[half, pl.ds(place, CHIP_ROWS)],
                    sems.at[at],
                )
            )
    for copy in copies:
        copy.start()
    for copy in copies:
        copy.wait()


def assemble(held, far, other_held, other_far):
    me = lax.axis_index("tok")
    core = me & 1
    chip = me >> 1
    places = jnp.concatenate(
        [slot_codes(core) ^ chip, slot_codes(1 - core) ^ chip, jnp.full((1,), core, jnp.int32)]
    )
    width = held.shape[1]
    return pl.pallas_call(
        assemble_kernel,
        in_specs=[SMEM, ANY, ANY, ANY, ANY],
        out_specs=ANY,
        out_shape=jax.ShapeDtypeStruct((2, D, width), BF),
        scratch_shapes=[pltpu.SemaphoreType.DMA((32,))],
        compiler_params=params(16),
        cost_estimate=pl.CostEstimate(flops=0, bytes_accessed=8 * D * width, transcendentals=0),
        name="assemble",
    )(places, held, far, other_held, other_far)


def gathered(shard):
    if not staged():
        full = lax.all_gather(shard, "tok", axis=0, tiled=True)
        half = full.shape[1] // 2
        return jnp.stack([full[:, :half], full[:, half:]])
    core = lax.axis_index("tok") & 1
    half = shard.shape[1] // 2
    keep = jnp.where(core == 0, shard[:, :half], shard[:, half:])
    send = jnp.where(core == 0, shard[:, half:], shard[:, :half])
    came = exchange(send, CORE)
    piece = jnp.concatenate(
        [jnp.where(core == 0, keep, came), jnp.where(core == 0, came, keep)], axis=0
    )
    held = jnp.concatenate([piece] + [exchange(piece, DEEP[step]) for step in (1, 2, 3)], axis=0)
    held = jnp.concatenate([held, exchange(held, NEAR)], axis=0)
    far = exchange(held, FAR)
    return assemble(held, far, exchange(held, CORE), exchange(far, CORE))


def added(left, right):
    return (left.astype(F32) + right.astype(F32)).astype(BF)


def scattered(keep, send):
    if not staged():
        full = jnp.concatenate([keep, send], axis=1)
        return lax.psum_scatter(full.astype(F32), "tok", scatter_dimension=0, tiled=True)
    core = lax.axis_index("tok") & 1
    came = exchange(send, CORE)
    near, far = (added(keep[:384], came[:384]), added(keep[384:], came[384:]))
    came = exchange(far, FAR)
    near, far = (added(near[:192], came[:192]), added(near[192:], came[192:]))
    came = exchange(far, NEAR)
    parts = [
        added(near[first : first + CHIP_ROWS], came[first : first + CHIP_ROWS])
        for first in range(0, 192, CHIP_ROWS)
    ]
    total = parts[0].astype(F32)
    for step in (1, 2, 3):
        total = total + exchange(parts[step], DEEP[step]).astype(F32)
    share = CHIP_ROWS // 2
    lower, upper = (total[:share], total[share:])
    own = jnp.where(core == 0, lower, upper)
    came = exchange(jnp.where(core == 0, upper, lower), CORE)
    return jnp.concatenate(
        [jnp.where(core == 0, own, came), jnp.where(core == 0, came, own)], axis=1
    )


def on_device(
    tokens,
    doc_lengths,
    first_gain,
    qkv_weight,
    attn_weight,
    second_gain,
    feed_in_weight,
    feed_out_weight,
    cotangent,
):
    row_count = tokens.shape[0]
    share = first_gain.shape[0]

    def spread(gain):
        return jnp.broadcast_to(gain[:, None], (share, LANES))

    shard_one = jnp.concatenate(
        [
            qkv_weight[:, :QKV_HALF],
            spread(first_gain),
            qkv_weight[:, QKV_HALF:],
            spread(second_gain),
        ],
        axis=1,
    )
    shard_two = jnp.concatenate(
        [
            feed_in_weight,
            feed_out_weight.T,
            attn_weight,
            jnp.zeros((share, FF_HALF - FF - D), BF),
        ],
        axis=1,
    )
    marks = doc_marks(doc_lengths, row_count)
    cosine, sine = rotary_tables(marks, row_count)
    weights_one = gathered(shard_one)
    weights_two = gathered(shard_two)
    gain_one = weights_one[0, :, QKV_HALF].astype(F32)[None]
    gain_two = weights_one[1, :, QKV_HALF].astype(F32)[None]
    normed, qkv = project_qkv(tokens, gain_one, weights_one, cosine, sine)
    lower = passed_along(qkv[row_count - HALF :, D:], 1)
    upper = passed_along(qkv[:HALF, D:], -1)
    mixed, logs = attend(marks, qkv, lower, upper)
    result, normed_two, both, hidden, low, mixed_grad, grad = middle(
        tokens, mixed, cotangent, gain_two, weights_two
    )
    if staged():
        me = lax.axis_index("tok")
        halves = (me & 1, 1 - (me & 1))
    else:
        halves = (0, 1)

    def order(half):
        if staged():
            slots = chip_slots(lax.axis_index("tok") >> 1, half)
        else:
            slots = jnp.arange(D // CHIP_ROWS, dtype=jnp.int32)
        return jnp.concatenate([jnp.full((1,), half, jnp.int32), slots])

    grads_ff = [
        ff_weight_grad(order(half), normed_two, cotangent, mixed, both, hidden, low)
        for half in halves
    ]
    dqkv, edge, away = attend_back(marks, qkv, mixed_grad, logs, cosine, sine, lower, upper)
    from_upper = passed_along(away[:HALF], -1)
    from_lower = passed_along(away[HALF:], 1)
    dqkv = patch(edge, jnp.concatenate([from_lower, from_upper], axis=0), cosine, sine, dqkv)
    grads_qkv = [qkv_weight_grad(order(half), normed, dqkv) for half in halves]
    grad_in = input_grad(tokens, gain_one, weights_one, dqkv, grad)
    sum_ff = scattered(*grads_ff)
    sum_qkv = scattered(*grads_qkv)
    sent_in = sum_ff[:, : 2 * FF]
    sent_down = sum_ff[:, 2 * FF : 3 * FF].T
    sent_attn = sum_ff[:, 3 * FF : 3 * FF + D]

    def gain_grad(summed, weight, gain):
        return jnp.sum(summed * weight.astype(F32), axis=1) / gain.astype(F32)

    return (
        result,
        grad_in,
        gain_grad(sum_qkv, qkv_weight, first_gain),
        sum_qkv,
        sent_attn,
        gain_grad(sent_in, feed_in_weight, second_gain),
        sent_in,
        sent_down,
    )


def solution(mesh):
    in_specs = (
        P("tok", None),
        P(),
        P("tok"),
        P("tok", None),
        P("tok", None),
        P("tok"),
        P("tok", None),
        P(None, "tok"),
        P("tok", None),
    )
    out_specs = (
        P("tok", None),
        P("tok", None),
        P("tok"),
        P("tok", None),
        P("tok", None),
        P("tok"),
        P("tok", None),
        P(None, "tok"),
    )
    return jax.shard_map(
        on_device, mesh=mesh, in_specs=in_specs, out_specs=out_specs, check_vma=False
    )
```

```python
from functools import partial

import jax
import jax.numpy as jnp
from jax import lax
from jax.experimental import pallas as pl
from jax.experimental.pallas import tpu as pltpu
from jax.sharding import PartitionSpec as P

D = 768
FF = 1152
HEADS = 12
HEAD_DIM = 64
HALF = 64
PAIRS = HEADS // 2
BLOCK = 128
SPAN = BLOCK + 2 * HALF
LANES = 128
QKV_HALF = 3 * D // 2
GROUP = D // 2
GROUP_PAIRS = PAIRS // 2
FF_HALF = 2 * FF
MIB = 1024 * 1024
BF = jnp.bfloat16
F32 = jnp.float32


def dot(left, right, left_dim=1, right_dim=0):
    return lax.dot_general(
        left, right, (((left_dim,), (right_dim,)), ((), ())), preferred_element_type=F32
    )


def params(mib):
    return pltpu.CompilerParams(vmem_limit_bytes=mib * MIB)


def whole(shape):
    return pl.BlockSpec(shape, lambda *_: (0,) * len(shape))


def rows(shape):
    return pl.BlockSpec(shape, lambda i: (i,) + (0,) * (len(shape) - 1))


SMEM = pl.BlockSpec(memory_space=pltpu.SMEM)
ANY = pl.BlockSpec(memory_space=pl.ANY)
VMEM = pl.BlockSpec(memory_space=pltpu.VMEM)


def lane_ids(shape):
    return lax.broadcasted_iota(jnp.int32, shape, len(shape) - 1)


def swap_halves(values):
    low = (lane_ids(values.shape) & (HEAD_DIM - 1)) < HEAD_DIM // 2
    return jnp.where(
        low, pltpu.roll(values, LANES - HEAD_DIM // 2, 1), pltpu.roll(values, HEAD_DIM // 2, 1)
    )


def normalized(values):
    centered = values - jnp.mean(values, axis=-1, keepdims=True)
    scale = lax.rsqrt(jnp.mean(centered * centered, axis=-1, keepdims=True) + 1e-05)
    return centered * scale, scale


def norm_back(grad, unit, scale, gains):
    grad_unit = grad * gains
    return scale * (
        grad_unit
        - jnp.mean(grad_unit, axis=-1, keepdims=True)
        - unit * jnp.mean(grad_unit * unit, axis=-1, keepdims=True)
    )


CHIP_ROWS = 48


class Weights:
    def __init__(self, arrays, places=None):
        self.arrays = arrays
        self.places = places

    def operands(self):
        if self.places is None:
            return list(self.arrays)
        return [self.places, *self.arrays]

    def specs(self):
        if self.places is None:
            return [ANY]
        return [SMEM, VMEM, VMEM, VMEM, VMEM]

    def scratch(self):
        width = self.arrays[0].shape[-1]
        return [pltpu.VMEM((2, D, width), BF), pltpu.SemaphoreType.DMA((1,))]


def load_weights(refs, out_ref, sems):
    if len(refs) == 1:
        copy = pltpu.make_async_copy(refs[0], out_ref, sems.at[0])
        copy.start()
        copy.wait()
        return
    places_ref = refs[0]
    core = places_ref[32]
    for index, source in enumerate(refs[1:]):
        half = core if index < 2 else 1 - core
        for slot in range(8):
            place = pl.multiple_of(places_ref[index * 8 + slot] * CHIP_ROWS, 16)
            out_ref[half, pl.ds(place, CHIP_ROWS), :] = source[
                slot * CHIP_ROWS : (slot + 1) * CHIP_ROWS, :
            ]


def qkv_kernel(count, x_ref, cos_ref, sin_ref, *refs):
    weight_refs = refs[:count]
    normed_ref, qkv_ref, gains_ref, w_ref, sems = refs[count:]

    @pl.when(pl.program_id(0) == 0)
    def _():
        load_weights(weight_refs, w_ref, sems)
        for half in range(2):
            turned = w_ref[half, :, QKV_HALF:].T.astype(F32)
            gains_ref[half * 8 : half * 8 + 8, :] = turned[:8]

    unit, _ = normalized(x_ref[...].astype(F32))
    normed = (unit * gains_ref[0:1, :]).astype(BF)
    normed_ref[...] = normed
    cosine = cos_ref[...]
    sine = sin_ref[...]
    for half in range(2):
        merged = dot(normed, w_ref[half, :, :QKV_HALF])
        for tile in range(QKV_HALF // LANES):
            lanes = slice(tile * LANES, (tile + 1) * LANES)
            part = merged[:, lanes]
            if tile * LANES < 2 * GROUP:
                part = part * cosine + swap_halves(part) * sine
            qkv_ref[half, :, lanes] = part.astype(BF)


def project_qkv(tokens, weights, cosine, sine):
    count = tokens.shape[0]
    size = min(256, count)
    operands = weights.operands()
    return pl.pallas_call(
        partial(qkv_kernel, len(operands)),
        grid=(count // size,),
        in_specs=[rows((size, D)), rows((size, LANES)), rows((size, LANES)), *weights.specs()],
        out_specs=[
            rows((size, D)),
            pl.BlockSpec((2, size, QKV_HALF), lambda i: (0, i, 0)),
            whole((16, D)),
        ],
        out_shape=[
            jax.ShapeDtypeStruct((count, D), BF),
            jax.ShapeDtypeStruct((2, count, QKV_HALF), BF),
            jax.ShapeDtypeStruct((16, D), F32),
        ],
        scratch_shapes=weights.scratch(),
        compiler_params=params(32),
        cost_estimate=pl.CostEstimate(
            flops=2 * count * D * 3 * D, bytes_accessed=count * D * 10 + 6 * D * D, transcendentals=0
        ),
        name="qkv",
    )(tokens, cosine, sine, *operands)


def window_bias(marks_ref, block):
    shape = (SPAN, 2 * BLOCK)
    first = marks_ref[3] + block * BLOCK
    key = lax.broadcasted_iota(jnp.int32, shape, 0)
    query = lax.broadcasted_iota(jnp.int32, (1, 2 * BLOCK), 1) & (BLOCK - 1)
    place = first + query
    lowest = query
    highest = query + 2 * HALF
    for index in range(3):
        mark = marks_ref[index]
        edge = mark - first + HALF
        past = place >= mark
        lowest = jnp.where(past, jnp.maximum(lowest, edge), lowest)
        highest = jnp.where(past, highest, jnp.minimum(highest, edge - 1))
    return jnp.where((key >= lowest) & (key <= highest), 0.0, -1e30).astype(F32)


def stacked(pair):
    low = lane_ids(pair.shape) < HEAD_DIM
    zero = jnp.zeros_like(pair)
    return jnp.concatenate([jnp.where(low, pair, zero), jnp.where(low, zero, pair)], axis=0)


def unstacked(both):
    low = lane_ids((BLOCK, LANES)) < HEAD_DIM
    return jnp.where(low, both[:BLOCK], both[BLOCK:])


def attend_kernel(marks_ref, query_ref, qkv_ref, lower_ref, upper_ref, out_ref, log_ref, span_ref, sems):
    block = pl.program_id(0)
    count = qkv_ref.shape[1]

    @pl.when(block == 0)
    def _():
        copies = []
        for half in range(2):
            copies += [
                pltpu.make_async_copy(
                    qkv_ref.at[half, :, pl.ds(GROUP, 2 * GROUP)],
                    span_ref.at[half, pl.ds(HALF, count)],
                    sems.at[3 * half],
                ),
                pltpu.make_async_copy(
                    lower_ref.at[half], span_ref.at[half, pl.ds(0, HALF)], sems.at[3 * half + 1]
                ),
                pltpu.make_async_copy(
                    upper_ref.at[half],
                    span_ref.at[half, pl.ds(HALF + count, HALF)],
                    sems.at[3 * half + 2],
                ),
            ]
        for copy in copies:
            copy.start()
        for copy in copies:
            copy.wait()

    bias = window_bias(marks_ref, block)
    window = pl.ds(pl.multiple_of(block * BLOCK, BLOCK), SPAN)
    for pair in range(PAIRS):
        half = pair // GROUP_PAIRS
        first = (pair % GROUP_PAIRS) * LANES
        lanes = slice(first, first + LANES)
        query = stacked(query_ref[half, :, lanes] * BF(0.125))
        keys = span_ref[half, window, lanes]
        values = span_ref[half, window, GROUP + first : GROUP + first + LANES]
        scores = dot(keys, query, 1, 1) + bias
        peak = jnp.max(scores, axis=0, keepdims=True)
        expo = jnp.exp(scores - peak)
        total = jnp.sum(expo, axis=0, keepdims=True)
        weights = (expo * (1.0 / total)).astype(BF)
        out_ref[:, pair * LANES : (pair + 1) * LANES] = unstacked(dot(weights, values, 0, 0)).astype(BF)
        log_ref[0, half, pair % GROUP_PAIRS : pair % GROUP_PAIRS + 1, :] = peak + jnp.log(total)


def attend(marks, qkv, lower, upper):
    count = qkv.shape[1]
    blocks = count // BLOCK
    return pl.pallas_call(
        attend_kernel,
        grid=(blocks,),
        in_specs=[SMEM, pl.BlockSpec((2, BLOCK, GROUP), lambda i: (0, i, 0)), ANY, ANY, ANY],
        out_specs=[rows((BLOCK, D)), rows((1, 2, 8, 2 * BLOCK))],
        out_shape=[
            jax.ShapeDtypeStruct((count, D), BF),
            jax.ShapeDtypeStruct((blocks, 2, 8, 2 * BLOCK), F32),
        ],
        scratch_shapes=[
            pltpu.VMEM((2, count + 2 * HALF, 2 * GROUP), BF),
            pltpu.SemaphoreType.DMA((6,)),
        ],
        compiler_params=params(32),
        cost_estimate=pl.CostEstimate(
            flops=4 * count * SPAN * D * 2, bytes_accessed=count * D * 10, transcendentals=0
        ),
        name="attend",
    )(marks, qkv, qkv, lower, upper)


FF_PARTS = tuple((first, min(256, FF - first)) for first in range(0, FF, 256))


def middle_kernel(
    x_ref,
    mixed_ref,
    cot_ref,
    gains_ref,
    w_ref,
    result_ref,
    normed_ref,
    both_ref,
    hidden_ref,
    low_ref,
    mixed_grad_ref,
    grad_ref,
):
    gain = gains_ref[8:9, :]
    cot = cot_ref[...]
    weight_attn = w_ref[:, 3 * FF :]
    residual = x_ref[...].astype(F32) + dot(mixed_ref[...], weight_attn)
    unit, scale = normalized(residual)
    normed = (unit * gain).astype(BF)
    normed_ref[...] = normed
    result = residual
    grad_normed = None
    for first, size in FF_PARTS:
        gate_cols = slice(first, first + size)
        down_cols = slice(2 * FF + first, 2 * FF + first + size)
        up_cols = slice(FF + first, FF + first + size)
        gate = dot(normed, w_ref[:, gate_cols])
        up = dot(normed, w_ref[:, up_cols])
        grad_hidden = dot(cot, w_ref[:, down_cols])
        share = 0.5 + 0.5 * lax.erf(gate * 0.7071067811865476)
        active = gate * share
        slope = share + gate * (jnp.exp(-0.5 * gate * gate) * 0.3989422804014327)
        hidden = (active * up).astype(BF)
        hidden_ref[:, gate_cols] = hidden
        grad_gate = (grad_hidden * up * slope).astype(BF)
        grad_up = (grad_hidden * active).astype(BF)
        both_ref[:, gate_cols] = grad_gate
        both_ref[:, up_cols] = grad_up
        result = result + dot(hidden, w_ref[:, down_cols], 1, 1)
        piece = dot(grad_gate, w_ref[:, gate_cols], 1, 1) + dot(
            grad_up, w_ref[:, up_cols], 1, 1
        )
        grad_normed = piece if grad_normed is None else grad_normed + piece
    result_ref[...] = result.astype(BF)
    grad = cot.astype(F32) + norm_back(grad_normed, unit, scale, gain)
    grad_ref[...] = grad
    low = grad.astype(BF)
    low_ref[...] = low
    mixed_grad_ref[...] = dot(low, weight_attn, 1, 1).astype(BF)


def middle(tokens, mixed, cotangent, gains, weights):
    count = tokens.shape[0]
    size = min(256, count)
    wide = [(D, BF), (D, BF), (2 * FF, BF), (FF, BF), (D, BF), (D, BF), (D, F32)]
    return pl.pallas_call(
        middle_kernel,
        grid=(count // size,),
        in_specs=[
            rows((size, D)),
            rows((size, D)),
            rows((size, D)),
            whole((16, D)),
            whole(weights.shape),
        ],
        out_specs=[rows((size, width)) for width, _ in wide],
        out_shape=[jax.ShapeDtypeStruct((count, width), kind) for width, kind in wide],
        compiler_params=params(48),
        cost_estimate=pl.CostEstimate(
            flops=4 * count * D * (D + 3 * FF), bytes_accessed=count * D * 30, transcendentals=0
        ),
        name="middle",
    )(tokens, mixed, cotangent, gains, weights)


def pair_back(query, keys, values, out_grad, logs, bias):
    scores = dot(keys, query, 1, 1) + bias
    weights = jnp.exp(scores - logs)
    weight_grad = dot(values, out_grad, 1, 1)
    score_grad = weights * (weight_grad - jnp.sum(weights * weight_grad, axis=0, keepdims=True))
    score_grad = score_grad.astype(BF)
    key_grad = dot(score_grad, query)
    value_grad = dot(weights.astype(BF), out_grad)
    query_grad = unstacked(dot(score_grad, keys, 0, 0)) * 0.125
    return query_grad, key_grad, value_grad


def turned_back(values, cosine, sine):
    return values * cosine - swap_halves(values) * sine


def edge_back_kernel(
    marks_ref,
    query_ref,
    mixed_grad_ref,
    log_ref,
    cos_ref,
    sin_ref,
    qkv_ref,
    lower_ref,
    upper_ref,
    grad_ref,
    sum_ref,
    away_ref,
    span_ref,
    sems,
):
    side = pl.program_id(0)
    count = qkv_ref.shape[1]

    def fetch(own_first, own_place, halo_ref, halo_place):
        copies = []
        for half in range(2):
            copies += [
                pltpu.make_async_copy(
                    qkv_ref.at[half, pl.ds(own_first, SPAN - HALF), pl.ds(GROUP, 2 * GROUP)],
                    span_ref.at[half, pl.ds(own_place, SPAN - HALF)],
                    sems.at[2 * half],
                ),
                pltpu.make_async_copy(
                    halo_ref.at[half], span_ref.at[half, pl.ds(halo_place, HALF)], sems.at[2 * half + 1]
                ),
            ]
        for copy in copies:
            copy.start()
        for copy in copies:
            copy.wait()

    @pl.when(side == 0)
    def _():
        fetch(0, HALF, lower_ref, 0)

    @pl.when(side == 1)
    def _():
        fetch(count - SPAN + HALF, 0, upper_ref, SPAN - HALF)

    bias = window_bias(marks_ref, side * (count // BLOCK - 1))
    cosine = cos_ref[...]
    sine = sin_ref[...]
    for pair in range(PAIRS):
        half = pair // GROUP_PAIRS
        sub = pair % GROUP_PAIRS
        lanes = slice(sub * LANES, (sub + 1) * LANES)
        value_lanes = slice(GROUP + sub * LANES, GROUP + (sub + 1) * LANES)
        query_grad, key_grad, value_grad = pair_back(
            stacked(query_ref[half, :, lanes] * BF(0.125)),
            span_ref[half, :, lanes],
            span_ref[half, :, value_lanes],
            stacked(mixed_grad_ref[:, pair * LANES : (pair + 1) * LANES]),
            log_ref[0, half, sub : sub + 1, :],
            bias,
        )
        grad_ref[half, 0, :, lanes] = turned_back(query_grad, cosine, sine).astype(BF)
        sum_ref[half, 0, :, lanes] = key_grad
        sum_ref[half, 0, :, value_lanes] = value_grad

    @pl.when(side == 0)
    def _():
        for half in range(2):
            away_ref[0, half] = sum_ref[half, 0, 0:HALF, :].astype(BF)

    @pl.when(side == 1)
    def _():
        for half in range(2):
            away_ref[0, half] = sum_ref[half, 0, SPAN - HALF :, :].astype(BF)


def edge_back(marks, qkv, mixed_grad, logs, cosine, sine, lower, upper):
    count = qkv.shape[1]
    last = count // BLOCK - 1
    return pl.pallas_call(
        edge_back_kernel,
        grid=(2,),
        in_specs=[
            SMEM,
            pl.BlockSpec((2, BLOCK, GROUP), lambda i: (0, i * last, 0)),
            pl.BlockSpec((BLOCK, D), lambda i: (i * last, 0)),
            pl.BlockSpec((1, 2, 8, 2 * BLOCK), lambda i: (i * last, 0, 0, 0)),
            pl.BlockSpec((BLOCK, LANES), lambda i: (i * last, 0)),
            pl.BlockSpec((BLOCK, LANES), lambda i: (i * last, 0)),
            ANY,
            ANY,
            ANY,
        ],
        out_specs=[
            pl.BlockSpec((2, 1, BLOCK, GROUP), lambda i: (0, i, 0, 0)),
            pl.BlockSpec((2, 1, SPAN, 2 * GROUP), lambda i: (0, i, 0, 0)),
            pl.BlockSpec((1, 2, HALF, 2 * GROUP), lambda i: (i, 0, 0, 0)),
        ],
        out_shape=[
            jax.ShapeDtypeStruct((2, 2, BLOCK, GROUP), BF),
            jax.ShapeDtypeStruct((2, 2, SPAN, 2 * GROUP), F32),
            jax.ShapeDtypeStruct((2, 2, HALF, 2 * GROUP), BF),
        ],
        scratch_shapes=[
            pltpu.VMEM((2, SPAN, 2 * GROUP), BF),
            pltpu.SemaphoreType.DMA((4,)),
        ],
        compiler_params=params(32),
        cost_estimate=pl.CostEstimate(
            flops=10 * 2 * BLOCK * SPAN * D * 2, bytes_accessed=BLOCK * D * 20, transcendentals=0
        ),
        name="edge_back",
    )(marks, qkv, mixed_grad, logs, cosine, sine, qkv, lower, upper)


def inner_back_kernel(
    group_ref,
    marks_ref,
    query_ref,
    mixed_grad_ref,
    log_ref,
    cos_ref,
    sin_ref,
    edge_grad_ref,
    edge_sum_ref,
    from_lower_ref,
    from_upper_ref,
    qkv_ref,
    *rest,
):
    grad_ref, span_ref, sum_ref, sems = rest[-4:]
    step = pl.program_id(0)
    block = step + 1
    count = qkv_ref.shape[1]

    @pl.when(step == 0)
    def _():
        copy = pltpu.make_async_copy(
            qkv_ref.at[group_ref[0], :, pl.ds(GROUP, 2 * GROUP)], span_ref, sems.at[0]
        )
        copy.start()
        sum_ref[0 : SPAN - HALF, :] = edge_sum_ref[0, 0, HALF:, :]
        sum_ref[0:HALF, :] += from_lower_ref[0].astype(F32)
        grad_ref[0:BLOCK, 0:GROUP] = edge_grad_ref[0, 0]
        grad_ref[count - BLOCK :, 0:GROUP] = edge_grad_ref[0, 1]
        copy.wait()

    bias = window_bias(marks_ref, block)
    start = pl.multiple_of(block * BLOCK - HALF, HALF)
    window = pl.ds(start, SPAN)
    older = pl.ds(start, BLOCK)
    newer = pl.ds(pl.multiple_of(start + BLOCK, HALF), BLOCK)
    mine = pl.ds(pl.multiple_of(block * BLOCK, BLOCK), BLOCK)
    cosine = cos_ref[mine, :]
    sine = sin_ref[mine, :]

    def finish(place):
        own_cosine = cos_ref[place, :]
        own_sine = sin_ref[place, :]
        for sub in range(GROUP_PAIRS):
            lanes = slice(sub * LANES, (sub + 1) * LANES)
            key_lanes = slice(GROUP + sub * LANES, GROUP + (sub + 1) * LANES)
            grad_ref[place, key_lanes] = turned_back(
                sum_ref[place, lanes], own_cosine, own_sine
            ).astype(BF)
        grad_ref[place, 2 * GROUP :] = sum_ref[place, GROUP:].astype(BF)

    for sub in range(GROUP_PAIRS):
        lanes = slice(sub * LANES, (sub + 1) * LANES)
        value_lanes = slice(GROUP + sub * LANES, GROUP + (sub + 1) * LANES)
        query_grad, key_grad, value_grad = pair_back(
            stacked(query_ref[0, :, lanes] * BF(0.125)),
            span_ref[window, lanes],
            span_ref[window, value_lanes],
            stacked(mixed_grad_ref[:, lanes]),
            log_ref[0, 0, sub : sub + 1, :],
            bias,
        )
        sum_ref[older, lanes] += key_grad[:BLOCK]
        sum_ref[newer, lanes] = key_grad[BLOCK:]
        sum_ref[older, value_lanes] += value_grad[:BLOCK]
        sum_ref[newer, value_lanes] = value_grad[BLOCK:]
        grad_ref[mine, lanes] = turned_back(query_grad, cosine, sine).astype(BF)

    finish(older)

    @pl.when(step == 0)
    def _():
        finish(pl.ds(0, HALF))

    @pl.when(step == pl.num_programs(0) - 1)
    def _():
        tail = SPAN - HALF
        sum_ref[count - tail : count - HALF, :] += edge_sum_ref[0, 1, 0:BLOCK, :]
        sum_ref[count - HALF :, :] = edge_sum_ref[0, 1, BLOCK:tail, :] + from_upper_ref[0].astype(F32)
        finish(pl.ds(count - tail, tail))


def inner_back(group, marks, qkv, mixed_grad, logs, cosine, sine, edge_grad, edge_sum, from_lower, from_upper, after):
    count = qkv.shape[1]
    steps = count // BLOCK - 2
    return pl.pallas_call(
        inner_back_kernel,
        grid_spec=pltpu.PrefetchScalarGridSpec(
            num_scalar_prefetch=1,
            grid=(steps,),
            in_specs=[
                SMEM,
                pl.BlockSpec((1, BLOCK, GROUP), lambda i, g: (g[0], i + 1, 0)),
                pl.BlockSpec((BLOCK, GROUP), lambda i, g: (i + 1, g[0])),
                pl.BlockSpec((1, 1, 8, 2 * BLOCK), lambda i, g: (i + 1, g[0], 0, 0)),
                pl.BlockSpec((count, LANES), lambda i, g: (0, 0)),
                pl.BlockSpec((count, LANES), lambda i, g: (0, 0)),
                pl.BlockSpec((1, 2, BLOCK, GROUP), lambda i, g: (g[0], 0, 0, 0)),
                pl.BlockSpec((1, 2, SPAN, 2 * GROUP), lambda i, g: (g[0], 0, 0, 0)),
                pl.BlockSpec((1, HALF, 2 * GROUP), lambda i, g: (g[0], 0, 0)),
                pl.BlockSpec((1, HALF, 2 * GROUP), lambda i, g: (g[0], 0, 0)),
                ANY,
                *[ANY for _ in after],
            ],
            out_specs=pl.BlockSpec((count, QKV_HALF), lambda i, g: (0, 0)),
            scratch_shapes=[
                pltpu.VMEM((count, 2 * GROUP), BF),
                pltpu.VMEM((count, 2 * GROUP), F32),
                pltpu.SemaphoreType.DMA((1,)),
            ],
        ),
        out_shape=jax.ShapeDtypeStruct((count, QKV_HALF), BF),
        compiler_params=params(32),
        cost_estimate=pl.CostEstimate(
            flops=10 * count * SPAN * D, bytes_accessed=count * D * 10, transcendentals=0
        ),
        name="inner_back",
    )(
        jnp.reshape(group, (1,)).astype(jnp.int32),
        marks,
        qkv,
        mixed_grad,
        logs,
        cosine,
        sine,
        edge_grad,
        edge_sum,
        from_lower,
        from_upper,
        qkv,
        *after,
    )


def input_grad_kernel(count, order_ref, x_ref, gains_ref, first_ref, second_ref, grad_ref, *refs):
    weight_refs = refs[:count]
    out_ref, w_ref, sems = refs[count:]

    @pl.when(pl.program_id(0) == 0)
    def _():
        load_weights(weight_refs, w_ref, sems)

    unit, scale = normalized(x_ref[...].astype(F32))
    half = order_ref[0]
    grad_normed = dot(first_ref[...], w_ref[half, :, :QKV_HALF], 1, 1) + dot(
        second_ref[...], w_ref[1 - half, :, :QKV_HALF], 1, 1
    )
    out_ref[...] = grad_ref[...] + norm_back(grad_normed, unit, scale, gains_ref[0:1, :])


def input_grad(half, tokens, gains, weights, first, second, grad):
    count = tokens.shape[0]
    size = min(256, count)
    operands = weights.operands()
    return pl.pallas_call(
        partial(input_grad_kernel, len(operands)),
        grid=(count // size,),
        in_specs=[
            SMEM,
            rows((size, D)),
            whole((16, D)),
            rows((size, QKV_HALF)),
            rows((size, QKV_HALF)),
            rows((size, D)),
            *weights.specs(),
        ],
        out_specs=rows((size, D)),
        out_shape=jax.ShapeDtypeStruct((count, D), F32),
        scratch_shapes=weights.scratch(),
        compiler_params=params(32),
        cost_estimate=pl.CostEstimate(
            flops=2 * count * D * 3 * D, bytes_accessed=count * D * 16, transcendentals=0
        ),
        name="input_grad",
    )(jnp.reshape(half, (1,)).astype(jnp.int32), tokens, gains, first, second, grad, *operands)


TILE = 384


def store_slots(slots_ref, out_ref, product):
    step = CHIP_ROWS
    for index in range(D // step):
        place = pl.multiple_of(slots_ref[1 + index] * step, 16)
        out_ref[pl.ds(place, step), :] = product[index * step : (index + 1) * step].astype(BF)


def qkv_weight_kernel(slots_ref, normed_ref, grad_ref, *rest):
    out_ref, turned_ref = rest[-2:]

    @pl.when(pl.program_id(0) == 0)
    def _():
        turned_ref[...] = normed_ref[...].T

    store_slots(slots_ref, out_ref, dot(turned_ref[...], grad_ref[...]))


def qkv_weight_grad(slots, normed, dqkv, after=()):
    count = normed.shape[0]
    tiles = QKV_HALF // TILE
    return pl.pallas_call(
        qkv_weight_kernel,
        grid_spec=pltpu.PrefetchScalarGridSpec(
            num_scalar_prefetch=1,
            grid=(tiles,),
            in_specs=[
                pl.BlockSpec((count, D), lambda t, s: (0, 0)),
                pl.BlockSpec((count, TILE), lambda t, s: (0, t)),
                *[ANY for _ in after],
            ],
            out_specs=pl.BlockSpec((D, TILE), lambda t, s: (0, t)),
            scratch_shapes=[pltpu.VMEM((D, count), BF)],
        ),
        out_shape=jax.ShapeDtypeStruct((D, QKV_HALF), BF),
        compiler_params=params(32),
        cost_estimate=pl.CostEstimate(
            flops=2 * count * D * QKV_HALF, bytes_accessed=count * D * 8, transcendentals=0
        ),
        name="qkv_weight_grad",
    )(slots, normed, dqkv, *after)


def ff_weight_kernel(slots_ref, normed_ref, cot_ref, mixed_ref, both_ref, hidden_ref, low_ref, *rest):
    out_ref, turned_ref = rest[-2:]
    step = pl.program_id(0)
    second = slots_ref[0] == 1

    @pl.when((step == 0) & ~second)
    def _():
        turned_ref[...] = normed_ref[...].T

    @pl.when((step == 0) & second)
    def _():
        turned_ref[...] = cot_ref[...].T

    @pl.when((step == 3) & second)
    def _():
        turned_ref[...] = mixed_ref[...].T

    @pl.when(~second)
    def _():
        store_slots(slots_ref, out_ref, dot(turned_ref[...], both_ref[...]))

    @pl.when(second & (step < 3))
    def _():
        store_slots(slots_ref, out_ref, dot(turned_ref[...], hidden_ref[...]))

    @pl.when(second & (step >= 3) & (step < 5))
    def _():
        store_slots(slots_ref, out_ref, dot(turned_ref[...], low_ref[...]))

    @pl.when(second & (step == 5))
    def _():
        out_ref[...] = jnp.zeros_like(out_ref)


def ff_weight_grad(slots, normed, cot, mixed, both, hidden, low, after):
    count = normed.shape[0]
    full = pl.BlockSpec((count, D), lambda t, s: (0, 0))
    return pl.pallas_call(
        ff_weight_kernel,
        grid_spec=pltpu.PrefetchScalarGridSpec(
            num_scalar_prefetch=1,
            grid=(FF_HALF // TILE,),
            in_specs=[
                full,
                full,
                full,
                pl.BlockSpec((count, TILE), lambda t, s: (0, jnp.where(s[0] == 0, t, 0))),
                pl.BlockSpec((count, TILE), lambda t, s: (0, jnp.where(s[0] == 0, 0, jnp.minimum(t, 2)))),
                pl.BlockSpec(
                    (count, TILE), lambda t, s: (0, jnp.where(s[0] == 0, 0, jnp.clip(t - 3, 0, 1)))
                ),
                *[ANY for _ in after],
            ],
            out_specs=pl.BlockSpec((D, TILE), lambda t, s: (0, t)),
            scratch_shapes=[pltpu.VMEM((D, count), BF)],
        ),
        out_shape=jax.ShapeDtypeStruct((D, FF_HALF), BF),
        compiler_params=params(40),
        cost_estimate=pl.CostEstimate(
            flops=2 * count * D * FF_HALF, bytes_accessed=count * D * 12, transcendentals=0
        ),
        name="ff_weight_grad",
    )(slots, normed, cot, mixed, both, hidden, low, *after)


def doc_marks(doc_lengths, row_count):
    me = lax.axis_index("tok")
    ends = jnp.cumsum(doc_lengths).astype(jnp.int32)
    before = jnp.where(me > 0, ends[jnp.maximum(me - 1, 0)], 0)
    return jnp.stack([before, ends[me], ends[me + 1], me * row_count]).astype(jnp.int32)


def rotary_tables(marks, row_count):
    place = marks[3] + jnp.arange(row_count, dtype=jnp.int32)
    offset = place - jnp.where(place >= marks[1], marks[1], marks[0])
    frequency = 10000.0 ** (-jnp.arange(0, HEAD_DIM, 2, dtype=F32) / HEAD_DIM)
    angles = offset.astype(F32)[:, None] * frequency[None, :]
    cosine = jnp.cos(angles)
    sine = jnp.sin(angles)
    return (
        jnp.concatenate([cosine] * 4, axis=1),
        jnp.concatenate([-sine, sine, -sine, sine], axis=1),
    )


def passed_along(value, steps):
    count = lax.axis_size("tok")
    first, last = (max(0, -steps), min(count, count - steps))
    return lax.ppermute(value, "tok", [(at, at + steps) for at in range(first, last)])


STAGED_DEVICES = 32


def staged():
    return lax.axis_size("tok") == STAGED_DEVICES


def exchange(value, by_core):
    pairs = [(at, at ^ by_core[at & 1]) for at in range(lax.axis_size("tok"))]
    return lax.ppermute(value, "tok", pairs)


CORE = (1, 1)
DEEP = tuple((step << 3, step << 3) for step in range(4))
NEAR = (2, 4)
FAR = (4, 2)


def slot_codes(core):
    slot = jnp.arange(16, dtype=jnp.int32)
    depth, near, far = (slot & 3, (slot >> 2) & 1, slot >> 3)
    return (depth << 2) | jnp.where(core == 0, (far << 1) | near, (near << 1) | far)


def chip_slots(chip, core):
    code = jnp.arange(16, dtype=jnp.int32) ^ chip
    depth, second, first = (code >> 2, (code >> 1) & 1, code & 1)
    return depth | jnp.where(core == 0, (second << 3) | (first << 2), (first << 3) | (second << 2))


def stage_after(value, *others):
    return lax.optimization_barrier((value, *others))[0]


def core_pieces(shard):
    core = lax.axis_index("tok") & 1
    half = shard.shape[1] // 2
    keep = jnp.where(core == 0, shard[:, :half], shard[:, half:])
    send = jnp.where(core == 0, shard[:, half:], shard[:, :half])
    came = exchange(send, CORE)
    return jnp.concatenate(
        [jnp.where(core == 0, keep, came), jnp.where(core == 0, came, keep)], axis=0
    )


def deep_gather(piece):
    return jnp.concatenate([piece] + [exchange(piece, DEEP[step]) for step in (1, 2, 3)], axis=0)


def final_gather(held, far):
    me = lax.axis_index("tok")
    core = me & 1
    chip = me >> 1
    places = jnp.concatenate(
        [slot_codes(core) ^ chip, slot_codes(1 - core) ^ chip, jnp.full((1,), core, jnp.int32)]
    )
    return Weights([held, far, exchange(held, CORE), exchange(far, CORE)], places)


def whole_weights(shard):
    full = lax.all_gather(shard, "tok", axis=0, tiled=True)
    half = full.shape[1] // 2
    return Weights([jnp.stack([full[:, :half], full[:, half:]])])


def added(left, right):
    return (left.astype(F32) + right.astype(F32)).astype(BF)


def core_sum(keep, came):
    return added(keep[:384], came[:384]), added(keep[384:], came[384:])


def far_sum(near, came):
    return added(near[:192], came[:192]), added(near[192:], came[192:])


def near_sum(near, came):
    return [
        added(near[first : first + CHIP_ROWS], came[first : first + CHIP_ROWS])
        for first in range(0, 192, CHIP_ROWS)
    ]


def deep_sum(parts, after):
    core = lax.axis_index("tok") & 1
    total = parts[0].astype(F32)
    for step in (1, 2, 3):
        total = total + stage_after(exchange(parts[step], DEEP[step]), after).astype(F32)
    share = CHIP_ROWS // 2
    lower, upper = (total[:share], total[share:])
    own = jnp.where(core == 0, lower, upper)
    came = exchange(jnp.where(core == 0, upper, lower), CORE)
    return jnp.concatenate(
        [jnp.where(core == 0, own, came), jnp.where(core == 0, came, own)], axis=1
    )


def summed(keep, send):
    full = jnp.concatenate([keep, send], axis=1)
    return lax.psum_scatter(full.astype(F32), "tok", scatter_dimension=0, tiled=True)


def by_part(groups):
    return jnp.concatenate(
        [
            groups[:, half * QKV_HALF + part * GROUP : half * QKV_HALF + (part + 1) * GROUP]
            for part in range(3)
            for half in range(2)
        ],
        axis=1,
    )


def on_device(
    tokens,
    doc_lengths,
    first_gain,
    qkv_weight,
    attn_weight,
    second_gain,
    feed_in_weight,
    feed_out_weight,
    cotangent,
):
    row_count = tokens.shape[0]
    share = first_gain.shape[0]

    def spread(gain):
        return jnp.broadcast_to(gain[:, None], (share, LANES))

    def group_of(half):
        return [
            qkv_weight[:, part * D + half * GROUP : part * D + (half + 1) * GROUP]
            for part in range(3)
        ]

    shard_one = jnp.concatenate(
        [*group_of(0), spread(first_gain), *group_of(1), spread(second_gain)], axis=1
    )
    shard_two = jnp.concatenate([feed_in_weight, feed_out_weight.T, attn_weight], axis=1)
    weights_two = lax.all_gather(shard_two, "tok", axis=0, tiled=True)
    marks = doc_marks(doc_lengths, row_count)
    cosine, sine = rotary_tables(marks, row_count)
    if staged():
        one = deep_gather(core_pieces(shard_one))
        one = jnp.concatenate([one, exchange(one, NEAR)], axis=0)
        weights_one = final_gather(one, exchange(one, FAR))
    else:
        weights_one = whole_weights(shard_one)
    normed, qkv, gains = project_qkv(tokens, weights_one, cosine, sine)
    lower = passed_along(qkv[:, row_count - HALF :, GROUP:], 1)
    upper = passed_along(qkv[:, :HALF, GROUP:], -1)
    mixed, logs = attend(marks, qkv, lower, upper)
    result, normed_two, both, hidden, low, mixed_grad, grad = middle(
        tokens, mixed, cotangent, gains, weights_two
    )
    edge_grad, edge_sum, away = edge_back(marks, qkv, mixed_grad, logs, cosine, sine, lower, upper)
    from_upper = passed_along(away[0], -1)
    from_lower = passed_along(away[1], 1)
    me = lax.axis_index("tok")
    if staged():
        halves = (1 - (me & 1), me & 1)
    else:
        halves = (jnp.int32(1), jnp.int32(0))

    def order(half):
        if staged():
            slots = chip_slots(me >> 1, half)
        else:
            slots = jnp.arange(D // CHIP_ROWS, dtype=jnp.int32)
        return jnp.concatenate([jnp.reshape(half, (1,)).astype(jnp.int32), slots])

    def ff_grad(half, after):
        return ff_weight_grad(order(half), normed_two, cotangent, mixed, both, hidden, low, after)

    def inner(half, after):
        return inner_back(
            half,
            marks,
            qkv,
            mixed_grad,
            logs,
            cosine,
            sine,
            edge_grad,
            edge_sum,
            from_lower,
            from_upper,
            after,
        )

    def finish(first, second):
        return input_grad(halves[0], tokens, gains, weights_one, first, second, grad)

    send, keep = halves
    ff_send = ff_grad(send, [away])
    ff_keep = ff_grad(keep, [ff_send, from_lower, from_upper])
    if staged():
        near, far = core_sum(ff_keep, exchange(ff_send, CORE))
        first = inner(send, [far])
        near, far = far_sum(near, stage_after(exchange(far, FAR), first))
        qkv_send = qkv_weight_grad(order(send), normed, first, [far])
        second = inner(keep, [qkv_send])
        parts = near_sum(near, stage_after(exchange(far, NEAR), second))
        qkv_keep = qkv_weight_grad(order(keep), normed, second, parts)
        near, far = core_sum(qkv_keep, exchange(qkv_send, CORE))
        grad_in = finish(first, stage_after(second, far))
        sum_ff = deep_sum(parts, far)
        near, far = far_sum(near, stage_after(exchange(far, FAR), grad_in))
        sum_qkv = deep_sum(near_sum(near, exchange(far, NEAR)), far)
    else:
        first, second = inner(send, []), inner(keep, [])
        grad_in = finish(first, second)
        sum_ff = summed(ff_keep, ff_send)
        sum_qkv = summed(
            qkv_weight_grad(order(keep), normed, second), qkv_weight_grad(order(send), normed, first)
        )
    sum_qkv = by_part(sum_qkv)
    sent_in = sum_ff[:, : 2 * FF]
    sent_down = sum_ff[:, 2 * FF : 3 * FF].T
    sent_attn = sum_ff[:, 3 * FF : 3 * FF + D]

    def gain_grad(summed, weight, gain):
        return jnp.sum(summed * weight.astype(F32), axis=1) / gain.astype(F32)

    return (
        result,
        grad_in,
        gain_grad(sum_qkv, qkv_weight, first_gain),
        sum_qkv,
        sent_attn,
        gain_grad(sent_in, feed_in_weight, second_gain),
        sent_in,
        sent_down,
    )


def solution(mesh):
    in_specs = (
        P("tok", None),
        P(),
        P("tok"),
        P("tok", None),
        P("tok", None),
        P("tok"),
        P("tok", None),
        P(None, "tok"),
        P("tok", None),
    )
    out_specs = (
        P("tok", None),
        P("tok", None),
        P("tok"),
        P("tok", None),
        P("tok", None),
        P("tok"),
        P("tok", None),
        P(None, "tok"),
    )
    return jax.shard_map(
        on_device, mesh=mesh, in_specs=in_specs, out_specs=out_specs, check_vma=False
    )
```

```python
from functools import partial

import jax
import jax.numpy as jnp
from jax import lax
from jax.experimental import pallas as pl
from jax.experimental.pallas import tpu as pltpu
from jax.sharding import PartitionSpec as P

D = 768
FF = 1152
HEADS = 12
HEAD_DIM = 64
HALF = 64
PAIRS = HEADS // 2
BLOCK = 128
SPAN = BLOCK + 2 * HALF
LANES = 128
QKV_HALF = 3 * D // 2
GROUP = D // 2
GROUP_PAIRS = PAIRS // 2
FF_HALF = 1792
FF_LEFT = 2 * FF - FF_HALF
MIXED_HALF = QKV_HALF + GROUP
MIB = 1024 * 1024
BF = jnp.bfloat16
F32 = jnp.float32


def dot(left, right, left_dim=1, right_dim=0):
    return lax.dot_general(
        left, right, (((left_dim,), (right_dim,)), ((), ())), preferred_element_type=F32
    )


def params(mib):
    return pltpu.CompilerParams(vmem_limit_bytes=mib * MIB)


def whole(shape):
    return pl.BlockSpec(shape, lambda *_: (0,) * len(shape))


def rows(shape):
    return pl.BlockSpec(shape, lambda i: (i,) + (0,) * (len(shape) - 1))


SMALL = pl.CostEstimate(flops=4000000000, bytes_accessed=1000, transcendentals=0)
SMEM = pl.BlockSpec(memory_space=pltpu.SMEM)
ANY = pl.BlockSpec(memory_space=pl.ANY)
VMEM = pl.BlockSpec(memory_space=pltpu.VMEM)
HBM = pl.BlockSpec(memory_space=pltpu.HBM)


def lane_ids(shape):
    return lax.broadcasted_iota(jnp.int32, shape, len(shape) - 1)


def swap_halves(values):
    low = (lane_ids(values.shape) & (HEAD_DIM - 1)) < HEAD_DIM // 2
    return jnp.where(
        low, pltpu.roll(values, LANES - HEAD_DIM // 2, 1), pltpu.roll(values, HEAD_DIM // 2, 1)
    )


def normalized(values):
    centered = values - jnp.mean(values, axis=-1, keepdims=True)
    scale = lax.rsqrt(jnp.mean(centered * centered, axis=-1, keepdims=True) + 1e-05)
    return centered * scale, scale


def norm_back(grad, unit, scale, gains):
    grad_unit = grad * gains
    return scale * (
        grad_unit
        - jnp.mean(grad_unit, axis=-1, keepdims=True)
        - unit * jnp.mean(grad_unit * unit, axis=-1, keepdims=True)
    )


CHIP_ROWS = 48


class Weights:
    def __init__(self, arrays, places=None):
        self.arrays = arrays
        self.places = places

    def operands(self):
        if self.places is None:
            return list(self.arrays)
        return [self.places, *self.arrays]

    def specs(self):
        if self.places is None:
            return [ANY]
        return [SMEM, VMEM, VMEM, VMEM, VMEM]

    def scratch(self):
        width = self.arrays[0].shape[-1]
        return [pltpu.VMEM((2, D, width), BF), pltpu.SemaphoreType.DMA((1,))]


def load_weights(refs, out_ref, sems):
    if len(refs) == 1:
        copy = pltpu.make_async_copy(refs[0], out_ref, sems.at[0])
        copy.start()
        copy.wait()
        return
    places_ref = refs[0]
    core = places_ref[32]
    for index, source in enumerate(refs[1:]):
        half = core if index < 2 else 1 - core
        for slot in range(8):
            place = pl.multiple_of(places_ref[index * 8 + slot] * CHIP_ROWS, 16)
            out_ref[half, pl.ds(place, CHIP_ROWS), :] = source[
                slot * CHIP_ROWS : (slot + 1) * CHIP_ROWS, :
            ]


def qkv_kernel(count, x_ref, cos_ref, sin_ref, *refs):
    weight_refs = refs[:count]
    normed_ref, qkv_ref, gains_ref, w_ref, sems = refs[count:]

    @pl.when(pl.program_id(0) == 0)
    def _():
        load_weights(weight_refs, w_ref, sems)
        for half in range(2):
            turned = w_ref[half, :, QKV_HALF:].T.astype(F32)
            gains_ref[half * 8 : half * 8 + 8, :] = turned[:8]

    unit, _ = normalized(x_ref[...].astype(F32))
    normed = (unit * gains_ref[0:1, :]).astype(BF)
    normed_ref[...] = normed
    cosine = cos_ref[...]
    sine = sin_ref[...]
    for half in range(2):
        merged = dot(normed, w_ref[half, :, :QKV_HALF])
        for tile in range(QKV_HALF // LANES):
            lanes = slice(tile * LANES, (tile + 1) * LANES)
            part = merged[:, lanes]
            if tile * LANES < 2 * GROUP:
                part = part * cosine + swap_halves(part) * sine
            qkv_ref[half, :, lanes] = part.astype(BF)


def project_qkv(tokens, weights, cosine, sine):
    count = tokens.shape[0]
    size = min(256, count)
    operands = weights.operands()
    return pl.pallas_call(
        partial(qkv_kernel, len(operands)),
        grid=(count // size,),
        in_specs=[rows((size, D)), rows((size, LANES)), rows((size, LANES)), *weights.specs()],
        out_specs=[
            rows((size, D)),
            pl.BlockSpec((2, size, QKV_HALF), lambda i: (0, i, 0)),
            whole((16, D)),
        ],
        out_shape=[
            jax.ShapeDtypeStruct((count, D), BF),
            jax.ShapeDtypeStruct((2, count, QKV_HALF), BF),
            jax.ShapeDtypeStruct((16, D), F32),
        ],
        scratch_shapes=weights.scratch(),
        compiler_params=params(12),
        cost_estimate=SMALL,
        name="qkv",
    )(tokens, cosine, sine, *operands)


def window_bias(marks_ref, block):
    shape = (SPAN, 2 * BLOCK)
    first = marks_ref[3] + block * BLOCK
    key = lax.broadcasted_iota(jnp.int32, shape, 0)
    query = lax.broadcasted_iota(jnp.int32, (1, 2 * BLOCK), 1) & (BLOCK - 1)
    place = first + query
    lowest = query
    highest = query + 2 * HALF
    for index in range(3):
        mark = marks_ref[index]
        edge = mark - first + HALF
        past = place >= mark
        lowest = jnp.where(past, jnp.maximum(lowest, edge), lowest)
        highest = jnp.where(past, highest, jnp.minimum(highest, edge - 1))
    return jnp.where((key >= lowest) & (key <= highest), 0.0, -1e30).astype(F32)


def stacked(pair):
    low = lane_ids(pair.shape) < HEAD_DIM
    zero = jnp.zeros_like(pair)
    return jnp.concatenate([jnp.where(low, pair, zero), jnp.where(low, zero, pair)], axis=0)


def unstacked(both):
    low = lane_ids((BLOCK, LANES)) < HEAD_DIM
    return jnp.where(low, both[:BLOCK], both[BLOCK:])


def span_of(qkv_ref, lower_ref, upper_ref, half, block, part, sub):
    count = qkv_ref.shape[1]
    first = block * BLOCK - HALF
    lanes = slice(part * GROUP + sub * LANES, part * GROUP + (sub + 1) * LANES)
    halo_lanes = slice((part - 1) * GROUP + sub * LANES, (part - 1) * GROUP + (sub + 1) * LANES)
    own = qkv_ref[half, max(first, 0) : min(first + SPAN, count), lanes]
    if first < 0:
        own = jnp.concatenate([lower_ref[half, :, halo_lanes], own], axis=0)
    if first + SPAN > count:
        own = jnp.concatenate([own, upper_ref[half, :, halo_lanes]], axis=0)
    return own


def many_attend(operands):
    scores = [dot(keys, query, 1, 1) + bias for query, keys, _, bias in operands]
    peaks = [jnp.max(score, axis=0, keepdims=True) for score in scores]
    expos = [jnp.exp(score - peak) for score, peak in zip(scores, peaks)]
    totals = [jnp.sum(expo, axis=0, keepdims=True) for expo in expos]
    weights = [(expo * (1.0 / total)).astype(BF) for expo, total in zip(expos, totals)]
    mixed = [unstacked(dot(weight, item[2], 0, 0)) for weight, item in zip(weights, operands)]
    return [(mix, peak + jnp.log(total)) for mix, peak, total in zip(mixed, peaks, totals)]


def attend_kernel(marks_ref, qkv_ref, lower_ref, upper_ref, out_ref, log_ref):
    for block in range(qkv_ref.shape[1] // BLOCK):
        bias = window_bias(marks_ref, block)
        mine = slice(block * BLOCK, (block + 1) * BLOCK)
        for first in range(0, PAIRS, PAIRS_TOGETHER):
            pairs = range(first, first + PAIRS_TOGETHER)
            items = []
            for pair in pairs:
                half, sub = divmod(pair, GROUP_PAIRS)
                where = (qkv_ref, lower_ref, upper_ref, half, block)
                items.append(
                    (
                        stacked(qkv_ref[half, mine, sub * LANES : (sub + 1) * LANES] * BF(0.125)),
                        span_of(*where, 1, sub),
                        span_of(*where, 2, sub),
                        bias,
                    )
                )
            for pair, (mix, logs) in zip(pairs, many_attend(items)):
                half, sub = divmod(pair, GROUP_PAIRS)
                out_ref[mine, pair * LANES : (pair + 1) * LANES] = mix.astype(BF)
                log_ref[block, half, sub : sub + 1, :] = logs


def attend(marks, qkv, lower, upper):
    count = qkv.shape[1]
    blocks = count // BLOCK
    return pl.pallas_call(
        attend_kernel,
        in_specs=[SMEM, VMEM, VMEM, VMEM],
        out_specs=[VMEM, VMEM],
        out_shape=[
            jax.ShapeDtypeStruct((count, D), BF),
            jax.ShapeDtypeStruct((blocks, 2, 8, 2 * BLOCK), F32),
        ],
        compiler_params=params(8),
        cost_estimate=SMALL,
        name="attend",
    )(marks, qkv, lower, upper)


PAIRS_TOGETHER = 1
FF_PARTS = tuple((first, min(256, FF - first)) for first in range(0, FF, 256))


def dense_kernel(
    x_ref, mixed_ref, cot_ref, gains_ref, w_ref, residual_ref, normed_ref, both_ref, hidden_ref
):
    residual = x_ref[...].astype(F32) + dot(mixed_ref[...], w_ref[:, 3 * FF :])
    residual_ref[...] = residual
    unit, _ = normalized(residual)
    normed = (unit * gains_ref[8:9, :]).astype(BF)
    normed_ref[...] = normed
    cot = cot_ref[...]
    for first, size in FF_PARTS:
        gate_cols = slice(first, first + size)
        up_cols = slice(FF + first, FF + first + size)
        down_cols = slice(2 * FF + first, 2 * FF + first + size)
        gate = dot(normed, w_ref[:, gate_cols])
        up = dot(normed, w_ref[:, up_cols])
        grad_hidden = dot(cot, w_ref[:, down_cols])
        share = 0.5 + 0.5 * lax.erf(gate * 0.7071067811865476)
        active = gate * share
        slope = share + gate * (jnp.exp(-0.5 * gate * gate) * 0.3989422804014327)
        hidden_ref[:, gate_cols] = (active * up).astype(BF)
        both_ref[:, gate_cols] = (grad_hidden * up * slope).astype(BF)
        both_ref[:, up_cols] = (grad_hidden * active).astype(BF)


def dense(tokens, mixed, cotangent, gains, weights):
    count = tokens.shape[0]
    size = min(512, count)
    wide = [(D, F32), (D, BF), (2 * FF, BF), (FF, BF)]
    return pl.pallas_call(
        dense_kernel,
        grid=(count // size,),
        in_specs=[
            rows((size, D)),
            rows((size, D)),
            rows((size, D)),
            whole((16, D)),
            whole(weights.shape),
        ],
        out_specs=[rows((size, width)) for width, _ in wide],
        out_shape=[jax.ShapeDtypeStruct((count, width), kind) for width, kind in wide],
        compiler_params=params(20),
        cost_estimate=SMALL,
        name="dense",
    )(tokens, mixed, cotangent, gains, weights)


def dense_back_kernel(residual_ref, cot_ref, both_ref, gains_ref, w_ref, *rest):
    low_ref, mixed_grad_ref, grad_ref = rest[-3:]
    unit, scale = normalized(residual_ref[...])
    grad_normed = dot(both_ref[...], w_ref[:, : 2 * FF], 1, 1)
    grad = cot_ref[...].astype(F32) + norm_back(grad_normed, unit, scale, gains_ref[8:9, :])
    grad_ref[...] = grad
    low = grad.astype(BF)
    low_ref[...] = low
    mixed_grad_ref[...] = dot(low, w_ref[:, 3 * FF :], 1, 1).astype(BF)


def dense_back(residual, cotangent, both, gains, weights, after):
    count = residual.shape[0]
    size = min(512, count)
    wide = [(D, BF), (D, BF), (D, F32)]
    return pl.pallas_call(
        dense_back_kernel,
        grid=(count // size,),
        in_specs=[
            rows((size, D)),
            rows((size, D)),
            rows((size, 2 * FF)),
            whole((16, D)),
            whole(weights.shape),
            *[ANY for _ in after],
        ],
        out_specs=[rows((size, width)) for width, _ in wide],
        out_shape=[jax.ShapeDtypeStruct((count, width), kind) for width, kind in wide],
        compiler_params=params(20),
        cost_estimate=SMALL,
        name="dense_back",
    )(residual, cotangent, both, gains, weights, *after)


def result_kernel(residual_ref, hidden_ref, w_ref, *rest):
    product = dot(hidden_ref[...], w_ref[:, 2 * FF : 3 * FF], 1, 1)
    rest[-1][...] = (residual_ref[...] + product).astype(BF)


def result_of(residual, hidden, weights, after):
    count = residual.shape[0]
    size = min(512, count)
    return pl.pallas_call(
        result_kernel,
        grid=(count // size,),
        in_specs=[rows((size, D)), rows((size, FF)), whole(weights.shape), *[ANY for _ in after]],
        out_specs=rows((size, D)),
        out_shape=jax.ShapeDtypeStruct((count, D), BF),
        compiler_params=params(16),
        cost_estimate=SMALL,
        name="result",
    )(residual, hidden, weights, *after)


def pair_back(query, keys, values, out_grad, logs, bias):
    scores = dot(keys, query, 1, 1) + bias
    weights = jnp.exp(scores - logs)
    weight_grad = dot(values, out_grad, 1, 1)
    score_grad = weights * (weight_grad - jnp.sum(weights * weight_grad, axis=0, keepdims=True))
    score_grad = score_grad.astype(BF)
    key_grad = dot(score_grad, query)
    value_grad = dot(weights.astype(BF), out_grad)
    query_grad = unstacked(dot(score_grad, keys, 0, 0)) * 0.125
    return query_grad, key_grad, value_grad


def many_back(operands):
    scores = [dot(keys, query, 1, 1) for query, keys, _, _, _, _ in operands]
    weight_grads = [dot(values, out_grad, 1, 1) for _, _, values, out_grad, _, _ in operands]
    weights = [jnp.exp(score + item[5] - item[4]) for score, item in zip(scores, operands)]
    value_grads = [dot(weight.astype(BF), item[3]) for weight, item in zip(weights, operands)]
    score_grads = [
        (weight * (grad - jnp.sum(weight * grad, axis=0, keepdims=True))).astype(BF)
        for weight, grad in zip(weights, weight_grads)
    ]
    key_grads = [dot(grad, item[0]) for grad, item in zip(score_grads, operands)]
    query_grads = [
        unstacked(dot(grad, item[1], 0, 0)) * 0.125 for grad, item in zip(score_grads, operands)
    ]
    return list(zip(query_grads, key_grads, value_grads))


def turned_back(values, cosine, sine):
    return values * cosine - swap_halves(values) * sine


def edge_back_kernel(
    marks_ref,
    mixed_grad_ref,
    log_ref,
    cos_ref,
    sin_ref,
    qkv_ref,
    lower_ref,
    upper_ref,
    grad_ref,
    sum_ref,
    away_ref,
):
    count = qkv_ref.shape[1]
    for side, block in enumerate((0, count // BLOCK - 1)):
        bias = window_bias(marks_ref, block)
        mine = slice(block * BLOCK, (block + 1) * BLOCK)
        sent = slice(0, HALF) if side == 0 else slice(SPAN - HALF, SPAN)
        for half in range(2):
            items = []
            for sub in range(GROUP_PAIRS):
                pair = half * GROUP_PAIRS + sub
                where = (qkv_ref, lower_ref, upper_ref, half, block)
                items.append(
                    (
                        stacked(qkv_ref[half, mine, sub * LANES : (sub + 1) * LANES] * BF(0.125)),
                        span_of(*where, 1, sub),
                        span_of(*where, 2, sub),
                        stacked(mixed_grad_ref[mine, pair * LANES : (pair + 1) * LANES]),
                        log_ref[block, half, sub : sub + 1, :],
                        bias,
                    )
                )
            for sub, (query_grad, key_grad, value_grad) in enumerate(many_back(items)):
                lanes = slice(sub * LANES, (sub + 1) * LANES)
                value_lanes = slice(GROUP + sub * LANES, GROUP + (sub + 1) * LANES)
                grad_ref[half, side, :, lanes] = turned_back(
                    query_grad, cos_ref[mine, :], sin_ref[mine, :]
                ).astype(BF)
                sum_ref[half, side, :, lanes] = key_grad
                sum_ref[half, side, :, value_lanes] = value_grad
                away_ref[side, half, :, lanes] = key_grad[sent].astype(BF)
                away_ref[side, half, :, value_lanes] = value_grad[sent].astype(BF)


def edge_back(marks, qkv, mixed_grad, logs, cosine, sine, lower, upper):
    return pl.pallas_call(
        edge_back_kernel,
        in_specs=[SMEM, *[VMEM] * 7],
        out_specs=[VMEM, VMEM, VMEM],
        out_shape=[
            jax.ShapeDtypeStruct((2, 2, BLOCK, GROUP), BF),
            jax.ShapeDtypeStruct((2, 2, SPAN, 2 * GROUP), F32),
            jax.ShapeDtypeStruct((2, 2, HALF, 2 * GROUP), BF),
        ],
        compiler_params=params(8),
        cost_estimate=SMALL,
        name="edge_back",
    )(marks, mixed_grad, logs, cosine, sine, qkv, lower, upper)


TOGETHER = 1


def inner_back_kernel(
    group_ref,
    marks_ref,
    mixed_grad_ref,
    log_ref,
    cos_ref,
    sin_ref,
    edge_grad_ref,
    edge_sum_ref,
    from_lower_ref,
    from_upper_ref,
    qkv_ref,
    *rest,
):
    grad_ref, sum_ref = rest[-2:]
    count = qkv_ref.shape[1]
    inner = count // BLOCK - 2
    sum_ref[0 : SPAN - HALF, :] = edge_sum_ref[0, 0, HALF:, :]
    sum_ref[0:HALF, :] += from_lower_ref[0].astype(F32)
    grad_ref[0:BLOCK, 0:GROUP] = edge_grad_ref[0, 0]
    grad_ref[count - BLOCK :, 0:GROUP] = edge_grad_ref[0, 1]

    def finish(place):
        own_cosine = cos_ref[place, :]
        own_sine = sin_ref[place, :]
        for sub in range(GROUP_PAIRS):
            lanes = slice(sub * LANES, (sub + 1) * LANES)
            key_lanes = slice(GROUP + sub * LANES, GROUP + (sub + 1) * LANES)
            grad_ref[place, key_lanes] = turned_back(
                sum_ref[place, lanes], own_cosine, own_sine
            ).astype(BF)
        grad_ref[place, 2 * GROUP :] = sum_ref[place, GROUP:].astype(BF)

    for first in range(1, inner + 1, TOGETHER):
        blocks = range(first, min(first + TOGETHER, inner + 1))
        places = []
        items = []
        for block in blocks:
            bias = window_bias(marks_ref, block)
            start = block * BLOCK - HALF
            window = slice(start, start + SPAN)
            mine = slice(block * BLOCK, (block + 1) * BLOCK)
            for sub in range(GROUP_PAIRS):
                lanes = slice(sub * LANES, (sub + 1) * LANES)
                places.append((mine, start, sub))
                items.append(
                    (
                        stacked(qkv_ref[0, mine, lanes] * BF(0.125)),
                        qkv_ref[0, window, GROUP + sub * LANES : GROUP + (sub + 1) * LANES],
                        qkv_ref[0, window, 2 * GROUP + sub * LANES : 2 * GROUP + (sub + 1) * LANES],
                        stacked(mixed_grad_ref[mine, lanes]),
                        log_ref[block, 0, sub : sub + 1, :],
                        bias,
                    )
                )
        for (mine, start, sub), (query_grad, key_grad, value_grad) in zip(places, many_back(items)):
            lanes = slice(sub * LANES, (sub + 1) * LANES)
            value_lanes = slice(GROUP + sub * LANES, GROUP + (sub + 1) * LANES)
            older = slice(start, start + BLOCK)
            newer = slice(start + BLOCK, start + SPAN)
            sum_ref[older, lanes] += key_grad[:BLOCK]
            sum_ref[newer, lanes] = key_grad[BLOCK:]
            sum_ref[older, value_lanes] += value_grad[:BLOCK]
            sum_ref[newer, value_lanes] = value_grad[BLOCK:]
            grad_ref[mine, lanes] = turned_back(query_grad, cos_ref[mine, :], sin_ref[mine, :]).astype(BF)
        finish(slice(0 if first == 1 else blocks[0] * BLOCK - HALF, (blocks[-1] + 1) * BLOCK - HALF))

    tail = SPAN - HALF
    sum_ref[count - tail : count - HALF, :] += edge_sum_ref[0, 1, 0:BLOCK, :]
    sum_ref[count - HALF :, :] = edge_sum_ref[0, 1, BLOCK:tail, :] + from_upper_ref[0].astype(F32)
    finish(slice(count - tail, count))


def inner_back(group, marks, qkv, mixed_grad, logs, cosine, sine, edge_grad, edge_sum, from_lower, from_upper, after):
    count = qkv.shape[1]
    return pl.pallas_call(
        inner_back_kernel,
        grid_spec=pltpu.PrefetchScalarGridSpec(
            num_scalar_prefetch=1,
            grid=(1,),
            in_specs=[
                SMEM,
                pl.BlockSpec((count, GROUP), lambda i, g: (0, g[0])),
                pl.BlockSpec((count // BLOCK, 1, 8, 2 * BLOCK), lambda i, g: (0, g[0], 0, 0)),
                pl.BlockSpec((count, LANES), lambda i, g: (0, 0)),
                pl.BlockSpec((count, LANES), lambda i, g: (0, 0)),
                pl.BlockSpec((1, 2, BLOCK, GROUP), lambda i, g: (g[0], 0, 0, 0)),
                pl.BlockSpec((1, 2, SPAN, 2 * GROUP), lambda i, g: (g[0], 0, 0, 0)),
                pl.BlockSpec((1, HALF, 2 * GROUP), lambda i, g: (g[0], 0, 0)),
                pl.BlockSpec((1, HALF, 2 * GROUP), lambda i, g: (g[0], 0, 0)),
                pl.BlockSpec((1, count, QKV_HALF), lambda i, g: (g[0], 0, 0)),
                *[ANY for _ in after],
            ],
            out_specs=pl.BlockSpec((count, QKV_HALF), lambda i, g: (0, 0)),
            scratch_shapes=[
                pltpu.VMEM((count, 2 * GROUP), F32),
            ],
        ),
        out_shape=jax.ShapeDtypeStruct((count, QKV_HALF), BF),
        compiler_params=params(8),
        cost_estimate=SMALL,
        name="inner_back",
    )(
        jnp.reshape(group, (1,)).astype(jnp.int32),
        marks,
        mixed_grad,
        logs,
        cosine,
        sine,
        edge_grad,
        edge_sum,
        from_lower,
        from_upper,
        qkv,
        *after,
    )


def input_grad_kernel(count, order_ref, x_ref, gains_ref, first_ref, second_ref, grad_ref, *refs):
    weight_refs = refs[:count]
    out_ref, w_ref, sems = refs[count:]

    @pl.when(pl.program_id(0) == 0)
    def _():
        load_weights(weight_refs, w_ref, sems)

    unit, scale = normalized(x_ref[...].astype(F32))
    half = order_ref[0]
    grad_normed = dot(first_ref[...], w_ref[half, :, :QKV_HALF], 1, 1) + dot(
        second_ref[...], w_ref[1 - half, :, :QKV_HALF], 1, 1
    )
    out_ref[...] = grad_ref[...] + norm_back(grad_normed, unit, scale, gains_ref[0:1, :])


def input_grad(half, tokens, gains, weights, first, second, grad):
    count = tokens.shape[0]
    size = min(256, count)
    operands = weights.operands()
    return pl.pallas_call(
        partial(input_grad_kernel, len(operands)),
        grid=(count // size,),
        in_specs=[
            SMEM,
            rows((size, D)),
            whole((16, D)),
            rows((size, QKV_HALF)),
            rows((size, QKV_HALF)),
            rows((size, D)),
            *weights.specs(),
        ],
        out_specs=rows((size, D)),
        out_shape=jax.ShapeDtypeStruct((count, D), F32),
        scratch_shapes=weights.scratch(),
        compiler_params=params(12),
        cost_estimate=SMALL,
        name="input_grad",
    )(jnp.reshape(half, (1,)).astype(jnp.int32), tokens, gains, first, second, grad, *operands)


TILE = 256


def store_slots(slots_ref, out_ref, product):
    step = CHIP_ROWS
    for index in range(D // step):
        place = pl.multiple_of(slots_ref[1 + index] * step, 16)
        out_ref[pl.ds(place, step), :] = product[index * step : (index + 1) * step].astype(BF)


def weight_products(slots_ref, out_ref, turned, grad_ref, first, size):
    for tile in range(0, size, TILE):
        width = min(TILE, size - tile)
        product = dot(turned, grad_ref[:, tile : tile + width])
        for index in range(D // CHIP_ROWS):
            place = pl.multiple_of(slots_ref[1 + index] * CHIP_ROWS, 16)
            out_ref[pl.ds(place, CHIP_ROWS), first + tile : first + tile + width] = product[
                index * CHIP_ROWS : (index + 1) * CHIP_ROWS
            ].astype(BF)


def mixed_weight_kernel(slots_ref, normed_ref, grad_ref, mixed_ref, low_ref, *rest):
    out_ref = rest[-1]
    weight_products(slots_ref, out_ref, normed_ref[...].T, grad_ref, 0, QKV_HALF)
    lanes = pl.ds(pl.multiple_of(slots_ref[0] * GROUP, LANES), GROUP)
    weight_products(slots_ref, out_ref, mixed_ref[...].T, low_ref.at[:, lanes], QKV_HALF, GROUP)


def mixed_weight_grad(slots, normed, dqkv, mixed, low, after=()):
    count = normed.shape[0]
    return pl.pallas_call(
        mixed_weight_kernel,
        in_specs=[SMEM, *[VMEM] * 4, *[ANY for _ in after]],
        out_specs=VMEM,
        out_shape=jax.ShapeDtypeStruct((D, MIXED_HALF), BF),
        compiler_params=params(8),
        cost_estimate=SMALL,
        name="mixed_weight_grad",
    )(slots, normed, dqkv, mixed, low, *after)


def ff_weight_kernel(slots_ref, normed_ref, cot_ref, both_ref, hidden_ref, *rest):
    out_ref = rest[-1]

    @pl.when(slots_ref[0] == 0)
    def _():
        left = both_ref.at[:, 0:FF_HALF]
        weight_products(slots_ref, out_ref, normed_ref[...].T, left, 0, FF_HALF)

    @pl.when(slots_ref[0] == 1)
    def _():
        left = both_ref.at[:, FF_HALF : 2 * FF]
        weight_products(slots_ref, out_ref, normed_ref[...].T, left, 0, FF_LEFT)
        weight_products(slots_ref, out_ref, cot_ref[...].T, hidden_ref, FF_LEFT, FF)
        out_ref[:, FF_LEFT + FF :] = jnp.zeros((D, FF_HALF - FF_LEFT - FF), BF)


def ff_weight_grad(slots, normed, cot, both, hidden, after):
    count = normed.shape[0]
    return pl.pallas_call(
        ff_weight_kernel,
        in_specs=[SMEM, *[VMEM] * 4, *[ANY for _ in after]],
        out_specs=VMEM,
        out_shape=jax.ShapeDtypeStruct((D, FF_HALF), BF),
        compiler_params=params(8),
        cost_estimate=SMALL,
        name="ff_weight_grad",
    )(slots, normed, cot, both, hidden, *after)


def join_kernel(*refs):
    out_ref = refs[-1]
    first = 0
    for ref in refs[:-1]:
        out_ref[first : first + ref.shape[0], :] = ref[...]
        first += ref.shape[0]


def join(*parts):
    count = sum(part.shape[0] for part in parts)
    width = parts[0].shape[1]
    return pl.pallas_call(
        join_kernel,
        in_specs=[VMEM for _ in parts],
        out_specs=VMEM,
        out_shape=jax.ShapeDtypeStruct((count, width), parts[0].dtype),
        compiler_params=params(8),
        cost_estimate=SMALL,
        name="join",
    )(*parts)


def doc_marks(doc_lengths, row_count):
    me = lax.axis_index("tok")
    ends = jnp.cumsum(doc_lengths).astype(jnp.int32)
    before = jnp.where(me > 0, ends[jnp.maximum(me - 1, 0)], 0)
    return jnp.stack([before, ends[me], ends[me + 1], me * row_count]).astype(jnp.int32)


def rotary_tables(marks, row_count):
    place = marks[3] + jnp.arange(row_count, dtype=jnp.int32)
    offset = place - jnp.where(place >= marks[1], marks[1], marks[0])
    frequency = 10000.0 ** (-jnp.arange(0, HEAD_DIM, 2, dtype=F32) / HEAD_DIM)
    angles = offset.astype(F32)[:, None] * frequency[None, :]
    cosine = jnp.cos(angles)
    sine = jnp.sin(angles)
    return (
        jnp.concatenate([cosine] * 4, axis=1),
        jnp.concatenate([-sine, sine, -sine, sine], axis=1),
    )


def passed_along(value, steps):
    count = lax.axis_size("tok")
    first, last = (max(0, -steps), min(count, count - steps))
    return lax.ppermute(value, "tok", [(at, at + steps) for at in range(first, last)])


STAGED_DEVICES = 32


def staged():
    return lax.axis_size("tok") == STAGED_DEVICES


def exchange(value, by_core):
    pairs = [(at, at ^ by_core[at & 1]) for at in range(lax.axis_size("tok"))]
    return lax.ppermute(value, "tok", pairs)


CORE = (1, 1)
DEEP = tuple((step << 3, step << 3) for step in range(4))
NEAR = (2, 4)
FAR = (4, 2)


def slot_codes(core):
    slot = jnp.arange(16, dtype=jnp.int32)
    depth, near, far = (slot & 3, (slot >> 2) & 1, slot >> 3)
    return (depth << 2) | jnp.where(core == 0, (far << 1) | near, (near << 1) | far)


def chip_slots(chip, core):
    code = jnp.arange(16, dtype=jnp.int32) ^ chip
    depth, second, first = (code >> 2, (code >> 1) & 1, code & 1)
    return depth | jnp.where(core == 0, (second << 3) | (first << 2), (first << 3) | (second << 2))


def stage_after(value, *others):
    return lax.optimization_barrier((value, *others))[0]


def core_pieces(shard):
    core = lax.axis_index("tok") & 1
    half = shard.shape[1] // 2
    keep = jnp.where(core == 0, shard[:, :half], shard[:, half:])
    send = jnp.where(core == 0, shard[:, half:], shard[:, :half])
    came = exchange(send, CORE)
    return jnp.concatenate(
        [jnp.where(core == 0, keep, came), jnp.where(core == 0, came, keep)], axis=0
    )


def final_gather(held, far):
    me = lax.axis_index("tok")
    core = me & 1
    chip = me >> 1
    places = jnp.concatenate(
        [slot_codes(core) ^ chip, slot_codes(1 - core) ^ chip, jnp.full((1,), core, jnp.int32)]
    )
    return Weights([held, far, exchange(held, CORE), exchange(far, CORE)], places)


def whole_weights(shard):
    full = lax.all_gather(shard, "tok", axis=0, tiled=True)
    half = full.shape[1] // 2
    return Weights([jnp.stack([full[:, :half], full[:, half:]])])


def added(left, right):
    return (left.astype(F32) + right.astype(F32)).astype(BF)


def core_sum(keep, came):
    return added(keep[:384], came[:384]), added(keep[384:], came[384:])


def far_sum(near, came):
    return added(near[:192], came[:192]), added(near[192:], came[192:])


def near_sum(near, came):
    return [
        added(near[first : first + CHIP_ROWS], came[first : first + CHIP_ROWS])
        for first in range(0, 192, CHIP_ROWS)
    ]


def deep_sum(parts, after):
    core = lax.axis_index("tok") & 1
    total = parts[0].astype(F32)
    for step in (1, 2, 3):
        total = total + stage_after(exchange(parts[step], DEEP[step]), after).astype(F32)
    share = CHIP_ROWS // 2
    lower, upper = (total[:share], total[share:])
    own = jnp.where(core == 0, lower, upper)
    came = exchange(jnp.where(core == 0, upper, lower), CORE)
    return jnp.concatenate(
        [jnp.where(core == 0, own, came), jnp.where(core == 0, came, own)], axis=1
    )


def summed(keep, send):
    full = jnp.concatenate([keep, send], axis=1)
    return lax.psum_scatter(full.astype(F32), "tok", scatter_dimension=0, tiled=True)


def by_part(groups):
    return jnp.concatenate(
        [
            groups[:, half * MIXED_HALF + part * GROUP : half * MIXED_HALF + (part + 1) * GROUP]
            for part in range(3)
            for half in range(2)
        ],
        axis=1,
    )


def on_device(
    tokens,
    doc_lengths,
    first_gain,
    qkv_weight,
    attn_weight,
    second_gain,
    feed_in_weight,
    feed_out_weight,
    cotangent,
):
    row_count = tokens.shape[0]
    share = first_gain.shape[0]

    def spread(gain):
        return jnp.broadcast_to(gain[:, None], (share, LANES))

    def group_of(half):
        return [
            qkv_weight[:, part * D + half * GROUP : part * D + (half + 1) * GROUP]
            for part in range(3)
        ]

    shard_one = jnp.concatenate(
        [*group_of(0), spread(first_gain), *group_of(1), spread(second_gain)], axis=1
    )
    shard_two = jnp.concatenate([feed_in_weight, feed_out_weight.T, attn_weight], axis=1)
    weights_two = lax.all_gather(shard_two, "tok", axis=0, tiled=True)
    if staged():
        piece = core_pieces(shard_one)
        marks = doc_marks(stage_after(doc_lengths, piece), row_count)
        cosine, sine = rotary_tables(marks, row_count)
        came = [exchange(piece, DEEP[step]) for step in (1, 2, 3)]
        came = lax.optimization_barrier((*came, cosine, sine))[:3]
        one = join(piece, *came)
        one = join(one, exchange(one, NEAR))
        weights_one = final_gather(one, exchange(one, FAR))
    else:
        marks = doc_marks(doc_lengths, row_count)
        cosine, sine = rotary_tables(marks, row_count)
        weights_one = whole_weights(shard_one)
    normed, qkv, gains = project_qkv(tokens, weights_one, cosine, sine)
    lower = passed_along(qkv[:, row_count - HALF :, GROUP:], 1)
    upper = passed_along(qkv[:, :HALF, GROUP:], -1)
    mixed, logs = attend(marks, qkv, lower, upper)
    residual, normed_two, both, hidden = dense(tokens, mixed, cotangent, gains, weights_two)
    me = lax.axis_index("tok")
    if staged():
        halves = (1 - (me & 1), me & 1)
    else:
        halves = (jnp.int32(1), jnp.int32(0))

    def order(half):
        if staged():
            slots = chip_slots(me >> 1, half)
        else:
            slots = jnp.arange(D // CHIP_ROWS, dtype=jnp.int32)
        return jnp.concatenate([jnp.reshape(half, (1,)).astype(jnp.int32), slots])

    def ff_grad(half, after):
        return ff_weight_grad(order(half), normed_two, cotangent, both, hidden, after)

    def inner(half, after):
        return inner_back(
            half,
            marks,
            qkv,
            mixed_grad,
            logs,
            cosine,
            sine,
            edge_grad,
            edge_sum,
            from_lower,
            from_upper,
            after,
        )

    def finish(first, second):
        return input_grad(halves[0], tokens, gains, weights_one, first, second, grad)

    send, keep = halves
    def mixed_weight(half, dqkv):
        return mixed_weight_grad(order(half), normed, dqkv, mixed, low)

    ff_send = ff_grad(send, [])
    ff_keep = ff_grad(keep, [ff_send])
    result = result_of(residual, hidden, weights_two, [ff_keep])
    behind = []
    if staged():
        near, far = core_sum(ff_keep, stage_after(exchange(ff_send, CORE), result))
        behind = [far]
    low, mixed_grad, grad = dense_back(residual, cotangent, both, gains, weights_two, behind)
    edge_grad, edge_sum, away = edge_back(marks, qkv, mixed_grad, logs, cosine, sine, lower, upper)
    from_upper = passed_along(away[0], -1)
    from_lower = passed_along(away[1], 1)

    if staged():
        near, far = far_sum(near, stage_after(exchange(far, FAR), from_lower, from_upper))
        first = inner(send, [far])
        mixed_send = mixed_weight(send, first)
        parts = near_sum(near, stage_after(exchange(far, NEAR), mixed_send))
        second = inner(keep, parts)
        mixed_keep = mixed_weight(keep, second)
        mixed_near, mixed_far = core_sum(
            mixed_keep, exchange(stage_after(mixed_send, parts[0]), CORE)
        )
        grad_in = finish(first, stage_after(second, mixed_far))
        mixed_near, mixed_far = far_sum(mixed_near, stage_after(exchange(mixed_far, FAR), grad_in))
        sum_ff = deep_sum(parts, mixed_far)
        mixed_parts = near_sum(mixed_near, exchange(mixed_far, NEAR))
        sum_mixed = deep_sum(mixed_parts, mixed_parts[0])
    else:
        first, second = inner(send, []), inner(keep, [])
        grad_in = finish(first, second)
        sum_ff = summed(ff_keep, ff_send)
        sum_mixed = summed(mixed_weight(keep, second), mixed_weight(send, first))
    sum_qkv = by_part(sum_mixed)
    sent_attn = jnp.concatenate(
        [sum_mixed[:, QKV_HALF:MIXED_HALF], sum_mixed[:, MIXED_HALF + QKV_HALF :]], axis=1
    )
    sent_in = jnp.concatenate(
        [sum_ff[:, :FF_HALF], sum_ff[:, FF_HALF : FF_HALF + FF_LEFT]], axis=1
    )
    sent_down = sum_ff[:, FF_HALF + FF_LEFT : FF_HALF + FF_LEFT + FF].T

    def gain_grad(summed, weight, gain):
        return jnp.sum(summed * weight.astype(F32), axis=1) / gain.astype(F32)

    return (
        result,
        grad_in,
        gain_grad(sum_qkv, qkv_weight, first_gain),
        sum_qkv,
        sent_attn,
        gain_grad(sent_in, feed_in_weight, second_gain),
        sent_in,
        sent_down,
    )


def solution(mesh):
    in_specs = (
        P("tok", None),
        P(),
        P("tok"),
        P("tok", None),
        P("tok", None),
        P("tok"),
        P("tok", None),
        P(None, "tok"),
        P("tok", None),
    )
    out_specs = (
        P("tok", None),
        P("tok", None),
        P("tok"),
        P("tok", None),
        P("tok", None),
        P("tok"),
        P("tok", None),
        P(None, "tok"),
    )
    return jax.shard_map(
        on_device, mesh=mesh, in_specs=in_specs, out_specs=out_specs, check_vma=False
    )
```

```python
from functools import partial

import jax
import jax.numpy as jnp
from jax import lax
from jax.experimental import pallas as pl
from jax.experimental.pallas import tpu as pltpu
from jax.sharding import PartitionSpec as P

D = 768
FF = 1152
HEADS = 12
HEAD_DIM = 64
HALF = 64
PAIRS = HEADS // 2
BLOCK = 128
SPAN = BLOCK + 2 * HALF
LANES = 128
QKV_HALF = 3 * D // 2
GROUP = D // 2
GROUP_PAIRS = PAIRS // 2
FF_HALF = 1792
FF_LEFT = 2 * FF - FF_HALF
MIXED_HALF = QKV_HALF + GROUP
MIB = 1024 * 1024
BF = jnp.bfloat16
F32 = jnp.float32


def dot(left, right, left_dim=1, right_dim=0):
    return lax.dot_general(
        left, right, (((left_dim,), (right_dim,)), ((), ())), preferred_element_type=F32
    )


def params(mib):
    return pltpu.CompilerParams(vmem_limit_bytes=mib * MIB)


def whole(shape):
    return pl.BlockSpec(shape, lambda *_: (0,) * len(shape))


def rows(shape):
    return pl.BlockSpec(shape, lambda i: (i,) + (0,) * (len(shape) - 1))


SMALL = pl.CostEstimate(flops=4000000000, bytes_accessed=1000, transcendentals=0)
SMEM = pl.BlockSpec(memory_space=pltpu.SMEM)
ANY = pl.BlockSpec(memory_space=pl.ANY)
VMEM = pl.BlockSpec(memory_space=pltpu.VMEM)
HBM = pl.BlockSpec(memory_space=pltpu.HBM)
HBM = pl.BlockSpec(memory_space=pltpu.HBM)


def lane_ids(shape):
    return lax.broadcasted_iota(jnp.int32, shape, len(shape) - 1)


def swap_halves(values):
    low = (lane_ids(values.shape) & (HEAD_DIM - 1)) < HEAD_DIM // 2
    return jnp.where(
        low, pltpu.roll(values, LANES - HEAD_DIM // 2, 1), pltpu.roll(values, HEAD_DIM // 2, 1)
    )


def normalized(values):
    centered = values - jnp.mean(values, axis=-1, keepdims=True)
    scale = lax.rsqrt(jnp.mean(centered * centered, axis=-1, keepdims=True) + 1e-05)
    return centered * scale, scale


def norm_back(grad, unit, scale, gains):
    grad_unit = grad * gains
    return scale * (
        grad_unit
        - jnp.mean(grad_unit, axis=-1, keepdims=True)
        - unit * jnp.mean(grad_unit * unit, axis=-1, keepdims=True)
    )


CHIP_ROWS = 48


class Weights:
    def __init__(self, arrays, places=None):
        self.arrays = arrays
        self.places = places

    def operands(self):
        if self.places is None:
            return list(self.arrays)
        return [self.places, *self.arrays]

    def specs(self):
        if self.places is None:
            return [ANY]
        return [SMEM, VMEM, VMEM, VMEM, VMEM]

    def scratch(self):
        width = self.arrays[0].shape[-1]
        return [pltpu.VMEM((2, D, width), BF), pltpu.SemaphoreType.DMA((1,))]


def load_weights(refs, out_ref, sems):
    if len(refs) == 1:
        copy = pltpu.make_async_copy(refs[0], out_ref, sems.at[0])
        copy.start()
        copy.wait()
        return
    places_ref = refs[0]
    core = places_ref[32]
    for index, source in enumerate(refs[1:]):
        half = core if index < 2 else 1 - core
        for slot in range(8):
            place = pl.multiple_of(places_ref[index * 8 + slot] * CHIP_ROWS, 16)
            out_ref[half, pl.ds(place, CHIP_ROWS), :] = source[
                slot * CHIP_ROWS : (slot + 1) * CHIP_ROWS, :
            ]


def qkv_kernel(count, x_ref, cos_ref, sin_ref, *refs):
    weight_refs = refs[:count]
    normed_ref, qkv_ref, gains_ref, w_ref, sems = refs[count:]

    @pl.when(pl.program_id(0) == 0)
    def _():
        load_weights(weight_refs, w_ref, sems)
        for half in range(2):
            turned = w_ref[half, :, QKV_HALF:].T.astype(F32)
            gains_ref[half * 8 : half * 8 + 8, :] = turned[:8]

    unit, _ = normalized(x_ref[...].astype(F32))
    normed = (unit * gains_ref[0:1, :]).astype(BF)
    normed_ref[...] = normed
    cosine = cos_ref[...]
    sine = sin_ref[...]
    for half in range(2):
        merged = dot(normed, w_ref[half, :, :QKV_HALF])
        for tile in range(QKV_HALF // LANES):
            lanes = slice(tile * LANES, (tile + 1) * LANES)
            part = merged[:, lanes]
            if tile * LANES < 2 * GROUP:
                part = part * cosine + swap_halves(part) * sine
            qkv_ref[half, :, lanes] = part.astype(BF)


def project_qkv(tokens, weights, cosine, sine):
    count = tokens.shape[0]
    size = min(256, count)
    operands = weights.operands()
    return pl.pallas_call(
        partial(qkv_kernel, len(operands)),
        grid=(count // size,),
        in_specs=[rows((size, D)), rows((size, LANES)), rows((size, LANES)), *weights.specs()],
        out_specs=[
            rows((size, D)),
            pl.BlockSpec((2, size, QKV_HALF), lambda i: (0, i, 0)),
            whole((16, D)),
        ],
        out_shape=[
            jax.ShapeDtypeStruct((count, D), BF),
            jax.ShapeDtypeStruct((2, count, QKV_HALF), BF),
            jax.ShapeDtypeStruct((16, D), F32),
        ],
        scratch_shapes=weights.scratch(),
        compiler_params=params(12),
        cost_estimate=SMALL,
        name="qkv",
    )(tokens, cosine, sine, *operands)


def window_bias(marks_ref, block):
    shape = (SPAN, 2 * BLOCK)
    first = marks_ref[3] + block * BLOCK
    key = lax.broadcasted_iota(jnp.int32, shape, 0)
    query = lax.broadcasted_iota(jnp.int32, (1, 2 * BLOCK), 1) & (BLOCK - 1)
    place = first + query
    lowest = query
    highest = query + 2 * HALF
    for index in range(3):
        mark = marks_ref[index]
        edge = mark - first + HALF
        past = place >= mark
        lowest = jnp.where(past, jnp.maximum(lowest, edge), lowest)
        highest = jnp.where(past, highest, jnp.minimum(highest, edge - 1))
    return jnp.where((key >= lowest) & (key <= highest), 0.0, -1e30).astype(F32)


def stacked(pair):
    low = lane_ids(pair.shape) < HEAD_DIM
    zero = jnp.zeros_like(pair)
    return jnp.concatenate([jnp.where(low, pair, zero), jnp.where(low, zero, pair)], axis=0)


def unstacked(both):
    low = lane_ids((BLOCK, LANES)) < HEAD_DIM
    return jnp.where(low, both[:BLOCK], both[BLOCK:])


def span_of(qkv_ref, lower_ref, upper_ref, half, block, part, sub):
    count = qkv_ref.shape[1]
    first = block * BLOCK - HALF
    lanes = slice(part * GROUP + sub * LANES, part * GROUP + (sub + 1) * LANES)
    halo_lanes = slice((part - 1) * GROUP + sub * LANES, (part - 1) * GROUP + (sub + 1) * LANES)
    own = qkv_ref[half, max(first, 0) : min(first + SPAN, count), lanes]
    if first < 0:
        own = jnp.concatenate([lower_ref[half, :, halo_lanes], own], axis=0)
    if first + SPAN > count:
        own = jnp.concatenate([own, upper_ref[half, :, halo_lanes]], axis=0)
    return own


def many_attend(operands):
    scores = [dot(keys, query, 1, 1) + bias for query, keys, _, bias in operands]
    peaks = [jnp.max(score, axis=0, keepdims=True) for score in scores]
    expos = [jnp.exp(score - peak) for score, peak in zip(scores, peaks)]
    totals = [jnp.sum(expo, axis=0, keepdims=True) for expo in expos]
    weights = [(expo * (1.0 / total)).astype(BF) for expo, total in zip(expos, totals)]
    mixed = [unstacked(dot(weight, item[2], 0, 0)) for weight, item in zip(weights, operands)]
    return [(mix, peak + jnp.log(total)) for mix, peak, total in zip(mixed, peaks, totals)]


def attend_kernel(marks_ref, qkv_ref, lower_ref, upper_ref, out_ref, log_ref):
    for block in range(qkv_ref.shape[1] // BLOCK):
        bias = window_bias(marks_ref, block)
        mine = slice(block * BLOCK, (block + 1) * BLOCK)
        for first in range(0, PAIRS, PAIRS_TOGETHER):
            pairs = range(first, first + PAIRS_TOGETHER)
            items = []
            for pair in pairs:
                half, sub = divmod(pair, GROUP_PAIRS)
                where = (qkv_ref, lower_ref, upper_ref, half, block)
                items.append(
                    (
                        stacked(qkv_ref[half, mine, sub * LANES : (sub + 1) * LANES] * BF(0.125)),
                        span_of(*where, 1, sub),
                        span_of(*where, 2, sub),
                        bias,
                    )
                )
            for pair, (mix, logs) in zip(pairs, many_attend(items)):
                half, sub = divmod(pair, GROUP_PAIRS)
                out_ref[mine, pair * LANES : (pair + 1) * LANES] = mix.astype(BF)
                log_ref[block, half, sub : sub + 1, :] = logs


def attend(marks, qkv, lower, upper):
    count = qkv.shape[1]
    blocks = count // BLOCK
    return pl.pallas_call(
        attend_kernel,
        in_specs=[SMEM, VMEM, VMEM, VMEM],
        out_specs=[VMEM, VMEM],
        out_shape=[
            jax.ShapeDtypeStruct((count, D), BF),
            jax.ShapeDtypeStruct((blocks, 2, 8, 2 * BLOCK), F32),
        ],
        compiler_params=params(8),
        cost_estimate=SMALL,
        name="attend",
    )(marks, qkv, lower, upper)


PAIRS_TOGETHER = 1
FF_PARTS = tuple((first, min(256, FF - first)) for first in range(0, FF, 256))


def dense_kernel(
    x_ref,
    mixed_ref,
    cot_ref,
    gains_ref,
    source_ref,
    residual_ref,
    normed_ref,
    both_ref,
    hidden_ref,
    w_ref,
    sems,
):
    ranges = [(3 * FF, D), (0, 3 * FF)]
    copies = [
        pltpu.make_async_copy(
            source_ref.at[:, pl.ds(first, size)], w_ref.at[:, pl.ds(first, size)], sems.at[index]
        )
        for index, (first, size) in enumerate(ranges)
    ]
    for copy in copies:
        copy.start()
    copies[0].wait()
    count = x_ref.shape[0]
    size = min(512, count)
    blocks = [slice(first, first + size) for first in range(0, count, size)]
    for mine in blocks:
        residual = x_ref[mine, :].astype(F32) + dot(mixed_ref[mine, :], w_ref[:, 3 * FF :])
        residual_ref[mine, :] = residual
        unit, _ = normalized(residual)
        normed_ref[mine, :] = (unit * gains_ref[8:9, :]).astype(BF)
    copies[1].wait()
    for mine in blocks:
        normed = normed_ref[mine, :]
        cot = cot_ref[mine, :]
        for first, size in FF_PARTS:
            gate_cols = slice(first, first + size)
            up_cols = slice(FF + first, FF + first + size)
            down_cols = slice(2 * FF + first, 2 * FF + first + size)
            gate = dot(normed, w_ref[:, gate_cols])
            up = dot(normed, w_ref[:, up_cols])
            grad_hidden = dot(cot, w_ref[:, down_cols])
            share = 0.5 + 0.5 * lax.erf(gate * 0.7071067811865476)
            active = gate * share
            slope = share + gate * (jnp.exp(-0.5 * gate * gate) * 0.3989422804014327)
            hidden_ref[mine, gate_cols] = (active * up).astype(BF)
            both_ref[mine, gate_cols] = (grad_hidden * up * slope).astype(BF)
            both_ref[mine, up_cols] = (grad_hidden * active).astype(BF)


def dense(tokens, mixed, cotangent, gains, weights):
    count = tokens.shape[0]
    wide = [(D, F32), (D, BF), (2 * FF, BF), (FF, BF)]
    return pl.pallas_call(
        dense_kernel,
        in_specs=[VMEM, VMEM, VMEM, VMEM, HBM],
        out_specs=[VMEM] * 4,
        out_shape=[jax.ShapeDtypeStruct((count, width), kind) for width, kind in wide],
        scratch_shapes=[pltpu.VMEM(weights.shape, BF), pltpu.SemaphoreType.DMA((2,))],
        compiler_params=params(14),
        cost_estimate=SMALL,
        name="dense",
    )(tokens, mixed, cotangent, gains, weights)


def dense_back_kernel(residual_ref, cot_ref, both_ref, gains_ref, w_ref, *rest):
    low_ref, mixed_grad_ref, grad_ref = rest[-3:]
    unit, scale = normalized(residual_ref[...])
    grad_normed = dot(both_ref[...], w_ref[:, : 2 * FF], 1, 1)
    grad = cot_ref[...].astype(F32) + norm_back(grad_normed, unit, scale, gains_ref[8:9, :])
    grad_ref[...] = grad
    low = grad.astype(BF)
    low_ref[...] = low
    mixed_grad_ref[...] = dot(low, w_ref[:, 3 * FF :], 1, 1).astype(BF)


def dense_back(residual, cotangent, both, gains, weights, after):
    count = residual.shape[0]
    size = min(512, count)
    wide = [(D, BF), (D, BF), (D, F32)]
    return pl.pallas_call(
        dense_back_kernel,
        grid=(count // size,),
        in_specs=[
            rows((size, D)),
            rows((size, D)),
            rows((size, 2 * FF)),
            whole((16, D)),
            whole(weights.shape),
            *[ANY for _ in after],
        ],
        out_specs=[rows((size, width)) for width, _ in wide],
        out_shape=[jax.ShapeDtypeStruct((count, width), kind) for width, kind in wide],
        compiler_params=params(20),
        cost_estimate=SMALL,
        name="dense_back",
    )(residual, cotangent, both, gains, weights, *after)


def result_kernel(residual_ref, hidden_ref, w_ref, *rest):
    product = dot(hidden_ref[...], w_ref[:, 2 * FF : 3 * FF], 1, 1)
    rest[-1][...] = (residual_ref[...] + product).astype(BF)


def result_of(residual, hidden, weights, after):
    count = residual.shape[0]
    size = min(512, count)
    return pl.pallas_call(
        result_kernel,
        grid=(count // size,),
        in_specs=[rows((size, D)), rows((size, FF)), whole(weights.shape), *[ANY for _ in after]],
        out_specs=rows((size, D)),
        out_shape=jax.ShapeDtypeStruct((count, D), BF),
        compiler_params=params(16),
        cost_estimate=SMALL,
        name="result",
    )(residual, hidden, weights, *after)


def pair_back(query, keys, values, out_grad, logs, bias):
    scores = dot(keys, query, 1, 1) + bias
    weights = jnp.exp(scores - logs)
    weight_grad = dot(values, out_grad, 1, 1)
    score_grad = weights * (weight_grad - jnp.sum(weights * weight_grad, axis=0, keepdims=True))
    score_grad = score_grad.astype(BF)
    key_grad = dot(score_grad, query)
    value_grad = dot(weights.astype(BF), out_grad)
    query_grad = unstacked(dot(score_grad, keys, 0, 0)) * 0.125
    return query_grad, key_grad, value_grad


def many_back(operands):
    scores = [dot(keys, query, 1, 1) for query, keys, _, _, _, _ in operands]
    weight_grads = [dot(values, out_grad, 1, 1) for _, _, values, out_grad, _, _ in operands]
    weights = [jnp.exp(score + item[5] - item[4]) for score, item in zip(scores, operands)]
    value_grads = [dot(weight.astype(BF), item[3]) for weight, item in zip(weights, operands)]
    score_grads = [
        (weight * (grad - jnp.sum(weight * grad, axis=0, keepdims=True))).astype(BF)
        for weight, grad in zip(weights, weight_grads)
    ]
    key_grads = [dot(grad, item[0]) for grad, item in zip(score_grads, operands)]
    query_grads = [
        unstacked(dot(grad, item[1], 0, 0)) * 0.125 for grad, item in zip(score_grads, operands)
    ]
    return list(zip(query_grads, key_grads, value_grads))


def turned_back(values, cosine, sine):
    return values * cosine - swap_halves(values) * sine


def edge_back_kernel(
    marks_ref,
    mixed_grad_ref,
    log_ref,
    cos_ref,
    sin_ref,
    qkv_ref,
    lower_ref,
    upper_ref,
    grad_ref,
    sum_ref,
    away_ref,
):
    count = qkv_ref.shape[1]
    for side, block in enumerate((0, count // BLOCK - 1)):
        bias = window_bias(marks_ref, block)
        mine = slice(block * BLOCK, (block + 1) * BLOCK)
        sent = slice(0, HALF) if side == 0 else slice(SPAN - HALF, SPAN)
        for half in range(2):
            items = []
            for sub in range(GROUP_PAIRS):
                pair = half * GROUP_PAIRS + sub
                where = (qkv_ref, lower_ref, upper_ref, half, block)
                items.append(
                    (
                        stacked(qkv_ref[half, mine, sub * LANES : (sub + 1) * LANES] * BF(0.125)),
                        span_of(*where, 1, sub),
                        span_of(*where, 2, sub),
                        stacked(mixed_grad_ref[mine, pair * LANES : (pair + 1) * LANES]),
                        log_ref[block, half, sub : sub + 1, :],
                        bias,
                    )
                )
            for sub, (query_grad, key_grad, value_grad) in enumerate(many_back(items)):
                lanes = slice(sub * LANES, (sub + 1) * LANES)
                value_lanes = slice(GROUP + sub * LANES, GROUP + (sub + 1) * LANES)
                grad_ref[half, side, :, lanes] = turned_back(
                    query_grad, cos_ref[mine, :], sin_ref[mine, :]
                ).astype(BF)
                sum_ref[half, side, :, lanes] = key_grad
                sum_ref[half, side, :, value_lanes] = value_grad
                away_ref[side, half, :, lanes] = key_grad[sent].astype(BF)
                away_ref[side, half, :, value_lanes] = value_grad[sent].astype(BF)


def edge_back(marks, qkv, mixed_grad, logs, cosine, sine, lower, upper):
    return pl.pallas_call(
        edge_back_kernel,
        in_specs=[SMEM, *[VMEM] * 7],
        out_specs=[VMEM, VMEM, VMEM],
        out_shape=[
            jax.ShapeDtypeStruct((2, 2, BLOCK, GROUP), BF),
            jax.ShapeDtypeStruct((2, 2, SPAN, 2 * GROUP), F32),
            jax.ShapeDtypeStruct((2, 2, HALF, 2 * GROUP), BF),
        ],
        compiler_params=params(8),
        cost_estimate=SMALL,
        name="edge_back",
    )(marks, mixed_grad, logs, cosine, sine, qkv, lower, upper)


TOGETHER = 1


def inner_back_kernel(
    group_ref,
    marks_ref,
    mixed_grad_ref,
    log_ref,
    cos_ref,
    sin_ref,
    edge_grad_ref,
    edge_sum_ref,
    from_lower_ref,
    from_upper_ref,
    qkv_ref,
    *rest,
):
    grad_ref, sum_ref = rest[-2:]
    count = qkv_ref.shape[1]
    inner = count // BLOCK - 2
    sum_ref[0 : SPAN - HALF, :] = edge_sum_ref[0, 0, HALF:, :]
    sum_ref[0:HALF, :] += from_lower_ref[0].astype(F32)
    grad_ref[0:BLOCK, 0:GROUP] = edge_grad_ref[0, 0]
    grad_ref[count - BLOCK :, 0:GROUP] = edge_grad_ref[0, 1]

    def finish(place):
        own_cosine = cos_ref[place, :]
        own_sine = sin_ref[place, :]
        for sub in range(GROUP_PAIRS):
            lanes = slice(sub * LANES, (sub + 1) * LANES)
            key_lanes = slice(GROUP + sub * LANES, GROUP + (sub + 1) * LANES)
            grad_ref[place, key_lanes] = turned_back(
                sum_ref[place, lanes], own_cosine, own_sine
            ).astype(BF)
        grad_ref[place, 2 * GROUP :] = sum_ref[place, GROUP:].astype(BF)

    for first in range(1, inner + 1, TOGETHER):
        blocks = range(first, min(first + TOGETHER, inner + 1))
        places = []
        items = []
        for block in blocks:
            bias = window_bias(marks_ref, block)
            start = block * BLOCK - HALF
            window = slice(start, start + SPAN)
            mine = slice(block * BLOCK, (block + 1) * BLOCK)
            for sub in range(GROUP_PAIRS):
                lanes = slice(sub * LANES, (sub + 1) * LANES)
                places.append((mine, start, sub))
                items.append(
                    (
                        stacked(qkv_ref[0, mine, lanes] * BF(0.125)),
                        qkv_ref[0, window, GROUP + sub * LANES : GROUP + (sub + 1) * LANES],
                        qkv_ref[0, window, 2 * GROUP + sub * LANES : 2 * GROUP + (sub + 1) * LANES],
                        stacked(mixed_grad_ref[mine, lanes]),
                        log_ref[block, 0, sub : sub + 1, :],
                        bias,
                    )
                )
        for (mine, start, sub), (query_grad, key_grad, value_grad) in zip(places, many_back(items)):
            lanes = slice(sub * LANES, (sub + 1) * LANES)
            value_lanes = slice(GROUP + sub * LANES, GROUP + (sub + 1) * LANES)
            older = slice(start, start + BLOCK)
            newer = slice(start + BLOCK, start + SPAN)
            sum_ref[older, lanes] += key_grad[:BLOCK]
            sum_ref[newer, lanes] = key_grad[BLOCK:]
            sum_ref[older, value_lanes] += value_grad[:BLOCK]
            sum_ref[newer, value_lanes] = value_grad[BLOCK:]
            grad_ref[mine, lanes] = turned_back(query_grad, cos_ref[mine, :], sin_ref[mine, :]).astype(BF)
        finish(slice(0 if first == 1 else blocks[0] * BLOCK - HALF, (blocks[-1] + 1) * BLOCK - HALF))

    tail = SPAN - HALF
    sum_ref[count - tail : count - HALF, :] += edge_sum_ref[0, 1, 0:BLOCK, :]
    sum_ref[count - HALF :, :] = edge_sum_ref[0, 1, BLOCK:tail, :] + from_upper_ref[0].astype(F32)
    finish(slice(count - tail, count))


def inner_back(group, marks, qkv, mixed_grad, logs, cosine, sine, edge_grad, edge_sum, from_lower, from_upper, after):
    count = qkv.shape[1]
    return pl.pallas_call(
        inner_back_kernel,
        grid_spec=pltpu.PrefetchScalarGridSpec(
            num_scalar_prefetch=1,
            grid=(1,),
            in_specs=[
                SMEM,
                pl.BlockSpec((count, GROUP), lambda i, g: (0, g[0])),
                pl.BlockSpec((count // BLOCK, 1, 8, 2 * BLOCK), lambda i, g: (0, g[0], 0, 0)),
                pl.BlockSpec((count, LANES), lambda i, g: (0, 0)),
                pl.BlockSpec((count, LANES), lambda i, g: (0, 0)),
                pl.BlockSpec((1, 2, BLOCK, GROUP), lambda i, g: (g[0], 0, 0, 0)),
                pl.BlockSpec((1, 2, SPAN, 2 * GROUP), lambda i, g: (g[0], 0, 0, 0)),
                pl.BlockSpec((1, HALF, 2 * GROUP), lambda i, g: (g[0], 0, 0)),
                pl.BlockSpec((1, HALF, 2 * GROUP), lambda i, g: (g[0], 0, 0)),
                pl.BlockSpec((1, count, QKV_HALF), lambda i, g: (g[0], 0, 0)),
                *[ANY for _ in after],
            ],
            out_specs=pl.BlockSpec((count, QKV_HALF), lambda i, g: (0, 0)),
            scratch_shapes=[
                pltpu.VMEM((count, 2 * GROUP), F32),
            ],
        ),
        out_shape=jax.ShapeDtypeStruct((count, QKV_HALF), BF),
        compiler_params=params(8),
        cost_estimate=SMALL,
        name="inner_back",
    )(
        jnp.reshape(group, (1,)).astype(jnp.int32),
        marks,
        mixed_grad,
        logs,
        cosine,
        sine,
        edge_grad,
        edge_sum,
        from_lower,
        from_upper,
        qkv,
        *after,
    )


def input_grad_kernel(count, order_ref, x_ref, gains_ref, first_ref, second_ref, grad_ref, *refs):
    weight_refs = refs[:count]
    out_ref, w_ref, sems = refs[count:]

    @pl.when(pl.program_id(0) == 0)
    def _():
        load_weights(weight_refs, w_ref, sems)

    unit, scale = normalized(x_ref[...].astype(F32))
    half = order_ref[0]
    grad_normed = dot(first_ref[...], w_ref[half, :, :QKV_HALF], 1, 1) + dot(
        second_ref[...], w_ref[1 - half, :, :QKV_HALF], 1, 1
    )
    out_ref[...] = grad_ref[...] + norm_back(grad_normed, unit, scale, gains_ref[0:1, :])


def input_grad(half, tokens, gains, weights, first, second, grad):
    count = tokens.shape[0]
    size = min(256, count)
    operands = weights.operands()
    return pl.pallas_call(
        partial(input_grad_kernel, len(operands)),
        grid=(count // size,),
        in_specs=[
            SMEM,
            rows((size, D)),
            whole((16, D)),
            rows((size, QKV_HALF)),
            rows((size, QKV_HALF)),
            rows((size, D)),
            *weights.specs(),
        ],
        out_specs=rows((size, D)),
        out_shape=jax.ShapeDtypeStruct((count, D), F32),
        scratch_shapes=weights.scratch(),
        compiler_params=params(12),
        cost_estimate=SMALL,
        name="input_grad",
    )(jnp.reshape(half, (1,)).astype(jnp.int32), tokens, gains, first, second, grad, *operands)


TILE = 256


def store_slots(slots_ref, out_ref, product):
    step = CHIP_ROWS
    for index in range(D // step):
        place = pl.multiple_of(slots_ref[1 + index] * step, 16)
        out_ref[pl.ds(place, step), :] = product[index * step : (index + 1) * step].astype(BF)


def weight_products(slots_ref, out_ref, turned, grad_ref, first, size):
    for tile in range(0, size, TILE):
        width = min(TILE, size - tile)
        product = dot(turned, grad_ref[:, tile : tile + width])
        for index in range(D // CHIP_ROWS):
            place = pl.multiple_of(slots_ref[1 + index] * CHIP_ROWS, 16)
            out_ref[pl.ds(place, CHIP_ROWS), first + tile : first + tile + width] = product[
                index * CHIP_ROWS : (index + 1) * CHIP_ROWS
            ].astype(BF)


def mixed_weight_kernel(slots_ref, normed_ref, grad_ref, mixed_ref, low_ref, *rest):
    out_ref = rest[-1]
    weight_products(slots_ref, out_ref, normed_ref[...].T, grad_ref, 0, QKV_HALF)
    lanes = pl.ds(pl.multiple_of(slots_ref[0] * GROUP, LANES), GROUP)
    weight_products(slots_ref, out_ref, mixed_ref[...].T, low_ref.at[:, lanes], QKV_HALF, GROUP)


def mixed_weight_grad(slots, normed, dqkv, mixed, low, after=()):
    count = normed.shape[0]
    return pl.pallas_call(
        mixed_weight_kernel,
        in_specs=[SMEM, *[VMEM] * 4, *[ANY for _ in after]],
        out_specs=VMEM,
        out_shape=jax.ShapeDtypeStruct((D, MIXED_HALF), BF),
        compiler_params=params(8),
        cost_estimate=SMALL,
        name="mixed_weight_grad",
    )(slots, normed, dqkv, mixed, low, *after)


def ff_weight_kernel(slots_ref, normed_ref, cot_ref, both_ref, hidden_ref, *rest):
    out_ref = rest[-1]

    @pl.when(slots_ref[0] == 0)
    def _():
        left = both_ref.at[:, 0:FF_HALF]
        weight_products(slots_ref, out_ref, normed_ref[...].T, left, 0, FF_HALF)

    @pl.when(slots_ref[0] == 1)
    def _():
        left = both_ref.at[:, FF_HALF : 2 * FF]
        weight_products(slots_ref, out_ref, normed_ref[...].T, left, 0, FF_LEFT)
        weight_products(slots_ref, out_ref, cot_ref[...].T, hidden_ref, FF_LEFT, FF)
        out_ref[:, FF_LEFT + FF :] = jnp.zeros((D, FF_HALF - FF_LEFT - FF), BF)


def ff_weight_grad(slots, normed, cot, both, hidden, after):
    count = normed.shape[0]
    return pl.pallas_call(
        ff_weight_kernel,
        in_specs=[SMEM, *[VMEM] * 4, *[ANY for _ in after]],
        out_specs=VMEM,
        out_shape=jax.ShapeDtypeStruct((D, FF_HALF), BF),
        compiler_params=params(8),
        cost_estimate=SMALL,
        name="ff_weight_grad",
    )(slots, normed, cot, both, hidden, *after)


def join_kernel(*refs):
    out_ref = refs[-1]
    first = 0
    for ref in refs[:-1]:
        out_ref[first : first + ref.shape[0], :] = ref[...]
        first += ref.shape[0]


def join(*parts):
    count = sum(part.shape[0] for part in parts)
    width = parts[0].shape[1]
    return pl.pallas_call(
        join_kernel,
        in_specs=[VMEM for _ in parts],
        out_specs=VMEM,
        out_shape=jax.ShapeDtypeStruct((count, width), parts[0].dtype),
        compiler_params=params(8),
        cost_estimate=SMALL,
        name="join",
    )(*parts)


def doc_marks(doc_lengths, row_count):
    me = lax.axis_index("tok")
    ends = jnp.cumsum(doc_lengths).astype(jnp.int32)
    before = jnp.where(me > 0, ends[jnp.maximum(me - 1, 0)], 0)
    return jnp.stack([before, ends[me], ends[me + 1], me * row_count]).astype(jnp.int32)


def rotary_tables(marks, row_count):
    place = marks[3] + jnp.arange(row_count, dtype=jnp.int32)
    offset = place - jnp.where(place >= marks[1], marks[1], marks[0])
    frequency = 10000.0 ** (-jnp.arange(0, HEAD_DIM, 2, dtype=F32) / HEAD_DIM)
    angles = offset.astype(F32)[:, None] * frequency[None, :]
    cosine = jnp.cos(angles)
    sine = jnp.sin(angles)
    return (
        jnp.concatenate([cosine] * 4, axis=1),
        jnp.concatenate([-sine, sine, -sine, sine], axis=1),
    )


def passed_along(value, steps):
    count = lax.axis_size("tok")
    first, last = (max(0, -steps), min(count, count - steps))
    return lax.ppermute(value, "tok", [(at, at + steps) for at in range(first, last)])


STAGED_DEVICES = 32


def staged():
    return lax.axis_size("tok") == STAGED_DEVICES


def exchange(value, by_core):
    pairs = [(at, at ^ by_core[at & 1]) for at in range(lax.axis_size("tok"))]
    return lax.ppermute(value, "tok", pairs)


CORE = (1, 1)
DEEP = tuple((step << 3, step << 3) for step in range(4))
NEAR = (2, 4)
FAR = (4, 2)


def slot_codes(core):
    slot = jnp.arange(16, dtype=jnp.int32)
    depth, near, far = (slot & 3, (slot >> 2) & 1, slot >> 3)
    return (depth << 2) | jnp.where(core == 0, (far << 1) | near, (near << 1) | far)


def chip_slots(chip, core):
    code = jnp.arange(16, dtype=jnp.int32) ^ chip
    depth, second, first = (code >> 2, (code >> 1) & 1, code & 1)
    return depth | jnp.where(core == 0, (second << 3) | (first << 2), (first << 3) | (second << 2))


def stage_after(value, *others):
    return lax.optimization_barrier((value, *others))[0]


def in_hbm(value):
    return pltpu.with_memory_space_constraint(value, pltpu.HBM)


def core_pieces(shard):
    core = lax.axis_index("tok") & 1
    half = shard.shape[1] // 2
    keep = jnp.where(core == 0, shard[:, :half], shard[:, half:])
    send = jnp.where(core == 0, shard[:, half:], shard[:, :half])
    came = exchange(send, CORE)
    return jnp.concatenate(
        [jnp.where(core == 0, keep, came), jnp.where(core == 0, came, keep)], axis=0
    )


def final_gather(held, far):
    me = lax.axis_index("tok")
    core = me & 1
    chip = me >> 1
    places = jnp.concatenate(
        [slot_codes(core) ^ chip, slot_codes(1 - core) ^ chip, jnp.full((1,), core, jnp.int32)]
    )
    return Weights([held, far, exchange(held, CORE), exchange(far, CORE)], places)


def whole_weights(shard):
    full = lax.all_gather(shard, "tok", axis=0, tiled=True)
    half = full.shape[1] // 2
    return Weights([jnp.stack([full[:, :half], full[:, half:]])])


def added(left, right):
    return (left.astype(F32) + right.astype(F32)).astype(BF)


def core_sum(keep, came):
    return added(keep[:384], came[:384]), added(keep[384:], came[384:])


def far_sum(near, came):
    return added(near[:192], came[:192]), added(near[192:], came[192:])


def near_sum(near, came):
    return [
        added(near[first : first + CHIP_ROWS], came[first : first + CHIP_ROWS])
        for first in range(0, 192, CHIP_ROWS)
    ]


def deep_sum(parts, *after):
    core = lax.axis_index("tok") & 1
    total = parts[0].astype(F32)
    for step in (1, 2, 3):
        total = total + stage_after(exchange(parts[step], DEEP[step]), after[step - 1]).astype(F32)
    share = CHIP_ROWS // 2
    lower, upper = (total[:share], total[share:])
    own = jnp.where(core == 0, lower, upper)
    came = exchange(jnp.where(core == 0, upper, lower), CORE)
    return jnp.concatenate(
        [jnp.where(core == 0, own, came), jnp.where(core == 0, came, own)], axis=1
    )


def summed(keep, send):
    full = jnp.concatenate([keep, send], axis=1)
    return lax.psum_scatter(full.astype(F32), "tok", scatter_dimension=0, tiled=True)


def by_part(groups):
    return jnp.concatenate(
        [
            groups[:, half * MIXED_HALF + part * GROUP : half * MIXED_HALF + (part + 1) * GROUP]
            for part in range(3)
            for half in range(2)
        ],
        axis=1,
    )


def on_device(
    tokens,
    doc_lengths,
    first_gain,
    qkv_weight,
    attn_weight,
    second_gain,
    feed_in_weight,
    feed_out_weight,
    cotangent,
):
    row_count = tokens.shape[0]
    share = first_gain.shape[0]

    def spread(gain):
        return jnp.broadcast_to(gain[:, None], (share, LANES))

    def group_of(half):
        return [
            qkv_weight[:, part * D + half * GROUP : part * D + (half + 1) * GROUP]
            for part in range(3)
        ]

    shard_one = jnp.concatenate(
        [*group_of(0), spread(first_gain), *group_of(1), spread(second_gain)], axis=1
    )
    shard_two = jnp.concatenate([feed_in_weight, feed_out_weight.T, attn_weight], axis=1)
    weights_two = lax.all_gather(shard_two, "tok", axis=0, tiled=True)
    if staged():
        piece = core_pieces(shard_one)
        marks = doc_marks(stage_after(doc_lengths, piece), row_count)
        cosine, sine = rotary_tables(marks, row_count)
        came = [exchange(piece, DEEP[step]) for step in (1, 2, 3)]
        *came, marks = lax.optimization_barrier((*came, marks, cosine, sine))[:4]
        one = join(piece, *came)
        one = join(one, exchange(one, NEAR))
        weights_one = final_gather(one, exchange(one, FAR))
    else:
        marks = doc_marks(doc_lengths, row_count)
        cosine, sine = rotary_tables(marks, row_count)
        weights_one = whole_weights(shard_one)
    normed, qkv, gains = project_qkv(tokens, weights_one, in_hbm(cosine), in_hbm(sine))
    lower = passed_along(qkv[:, row_count - HALF :, GROUP:], 1)
    upper = passed_along(qkv[:, :HALF, GROUP:], -1)
    mixed, logs = attend(marks, qkv, lower, upper)
    residual, normed_two, both, hidden = dense(tokens, mixed, cotangent, gains, in_hbm(weights_two))
    me = lax.axis_index("tok")
    if staged():
        halves = (1 - (me & 1), me & 1)
    else:
        halves = (jnp.int32(1), jnp.int32(0))

    def order(half):
        if staged():
            slots = chip_slots(me >> 1, half)
        else:
            slots = jnp.arange(D // CHIP_ROWS, dtype=jnp.int32)
        return jnp.concatenate([jnp.reshape(half, (1,)).astype(jnp.int32), slots])

    def ff_grad(half, after):
        return ff_weight_grad(order(half), normed_two, cotangent, both, hidden, after)

    def inner(half, after):
        return inner_back(
            half,
            marks,
            qkv,
            mixed_grad,
            logs,
            cosine,
            sine,
            edge_grad,
            edge_sum,
            from_lower,
            from_upper,
            after,
        )

    def finish(first, second):
        return input_grad(halves[0], tokens, gains, weights_one, first, second, grad)

    send, keep = halves
    def mixed_weight(half, dqkv):
        return mixed_weight_grad(order(half), normed, dqkv, mixed, low)

    ff_send = ff_grad(send, [])
    ff_keep = ff_grad(keep, [ff_send])
    result = result_of(residual, hidden, weights_two, [ff_keep])
    behind = []
    if staged():
        near, far = core_sum(ff_keep, stage_after(exchange(ff_send, CORE), result))
        behind = [far]
    low, mixed_grad, grad = dense_back(residual, cotangent, both, gains, weights_two, behind)
    edge_grad, edge_sum, away = edge_back(marks, qkv, mixed_grad, logs, cosine, sine, lower, upper)
    from_upper = passed_along(away[0], -1)
    from_lower = passed_along(away[1], 1)

    if staged():
        near, far = far_sum(near, stage_after(exchange(far, FAR), from_lower, from_upper))
        first = inner(send, [far])
        mixed_send = mixed_weight(send, first)
        parts = near_sum(near, stage_after(exchange(far, NEAR), mixed_send))
        second = inner(keep, parts)
        mixed_keep = mixed_weight(keep, second)
        mixed_near, mixed_far = core_sum(
            mixed_keep, exchange(stage_after(mixed_send, parts[0]), CORE)
        )
        grad_in = finish(first, stage_after(second, mixed_far))
        mixed_near, mixed_far = far_sum(mixed_near, stage_after(exchange(mixed_far, FAR), grad_in))
        sum_ff = deep_sum(parts, *[mixed_far] * 3)
        mixed_parts = near_sum(mixed_near, exchange(mixed_far, NEAR))
        sum_mixed = deep_sum(mixed_parts, *[mixed_parts[0]] * 3)
    else:
        first, second = inner(send, []), inner(keep, [])
        grad_in = finish(first, second)
        sum_ff = summed(ff_keep, ff_send)
        sum_mixed = summed(mixed_weight(keep, second), mixed_weight(send, first))
    sum_qkv = by_part(sum_mixed)
    sent_attn = jnp.concatenate(
        [sum_mixed[:, QKV_HALF:MIXED_HALF], sum_mixed[:, MIXED_HALF + QKV_HALF :]], axis=1
    )
    sent_in = jnp.concatenate(
        [sum_ff[:, :FF_HALF], sum_ff[:, FF_HALF : FF_HALF + FF_LEFT]], axis=1
    )
    sent_down = sum_ff[:, FF_HALF + FF_LEFT : FF_HALF + FF_LEFT + FF].T

    def gain_grad(summed, weight, gain):
        return jnp.sum(summed * weight.astype(F32), axis=1) / gain.astype(F32)

    return (
        result,
        grad_in,
        gain_grad(sum_qkv, qkv_weight, first_gain),
        sum_qkv,
        sent_attn,
        gain_grad(sent_in, feed_in_weight, second_gain),
        sent_in,
        sent_down,
    )


def solution(mesh):
    in_specs = (
        P("tok", None),
        P(),
        P("tok"),
        P("tok", None),
        P("tok", None),
        P("tok"),
        P("tok", None),
        P(None, "tok"),
        P("tok", None),
    )
    out_specs = (
        P("tok", None),
        P("tok", None),
        P("tok"),
        P("tok", None),
        P("tok", None),
        P("tok"),
        P("tok", None),
        P(None, "tok"),
    )
    return jax.shard_map(
        on_device, mesh=mesh, in_specs=in_specs, out_specs=out_specs, check_vma=False
    )
```

```python
from functools import partial

import jax
import jax.numpy as jnp
from jax import lax
from jax.experimental import pallas as pl
from jax.experimental.pallas import tpu as pltpu
from jax.sharding import PartitionSpec as P

D = 768
FF = 1152
HEADS = 12
HEAD_DIM = 64
HALF = 64
PAIRS = HEADS // 2
BLOCK = 128
SPAN = BLOCK + 2 * HALF
LANES = 128
QKV_HALF = 3 * D // 2
GROUP = D // 2
GROUP_PAIRS = PAIRS // 2
FF_HALF = 1792
FF_LEFT = 2 * FF - FF_HALF
MIXED_HALF = QKV_HALF + GROUP
MIB = 1024 * 1024
BF = jnp.bfloat16
F32 = jnp.float32


def dot(left, right, left_dim=1, right_dim=0):
    return lax.dot_general(
        left, right, (((left_dim,), (right_dim,)), ((), ())), preferred_element_type=F32
    )


def params(mib):
    return pltpu.CompilerParams(vmem_limit_bytes=mib * MIB)


def whole(shape):
    return pl.BlockSpec(shape, lambda *_: (0,) * len(shape))


def rows(shape):
    return pl.BlockSpec(shape, lambda i: (i,) + (0,) * (len(shape) - 1))


SMALL = pl.CostEstimate(flops=4000000000, bytes_accessed=1000, transcendentals=0)
SMEM = pl.BlockSpec(memory_space=pltpu.SMEM)
ANY = pl.BlockSpec(memory_space=pl.ANY)
VMEM = pl.BlockSpec(memory_space=pltpu.VMEM)
HBM = pl.BlockSpec(memory_space=pltpu.HBM)
HBM = pl.BlockSpec(memory_space=pltpu.HBM)


def lane_ids(shape):
    return lax.broadcasted_iota(jnp.int32, shape, len(shape) - 1)


def swap_halves(values):
    low = (lane_ids(values.shape) & (HEAD_DIM - 1)) < HEAD_DIM // 2
    return jnp.where(
        low, pltpu.roll(values, LANES - HEAD_DIM // 2, 1), pltpu.roll(values, HEAD_DIM // 2, 1)
    )


def normalized(values):
    centered = values - jnp.mean(values, axis=-1, keepdims=True)
    scale = lax.rsqrt(jnp.mean(centered * centered, axis=-1, keepdims=True) + 1e-05)
    return centered * scale, scale


def norm_back(grad, unit, scale, gains):
    grad_unit = grad * gains
    return scale * (
        grad_unit
        - jnp.mean(grad_unit, axis=-1, keepdims=True)
        - unit * jnp.mean(grad_unit * unit, axis=-1, keepdims=True)
    )


CHIP_ROWS = 48


class Weights:
    def __init__(self, arrays, places=None):
        self.arrays = arrays
        self.places = places

    def operands(self):
        if self.places is None:
            return list(self.arrays)
        return [self.places, *self.arrays]

    def specs(self):
        if self.places is None:
            return [ANY]
        return [SMEM, VMEM, VMEM, VMEM, VMEM]

    def scratch(self):
        width = self.arrays[0].shape[-1]
        return [pltpu.VMEM((2, D, width), BF), pltpu.SemaphoreType.DMA((1,))]


def load_weights(refs, out_ref, sems):
    if len(refs) == 1:
        copy = pltpu.make_async_copy(refs[0], out_ref, sems.at[0])
        copy.start()
        copy.wait()
        return
    places_ref = refs[0]
    core = places_ref[32]
    for index, source in enumerate(refs[1:]):
        half = core if index < 2 else 1 - core
        for slot in range(8):
            place = pl.multiple_of(places_ref[index * 8 + slot] * CHIP_ROWS, 16)
            out_ref[half, pl.ds(place, CHIP_ROWS), :] = source[
                slot * CHIP_ROWS : (slot + 1) * CHIP_ROWS, :
            ]


def qkv_kernel(count, x_ref, cos_ref, sin_ref, *refs):
    weight_refs = refs[:count]
    normed_ref, qkv_ref, gains_ref, w_ref, sems = refs[count:]

    @pl.when(pl.program_id(0) == 0)
    def _():
        load_weights(weight_refs, w_ref, sems)
        for half in range(2):
            turned = w_ref[half, :, QKV_HALF:].T.astype(F32)
            gains_ref[half * 8 : half * 8 + 8, :] = turned[:8]

    unit, _ = normalized(x_ref[...].astype(F32))
    normed = (unit * gains_ref[0:1, :]).astype(BF)
    normed_ref[...] = normed
    cosine = cos_ref[...]
    sine = sin_ref[...]
    for half in range(2):
        merged = dot(normed, w_ref[half, :, :QKV_HALF])
        for tile in range(QKV_HALF // LANES):
            lanes = slice(tile * LANES, (tile + 1) * LANES)
            part = merged[:, lanes]
            if tile * LANES < 2 * GROUP:
                part = part * cosine + swap_halves(part) * sine
            qkv_ref[half, :, lanes] = part.astype(BF)


def project_qkv(tokens, weights, cosine, sine):
    count = tokens.shape[0]
    size = min(256, count)
    operands = weights.operands()
    return pl.pallas_call(
        partial(qkv_kernel, len(operands)),
        grid=(count // size,),
        in_specs=[rows((size, D)), rows((size, LANES)), rows((size, LANES)), *weights.specs()],
        out_specs=[
            rows((size, D)),
            pl.BlockSpec((2, size, QKV_HALF), lambda i: (0, i, 0)),
            whole((16, D)),
        ],
        out_shape=[
            jax.ShapeDtypeStruct((count, D), BF),
            jax.ShapeDtypeStruct((2, count, QKV_HALF), BF),
            jax.ShapeDtypeStruct((16, D), F32),
        ],
        scratch_shapes=weights.scratch(),
        compiler_params=params(12),
        cost_estimate=SMALL,
        name="qkv",
    )(tokens, cosine, sine, *operands)


def window_bias(marks_ref, block):
    shape = (SPAN, 2 * BLOCK)
    first = marks_ref[3] + block * BLOCK
    key = lax.broadcasted_iota(jnp.int32, shape, 0)
    query = lax.broadcasted_iota(jnp.int32, (1, 2 * BLOCK), 1) & (BLOCK - 1)
    place = first + query
    lowest = query
    highest = query + 2 * HALF
    for index in range(3):
        mark = marks_ref[index]
        edge = mark - first + HALF
        past = place >= mark
        lowest = jnp.where(past, jnp.maximum(lowest, edge), lowest)
        highest = jnp.where(past, highest, jnp.minimum(highest, edge - 1))
    return jnp.where((key >= lowest) & (key <= highest), 0.0, -1e30).astype(F32)


def stacked(pair):
    low = lane_ids(pair.shape) < HEAD_DIM
    zero = jnp.zeros_like(pair)
    return jnp.concatenate([jnp.where(low, pair, zero), jnp.where(low, zero, pair)], axis=0)


def unstacked(both):
    low = lane_ids((BLOCK, LANES)) < HEAD_DIM
    return jnp.where(low, both[:BLOCK], both[BLOCK:])


def span_of(qkv_ref, lower_ref, upper_ref, half, block, part, sub):
    count = qkv_ref.shape[1]
    first = block * BLOCK - HALF
    lanes = slice(part * GROUP + sub * LANES, part * GROUP + (sub + 1) * LANES)
    halo_lanes = slice((part - 1) * GROUP + sub * LANES, (part - 1) * GROUP + (sub + 1) * LANES)
    own = qkv_ref[half, max(first, 0) : min(first + SPAN, count), lanes]
    if first < 0:
        own = jnp.concatenate([lower_ref[half, :, halo_lanes], own], axis=0)
    if first + SPAN > count:
        own = jnp.concatenate([own, upper_ref[half, :, halo_lanes]], axis=0)
    return own


def many_attend(operands):
    scores = [dot(keys, query, 1, 1) + bias for query, keys, _, bias in operands]
    peaks = [jnp.max(score, axis=0, keepdims=True) for score in scores]
    expos = [jnp.exp(score - peak) for score, peak in zip(scores, peaks)]
    totals = [jnp.sum(expo, axis=0, keepdims=True) for expo in expos]
    weights = [(expo * (1.0 / total)).astype(BF) for expo, total in zip(expos, totals)]
    mixed = [unstacked(dot(weight, item[2], 0, 0)) for weight, item in zip(weights, operands)]
    return [(mix, peak + jnp.log(total)) for mix, peak, total in zip(mixed, peaks, totals)]


def attend_blocks(marks_ref, qkv_ref, lower_ref, upper_ref, blocks, store):
    for block in blocks:
        bias = window_bias(marks_ref, block)
        mine = slice(block * BLOCK, (block + 1) * BLOCK)
        for first in range(0, PAIRS, PAIRS_TOGETHER):
            pairs = range(first, first + PAIRS_TOGETHER)
            items = []
            for pair in pairs:
                half, sub = divmod(pair, GROUP_PAIRS)
                where = (qkv_ref, lower_ref, upper_ref, half, block)
                items.append(
                    (
                        stacked(qkv_ref[half, mine, sub * LANES : (sub + 1) * LANES] * BF(0.125)),
                        span_of(*where, 1, sub),
                        span_of(*where, 2, sub),
                        bias,
                    )
                )
            for pair, (mix, logs) in zip(pairs, many_attend(items)):
                store(block, pair, mix.astype(BF), logs)


def attend_inner_kernel(marks_ref, qkv_ref, out_ref, log_ref):
    def store(block, pair, mix, logs):
        half, sub = divmod(pair, GROUP_PAIRS)
        out_ref[block * BLOCK : (block + 1) * BLOCK, pair * LANES : (pair + 1) * LANES] = mix
        log_ref[block, half, sub : sub + 1, :] = logs

    blocks = range(1, qkv_ref.shape[1] // BLOCK - 1)
    attend_blocks(marks_ref, qkv_ref, None, None, blocks, store)


def attend_inner(marks, qkv):
    count = qkv.shape[1]
    return pl.pallas_call(
        attend_inner_kernel,
        in_specs=[SMEM, VMEM],
        out_specs=[VMEM, VMEM],
        out_shape=[
            jax.ShapeDtypeStruct((count, D), BF),
            jax.ShapeDtypeStruct((count // BLOCK, 2, 8, 2 * BLOCK), F32),
        ],
        compiler_params=params(8),
        cost_estimate=SMALL,
        name="attend_inner",
    )(marks, qkv)


def attend_edges_kernel(marks_ref, qkv_ref, lower_ref, upper_ref, _, out_ref, log_ref, edge_ref, sems):
    count = qkv_ref.shape[1]
    last = count // BLOCK - 1

    def store(block, pair, mix, logs):
        half, sub = divmod(pair, GROUP_PAIRS)
        side = min(block, 1)
        edge_ref[side, :, pair * LANES : (pair + 1) * LANES] = mix
        log_ref[side, half, sub : sub + 1, :] = logs

    attend_blocks(marks_ref, qkv_ref, lower_ref, upper_ref, (0, last), store)
    copies = [
        pltpu.make_async_copy(
            edge_ref.at[side], out_ref.at[pl.ds(block * BLOCK, BLOCK)], sems.at[side]
        )
        for side, block in enumerate((0, last))
    ]
    for copy in copies:
        copy.start()
    for copy in copies:
        copy.wait()


def attend_edges(marks, qkv, lower, upper, mixed):
    return pl.pallas_call(
        attend_edges_kernel,
        in_specs=[SMEM, VMEM, VMEM, VMEM, ANY],
        out_specs=[ANY, VMEM],
        out_shape=[
            jax.ShapeDtypeStruct(mixed.shape, BF),
            jax.ShapeDtypeStruct((2, 2, 8, 2 * BLOCK), F32),
        ],
        input_output_aliases={4: 0},
        scratch_shapes=[pltpu.VMEM((2, BLOCK, D), BF), pltpu.SemaphoreType.DMA((2,))],
        compiler_params=params(8),
        cost_estimate=SMALL,
        name="attend_edges",
    )(marks, qkv, lower, upper, mixed)


PAIRS_TOGETHER = 1
FF_PARTS = tuple((first, min(256, FF - first)) for first in range(0, FF, 256))


def dense_kernel(
    x_ref,
    mixed_ref,
    cot_ref,
    gains_ref,
    source_ref,
    residual_ref,
    normed_ref,
    both_ref,
    hidden_ref,
    near_ref,
    w_ref,
    sems,
):
    ranges = [(3 * FF, D), (0, 3 * FF)]
    fetch = pltpu.make_async_copy(mixed_ref, near_ref, sems.at[2])
    fetch.start()
    copies = [
        pltpu.make_async_copy(
            source_ref.at[:, pl.ds(first, size)], w_ref.at[:, pl.ds(first, size)], sems.at[index]
        )
        for index, (first, size) in enumerate(ranges)
    ]
    for copy in copies:
        copy.start()
    fetch.wait()
    copies[0].wait()
    count = x_ref.shape[0]
    size = min(512, count)
    blocks = [slice(first, first + size) for first in range(0, count, size)]
    for mine in blocks:
        residual = x_ref[mine, :].astype(F32) + dot(near_ref[mine, :], w_ref[:, 3 * FF :])
        residual_ref[mine, :] = residual
        unit, _ = normalized(residual)
        normed_ref[mine, :] = (unit * gains_ref[8:9, :]).astype(BF)
    copies[1].wait()
    for mine in blocks:
        normed = normed_ref[mine, :]
        cot = cot_ref[mine, :]
        for first, size in FF_PARTS:
            gate_cols = slice(first, first + size)
            up_cols = slice(FF + first, FF + first + size)
            down_cols = slice(2 * FF + first, 2 * FF + first + size)
            gate = dot(normed, w_ref[:, gate_cols])
            up = dot(normed, w_ref[:, up_cols])
            grad_hidden = dot(cot, w_ref[:, down_cols])
            share = 0.5 + 0.5 * lax.erf(gate * 0.7071067811865476)
            active = gate * share
            slope = share + gate * (jnp.exp(-0.5 * gate * gate) * 0.3989422804014327)
            hidden_ref[mine, gate_cols] = (active * up).astype(BF)
            both_ref[mine, gate_cols] = (grad_hidden * up * slope).astype(BF)
            both_ref[mine, up_cols] = (grad_hidden * active).astype(BF)


def dense(tokens, mixed, cotangent, gains, weights):
    count = tokens.shape[0]
    wide = [(D, F32), (D, BF), (2 * FF, BF), (FF, BF)]
    return pl.pallas_call(
        dense_kernel,
        in_specs=[VMEM, HBM, VMEM, VMEM, HBM],
        out_specs=[VMEM] * 4,
        out_shape=[jax.ShapeDtypeStruct((count, width), kind) for width, kind in wide],
        scratch_shapes=[
            pltpu.VMEM((count, D), BF),
            pltpu.VMEM(weights.shape, BF),
            pltpu.SemaphoreType.DMA((3,)),
        ],
        compiler_params=params(16),
        cost_estimate=SMALL,
        name="dense",
    )(tokens, mixed, cotangent, gains, weights)


def dense_back_kernel(residual_ref, cot_ref, both_ref, gains_ref, w_ref, *rest):
    low_ref, mixed_grad_ref, grad_ref = rest[-3:]
    unit, scale = normalized(residual_ref[...])
    grad_normed = dot(both_ref[...], w_ref[:, : 2 * FF], 1, 1)
    grad = cot_ref[...].astype(F32) + norm_back(grad_normed, unit, scale, gains_ref[8:9, :])
    grad_ref[...] = grad
    low = grad.astype(BF)
    low_ref[...] = low
    mixed_grad_ref[...] = dot(low, w_ref[:, 3 * FF :], 1, 1).astype(BF)


def dense_back(residual, cotangent, both, gains, weights, after):
    count = residual.shape[0]
    size = min(512, count)
    wide = [(D, BF), (D, BF), (D, F32)]
    return pl.pallas_call(
        dense_back_kernel,
        grid=(count // size,),
        in_specs=[
            rows((size, D)),
            rows((size, D)),
            rows((size, 2 * FF)),
            whole((16, D)),
            whole(weights.shape),
            *[ANY for _ in after],
        ],
        out_specs=[rows((size, width)) for width, _ in wide],
        out_shape=[jax.ShapeDtypeStruct((count, width), kind) for width, kind in wide],
        compiler_params=params(20),
        cost_estimate=SMALL,
        name="dense_back",
    )(residual, cotangent, both, gains, weights, *after)


def result_kernel(residual_ref, hidden_ref, w_ref, *rest):
    product = dot(hidden_ref[...], w_ref[:, 2 * FF : 3 * FF], 1, 1)
    rest[-1][...] = (residual_ref[...] + product).astype(BF)


def result_of(residual, hidden, weights, after):
    count = residual.shape[0]
    size = min(512, count)
    return pl.pallas_call(
        result_kernel,
        grid=(count // size,),
        in_specs=[rows((size, D)), rows((size, FF)), whole(weights.shape), *[ANY for _ in after]],
        out_specs=rows((size, D)),
        out_shape=jax.ShapeDtypeStruct((count, D), BF),
        compiler_params=params(16),
        cost_estimate=SMALL,
        name="result",
    )(residual, hidden, weights, *after)


def pair_back(query, keys, values, out_grad, logs, bias):
    scores = dot(keys, query, 1, 1) + bias
    weights = jnp.exp(scores - logs)
    weight_grad = dot(values, out_grad, 1, 1)
    score_grad = weights * (weight_grad - jnp.sum(weights * weight_grad, axis=0, keepdims=True))
    score_grad = score_grad.astype(BF)
    key_grad = dot(score_grad, query)
    value_grad = dot(weights.astype(BF), out_grad)
    query_grad = unstacked(dot(score_grad, keys, 0, 0)) * 0.125
    return query_grad, key_grad, value_grad


def many_back(operands):
    scores = [dot(keys, query, 1, 1) for query, keys, _, _, _, _ in operands]
    weight_grads = [dot(values, out_grad, 1, 1) for _, _, values, out_grad, _, _ in operands]
    weights = [jnp.exp(score + item[5] - item[4]) for score, item in zip(scores, operands)]
    value_grads = [dot(weight.astype(BF), item[3]) for weight, item in zip(weights, operands)]
    score_grads = [
        (weight * (grad - jnp.sum(weight * grad, axis=0, keepdims=True))).astype(BF)
        for weight, grad in zip(weights, weight_grads)
    ]
    key_grads = [dot(grad, item[0]) for grad, item in zip(score_grads, operands)]
    query_grads = [
        unstacked(dot(grad, item[1], 0, 0)) * 0.125 for grad, item in zip(score_grads, operands)
    ]
    return list(zip(query_grads, key_grads, value_grads))


def turned_back(values, cosine, sine):
    return values * cosine - swap_halves(values) * sine


def edge_back_kernel(
    marks_ref,
    mixed_grad_ref,
    log_ref,
    cos_ref,
    sin_ref,
    qkv_ref,
    lower_ref,
    upper_ref,
    grad_ref,
    sum_ref,
    away_ref,
):
    count = qkv_ref.shape[1]
    for side, block in enumerate((0, count // BLOCK - 1)):
        bias = window_bias(marks_ref, block)
        mine = slice(block * BLOCK, (block + 1) * BLOCK)
        sent = slice(0, HALF) if side == 0 else slice(SPAN - HALF, SPAN)
        for half in range(2):
            items = []
            for sub in range(GROUP_PAIRS):
                pair = half * GROUP_PAIRS + sub
                where = (qkv_ref, lower_ref, upper_ref, half, block)
                items.append(
                    (
                        stacked(qkv_ref[half, mine, sub * LANES : (sub + 1) * LANES] * BF(0.125)),
                        span_of(*where, 1, sub),
                        span_of(*where, 2, sub),
                        stacked(mixed_grad_ref[mine, pair * LANES : (pair + 1) * LANES]),
                        log_ref[side, half, sub : sub + 1, :],
                        bias,
                    )
                )
            for sub, (query_grad, key_grad, value_grad) in enumerate(many_back(items)):
                lanes = slice(sub * LANES, (sub + 1) * LANES)
                value_lanes = slice(GROUP + sub * LANES, GROUP + (sub + 1) * LANES)
                grad_ref[half, side, :, lanes] = turned_back(
                    query_grad, cos_ref[mine, :], sin_ref[mine, :]
                ).astype(BF)
                sum_ref[half, side, :, lanes] = key_grad
                sum_ref[half, side, :, value_lanes] = value_grad
                away_ref[side, half, :, lanes] = key_grad[sent].astype(BF)
                away_ref[side, half, :, value_lanes] = value_grad[sent].astype(BF)


def edge_back(marks, qkv, mixed_grad, logs, cosine, sine, lower, upper):
    return pl.pallas_call(
        edge_back_kernel,
        in_specs=[SMEM, *[VMEM] * 7],
        out_specs=[VMEM, VMEM, VMEM],
        out_shape=[
            jax.ShapeDtypeStruct((2, 2, BLOCK, GROUP), BF),
            jax.ShapeDtypeStruct((2, 2, SPAN, 2 * GROUP), F32),
            jax.ShapeDtypeStruct((2, 2, HALF, 2 * GROUP), BF),
        ],
        compiler_params=params(8),
        cost_estimate=SMALL,
        name="edge_back",
    )(marks, mixed_grad, logs, cosine, sine, qkv, lower, upper)


TOGETHER = 1


def inner_back_kernel(
    group_ref,
    marks_ref,
    mixed_grad_ref,
    log_ref,
    cos_ref,
    sin_ref,
    edge_grad_ref,
    edge_sum_ref,
    qkv_ref,
    *rest,
):
    grad_ref, sum_ref = rest[-2:]
    count = qkv_ref.shape[1]
    inner = count // BLOCK - 2
    sum_ref[0 : SPAN - HALF, :] = edge_sum_ref[0, 0, HALF:, :]
    grad_ref[0:BLOCK, 0:GROUP] = edge_grad_ref[0, 0]
    grad_ref[count - BLOCK :, 0:GROUP] = edge_grad_ref[0, 1]

    def finish(place):
        own_cosine = cos_ref[place, :]
        own_sine = sin_ref[place, :]
        for sub in range(GROUP_PAIRS):
            lanes = slice(sub * LANES, (sub + 1) * LANES)
            key_lanes = slice(GROUP + sub * LANES, GROUP + (sub + 1) * LANES)
            grad_ref[place, key_lanes] = turned_back(
                sum_ref[place, lanes], own_cosine, own_sine
            ).astype(BF)
        grad_ref[place, 2 * GROUP :] = sum_ref[place, GROUP:].astype(BF)

    for first in range(1, inner + 1, TOGETHER):
        blocks = range(first, min(first + TOGETHER, inner + 1))
        places = []
        items = []
        for block in blocks:
            bias = window_bias(marks_ref, block)
            start = block * BLOCK - HALF
            window = slice(start, start + SPAN)
            mine = slice(block * BLOCK, (block + 1) * BLOCK)
            for sub in range(GROUP_PAIRS):
                lanes = slice(sub * LANES, (sub + 1) * LANES)
                places.append((mine, start, sub))
                items.append(
                    (
                        stacked(qkv_ref[0, mine, lanes] * BF(0.125)),
                        qkv_ref[0, window, GROUP + sub * LANES : GROUP + (sub + 1) * LANES],
                        qkv_ref[0, window, 2 * GROUP + sub * LANES : 2 * GROUP + (sub + 1) * LANES],
                        stacked(mixed_grad_ref[mine, lanes]),
                        log_ref[block, 0, sub : sub + 1, :],
                        bias,
                    )
                )
        for (mine, start, sub), (query_grad, key_grad, value_grad) in zip(places, many_back(items)):
            lanes = slice(sub * LANES, (sub + 1) * LANES)
            value_lanes = slice(GROUP + sub * LANES, GROUP + (sub + 1) * LANES)
            older = slice(start, start + BLOCK)
            newer = slice(start + BLOCK, start + SPAN)
            sum_ref[older, lanes] += key_grad[:BLOCK]
            sum_ref[newer, lanes] = key_grad[BLOCK:]
            sum_ref[older, value_lanes] += value_grad[:BLOCK]
            sum_ref[newer, value_lanes] = value_grad[BLOCK:]
            grad_ref[mine, lanes] = turned_back(query_grad, cos_ref[mine, :], sin_ref[mine, :]).astype(BF)
        finish(slice(blocks[0] * BLOCK - HALF, (blocks[-1] + 1) * BLOCK - HALF))

    tail = SPAN - HALF
    sum_ref[count - tail : count - HALF, :] += edge_sum_ref[0, 1, 0:BLOCK, :]
    finish(slice(count - tail, count - HALF))


def inner_back(group, marks, qkv, mixed_grad, logs, cosine, sine, edge_grad, edge_sum, after):
    count = qkv.shape[1]
    return pl.pallas_call(
        inner_back_kernel,
        grid_spec=pltpu.PrefetchScalarGridSpec(
            num_scalar_prefetch=1,
            grid=(1,),
            in_specs=[
                SMEM,
                pl.BlockSpec((count, GROUP), lambda i, g: (0, g[0])),
                pl.BlockSpec((count // BLOCK, 1, 8, 2 * BLOCK), lambda i, g: (0, g[0], 0, 0)),
                pl.BlockSpec((count, LANES), lambda i, g: (0, 0)),
                pl.BlockSpec((count, LANES), lambda i, g: (0, 0)),
                pl.BlockSpec((1, 2, BLOCK, GROUP), lambda i, g: (g[0], 0, 0, 0)),
                pl.BlockSpec((1, 2, SPAN, 2 * GROUP), lambda i, g: (g[0], 0, 0, 0)),
                pl.BlockSpec((1, count, QKV_HALF), lambda i, g: (g[0], 0, 0)),
                *[ANY for _ in after],
            ],
            out_specs=pl.BlockSpec((count, QKV_HALF), lambda i, g: (0, 0)),
            scratch_shapes=[
                pltpu.VMEM((count, 2 * GROUP), F32),
            ],
        ),
        out_shape=jax.ShapeDtypeStruct((count, QKV_HALF), BF),
        compiler_params=params(8),
        cost_estimate=SMALL,
        name="inner_back",
    )(
        jnp.reshape(group, (1,)).astype(jnp.int32),
        marks,
        mixed_grad,
        logs,
        cosine,
        sine,
        edge_grad,
        edge_sum,
        qkv,
        *after,
    )


def patch_kernel(
    group_ref, cos_ref, sin_ref, edge_sum_ref, lower_ref, upper_ref, _, out_ref, edge_ref, sems
):
    group = group_ref[0]
    count = out_ref.shape[0]
    copies = []
    for side, (place, own, halo_ref) in enumerate(
        ((0, HALF, lower_ref), (count - HALF, BLOCK, upper_ref))
    ):
        total = edge_sum_ref[group, side, own : own + HALF, :] + halo_ref[group].astype(F32)
        cosine = cos_ref[place : place + HALF, :]
        sine = sin_ref[place : place + HALF, :]
        for sub in range(GROUP_PAIRS):
            lanes = slice(sub * LANES, (sub + 1) * LANES)
            edge_ref[side, :, lanes] = turned_back(total[:, lanes], cosine, sine).astype(BF)
        edge_ref[side, :, GROUP:] = total[:, GROUP:].astype(BF)
        copies.append(
            pltpu.make_async_copy(
                edge_ref.at[side],
                out_ref.at[pl.ds(place, HALF), pl.ds(GROUP, 2 * GROUP)],
                sems.at[side],
            )
        )
    for copy in copies:
        copy.start()
    for copy in copies:
        copy.wait()


def patch(group, cosine, sine, edge_sum, from_lower, from_upper, grads):
    return pl.pallas_call(
        patch_kernel,
        in_specs=[SMEM, *[VMEM] * 5, ANY],
        out_specs=ANY,
        out_shape=jax.ShapeDtypeStruct(grads.shape, BF),
        input_output_aliases={6: 0},
        scratch_shapes=[pltpu.VMEM((2, HALF, 2 * GROUP), BF), pltpu.SemaphoreType.DMA((2,))],
        compiler_params=params(8),
        cost_estimate=SMALL,
        name="patch",
    )(
        jnp.reshape(group, (1,)).astype(jnp.int32),
        cosine,
        sine,
        edge_sum,
        from_lower,
        from_upper,
        grads,
    )


def input_grad_kernel(count, order_ref, x_ref, gains_ref, first_ref, second_ref, grad_ref, *refs):
    weight_refs = refs[:count]
    out_ref, w_ref, sems = refs[count:]

    @pl.when(pl.program_id(0) == 0)
    def _():
        load_weights(weight_refs, w_ref, sems)

    unit, scale = normalized(x_ref[...].astype(F32))
    half = order_ref[0]
    grad_normed = dot(first_ref[...], w_ref[half, :, :QKV_HALF], 1, 1) + dot(
        second_ref[...], w_ref[1 - half, :, :QKV_HALF], 1, 1
    )
    out_ref[...] = grad_ref[...] + norm_back(grad_normed, unit, scale, gains_ref[0:1, :])


def input_grad(half, tokens, gains, weights, first, second, grad):
    count = tokens.shape[0]
    size = min(256, count)
    operands = weights.operands()
    return pl.pallas_call(
        partial(input_grad_kernel, len(operands)),
        grid=(count // size,),
        in_specs=[
            SMEM,
            rows((size, D)),
            whole((16, D)),
            rows((size, QKV_HALF)),
            rows((size, QKV_HALF)),
            rows((size, D)),
            *weights.specs(),
        ],
        out_specs=rows((size, D)),
        out_shape=jax.ShapeDtypeStruct((count, D), F32),
        scratch_shapes=weights.scratch(),
        compiler_params=params(12),
        cost_estimate=SMALL,
        name="input_grad",
    )(jnp.reshape(half, (1,)).astype(jnp.int32), tokens, gains, first, second, grad, *operands)


TILE = 256


def store_slots(slots_ref, out_ref, product):
    step = CHIP_ROWS
    for index in range(D // step):
        place = pl.multiple_of(slots_ref[1 + index] * step, 16)
        out_ref[pl.ds(place, step), :] = product[index * step : (index + 1) * step].astype(BF)


def weight_products(slots_ref, out_ref, turned, grad_ref, first, size):
    for tile in range(0, size, TILE):
        width = min(TILE, size - tile)
        product = dot(turned, grad_ref[:, tile : tile + width])
        for index in range(D // CHIP_ROWS):
            place = pl.multiple_of(slots_ref[1 + index] * CHIP_ROWS, 16)
            out_ref[pl.ds(place, CHIP_ROWS), first + tile : first + tile + width] = product[
                index * CHIP_ROWS : (index + 1) * CHIP_ROWS
            ].astype(BF)


def mixed_weight_kernel(slots_ref, normed_ref, grad_ref, mixed_ref, low_ref, *rest):
    out_ref = rest[-1]
    weight_products(slots_ref, out_ref, normed_ref[...].T, grad_ref, 0, QKV_HALF)
    lanes = pl.ds(pl.multiple_of(slots_ref[0] * GROUP, LANES), GROUP)
    weight_products(slots_ref, out_ref, mixed_ref[...].T, low_ref.at[:, lanes], QKV_HALF, GROUP)


def mixed_weight_grad(slots, normed, dqkv, mixed, low, after=()):
    count = normed.shape[0]
    return pl.pallas_call(
        mixed_weight_kernel,
        in_specs=[SMEM, *[VMEM] * 4, *[ANY for _ in after]],
        out_specs=VMEM,
        out_shape=jax.ShapeDtypeStruct((D, MIXED_HALF), BF),
        compiler_params=params(8),
        cost_estimate=SMALL,
        name="mixed_weight_grad",
    )(slots, normed, dqkv, mixed, low, *after)


def ff_weight_kernel(slots_ref, normed_ref, cot_ref, both_ref, hidden_ref, *rest):
    out_ref = rest[-1]

    @pl.when(slots_ref[0] == 0)
    def _():
        left = both_ref.at[:, 0:FF_HALF]
        weight_products(slots_ref, out_ref, normed_ref[...].T, left, 0, FF_HALF)

    @pl.when(slots_ref[0] == 1)
    def _():
        left = both_ref.at[:, FF_HALF : 2 * FF]
        weight_products(slots_ref, out_ref, normed_ref[...].T, left, 0, FF_LEFT)
        weight_products(slots_ref, out_ref, cot_ref[...].T, hidden_ref, FF_LEFT, FF)
        out_ref[:, FF_LEFT + FF :] = jnp.zeros((D, FF_HALF - FF_LEFT - FF), BF)


def ff_weight_grad(slots, normed, cot, both, hidden, after):
    count = normed.shape[0]
    return pl.pallas_call(
        ff_weight_kernel,
        in_specs=[SMEM, *[VMEM] * 4, *[ANY for _ in after]],
        out_specs=VMEM,
        out_shape=jax.ShapeDtypeStruct((D, FF_HALF), BF),
        compiler_params=params(8),
        cost_estimate=SMALL,
        name="ff_weight_grad",
    )(slots, normed, cot, both, hidden, *after)


def join_kernel(*refs):
    out_ref = refs[-1]
    first = 0
    for ref in refs[:-1]:
        out_ref[first : first + ref.shape[0], :] = ref[...]
        first += ref.shape[0]


def join(*parts):
    count = sum(part.shape[0] for part in parts)
    width = parts[0].shape[1]
    return pl.pallas_call(
        join_kernel,
        in_specs=[VMEM for _ in parts],
        out_specs=VMEM,
        out_shape=jax.ShapeDtypeStruct((count, width), parts[0].dtype),
        compiler_params=params(8),
        cost_estimate=SMALL,
        name="join",
    )(*parts)


def doc_marks(doc_lengths, row_count):
    me = lax.axis_index("tok")
    ends = jnp.cumsum(doc_lengths).astype(jnp.int32)
    before = jnp.where(me > 0, ends[jnp.maximum(me - 1, 0)], 0)
    return jnp.stack([before, ends[me], ends[me + 1], me * row_count]).astype(jnp.int32)


def rotary_tables(marks, row_count):
    place = marks[3] + jnp.arange(row_count, dtype=jnp.int32)
    offset = place - jnp.where(place >= marks[1], marks[1], marks[0])
    frequency = 10000.0 ** (-jnp.arange(0, HEAD_DIM, 2, dtype=F32) / HEAD_DIM)
    angles = offset.astype(F32)[:, None] * frequency[None, :]
    cosine = jnp.cos(angles)
    sine = jnp.sin(angles)
    return (
        jnp.concatenate([cosine] * 4, axis=1),
        jnp.concatenate([-sine, sine, -sine, sine], axis=1),
    )


def passed_along(value, steps):
    count = lax.axis_size("tok")
    first, last = (max(0, -steps), min(count, count - steps))
    return lax.ppermute(value, "tok", [(at, at + steps) for at in range(first, last)])


STAGED_DEVICES = 32


def staged():
    return lax.axis_size("tok") == STAGED_DEVICES


def exchange(value, by_core):
    pairs = [(at, at ^ by_core[at & 1]) for at in range(lax.axis_size("tok"))]
    return lax.ppermute(value, "tok", pairs)


CORE = (1, 1)
DEEP = tuple((step << 3, step << 3) for step in range(4))
NEAR = (2, 4)
FAR = (4, 2)


def slot_codes(core):
    slot = jnp.arange(16, dtype=jnp.int32)
    depth, near, far = (slot & 3, (slot >> 2) & 1, slot >> 3)
    return (depth << 2) | jnp.where(core == 0, (far << 1) | near, (near << 1) | far)


def chip_slots(chip, core):
    code = jnp.arange(16, dtype=jnp.int32) ^ chip
    depth, second, first = (code >> 2, (code >> 1) & 1, code & 1)
    return depth | jnp.where(core == 0, (second << 3) | (first << 2), (first << 3) | (second << 2))


def stage_after(value, *others):
    return lax.optimization_barrier((value, *others))[0]


def in_hbm(value):
    return pltpu.with_memory_space_constraint(value, pltpu.HBM)


def core_pieces(shard):
    core = lax.axis_index("tok") & 1
    half = shard.shape[1] // 2
    keep = jnp.where(core == 0, shard[:, :half], shard[:, half:])
    send = jnp.where(core == 0, shard[:, half:], shard[:, :half])
    came = exchange(send, CORE)
    return jnp.concatenate(
        [jnp.where(core == 0, keep, came), jnp.where(core == 0, came, keep)], axis=0
    )


def final_gather(held, far):
    me = lax.axis_index("tok")
    core = me & 1
    chip = me >> 1
    places = jnp.concatenate(
        [slot_codes(core) ^ chip, slot_codes(1 - core) ^ chip, jnp.full((1,), core, jnp.int32)]
    )
    return Weights([held, far, exchange(held, CORE), exchange(far, CORE)], places)


def whole_weights(shard):
    full = lax.all_gather(shard, "tok", axis=0, tiled=True)
    half = full.shape[1] // 2
    return Weights([jnp.stack([full[:, :half], full[:, half:]])])


def added(left, right):
    return (left.astype(F32) + right.astype(F32)).astype(BF)


def core_sum(keep, came):
    return added(keep[:384], came[:384]), added(keep[384:], came[384:])


def far_sum(near, came):
    return added(near[:192], came[:192]), added(near[192:], came[192:])


def near_sum(near, came):
    return [
        added(near[first : first + CHIP_ROWS], came[first : first + CHIP_ROWS])
        for first in range(0, 192, CHIP_ROWS)
    ]


def deep_sum(parts, *after):
    core = lax.axis_index("tok") & 1
    total = parts[0].astype(F32)
    for step in (1, 2, 3):
        total = total + stage_after(exchange(parts[step], DEEP[step]), after[step - 1]).astype(F32)
    share = CHIP_ROWS // 2
    lower, upper = (total[:share], total[share:])
    own = jnp.where(core == 0, lower, upper)
    came = exchange(jnp.where(core == 0, upper, lower), CORE)
    return jnp.concatenate(
        [jnp.where(core == 0, own, came), jnp.where(core == 0, came, own)], axis=1
    )


def summed(keep, send):
    full = jnp.concatenate([keep, send], axis=1)
    return lax.psum_scatter(full.astype(F32), "tok", scatter_dimension=0, tiled=True)


def by_part(groups):
    return jnp.concatenate(
        [
            groups[:, half * MIXED_HALF + part * GROUP : half * MIXED_HALF + (part + 1) * GROUP]
            for part in range(3)
            for half in range(2)
        ],
        axis=1,
    )


def on_device(
    tokens,
    doc_lengths,
    first_gain,
    qkv_weight,
    attn_weight,
    second_gain,
    feed_in_weight,
    feed_out_weight,
    cotangent,
):
    row_count = tokens.shape[0]
    share = first_gain.shape[0]

    def spread(gain):
        return jnp.broadcast_to(gain[:, None], (share, LANES))

    def group_of(half):
        return [
            qkv_weight[:, part * D + half * GROUP : part * D + (half + 1) * GROUP]
            for part in range(3)
        ]

    shard_one = jnp.concatenate(
        [*group_of(0), spread(first_gain), *group_of(1), spread(second_gain)], axis=1
    )
    shard_two = jnp.concatenate([feed_in_weight, feed_out_weight.T, attn_weight], axis=1)
    weights_two = lax.all_gather(shard_two, "tok", axis=0, tiled=True)
    if staged():
        piece = core_pieces(shard_one)
        marks = doc_marks(stage_after(doc_lengths, piece), row_count)
        cosine, sine = rotary_tables(marks, row_count)
        came = [exchange(piece, DEEP[step]) for step in (1, 2, 3)]
        *came, marks = lax.optimization_barrier((*came, marks, cosine, sine))[:4]
        one = join(piece, *came)
        one = join(one, exchange(one, NEAR))
        weights_one = final_gather(one, exchange(one, FAR))
    else:
        marks = doc_marks(doc_lengths, row_count)
        cosine, sine = rotary_tables(marks, row_count)
        weights_one = whole_weights(shard_one)
    normed, qkv, gains = project_qkv(tokens, weights_one, in_hbm(cosine), in_hbm(sine))
    lower = passed_along(qkv[:, row_count - HALF :, GROUP:], 1)
    upper = passed_along(qkv[:, :HALF, GROUP:], -1)
    mixed, logs = attend_inner(marks, qkv)
    mixed, edge_logs = attend_edges(marks, qkv, lower, upper, mixed)
    residual, normed_two, both, hidden = dense(tokens, in_hbm(mixed), cotangent, gains, in_hbm(weights_two))
    me = lax.axis_index("tok")
    if staged():
        halves = (1 - (me & 1), me & 1)
    else:
        halves = (jnp.int32(1), jnp.int32(0))

    def order(half):
        if staged():
            slots = chip_slots(me >> 1, half)
        else:
            slots = jnp.arange(D // CHIP_ROWS, dtype=jnp.int32)
        return jnp.concatenate([jnp.reshape(half, (1,)).astype(jnp.int32), slots])

    def ff_grad(half, after):
        return ff_weight_grad(order(half), normed_two, cotangent, both, hidden, after)

    def inner(half, after):
        return inner_back(
            half, marks, qkv, mixed_grad, logs, cosine, sine, edge_grad, edge_sum, after
        )

    def patched(half, grads):
        return patch(half, cosine, sine, edge_sum, from_lower, from_upper, grads)

    def finish(first, second):
        return input_grad(halves[0], tokens, gains, weights_one, first, second, grad)

    send, keep = halves
    def mixed_weight(half, dqkv):
        return mixed_weight_grad(order(half), normed, dqkv, mixed, low)

    ff_send = ff_grad(send, [])
    ff_keep = ff_grad(keep, [ff_send])
    result = result_of(residual, hidden, weights_two, [ff_keep])
    behind = []
    if staged():
        near, far = core_sum(ff_keep, stage_after(exchange(ff_send, CORE), result))
        behind = [far]
    low, mixed_grad, grad = dense_back(residual, cotangent, both, gains, weights_two, behind)
    edge_grad, edge_sum, away = edge_back(marks, qkv, mixed_grad, edge_logs, cosine, sine, lower, upper)
    from_upper = passed_along(away[0], -1)
    from_lower = passed_along(away[1], 1)

    if staged():
        first = inner(send, [])
        from_lower, from_upper, first = lax.optimization_barrier((from_lower, from_upper, first))
        near, far = far_sum(near, stage_after(exchange(far, FAR), from_lower, from_upper))
        first = patched(send, stage_after(first, far))
        mixed_send = mixed_weight(send, first)
        second = inner(keep, [mixed_send])
        parts = near_sum(near, stage_after(exchange(far, NEAR), second))
        second = patched(keep, stage_after(second, *parts))
        mixed_keep = mixed_weight(keep, second)
        mixed_near, mixed_far = core_sum(mixed_keep, exchange(stage_after(mixed_send, second), CORE))
        grad_in = finish(first, stage_after(second, mixed_far))
        mixed_near, mixed_far = far_sum(mixed_near, stage_after(exchange(mixed_far, FAR), grad_in))
        sum_ff = deep_sum(parts, *[mixed_far] * 3)
        mixed_parts = near_sum(mixed_near, exchange(mixed_far, NEAR))
        sum_mixed = deep_sum(mixed_parts, *[mixed_parts[0]] * 3)
    else:
        first = patched(send, inner(send, []))
        second = patched(keep, inner(keep, []))
        grad_in = finish(first, second)
        sum_ff = summed(ff_keep, ff_send)
        sum_mixed = summed(mixed_weight(keep, second), mixed_weight(send, first))
    sum_qkv = by_part(sum_mixed)
    sent_attn = jnp.concatenate(
        [sum_mixed[:, QKV_HALF:MIXED_HALF], sum_mixed[:, MIXED_HALF + QKV_HALF :]], axis=1
    )
    sent_in = jnp.concatenate(
        [sum_ff[:, :FF_HALF], sum_ff[:, FF_HALF : FF_HALF + FF_LEFT]], axis=1
    )
    sent_down = sum_ff[:, FF_HALF + FF_LEFT : FF_HALF + FF_LEFT + FF].T

    def gain_grad(summed, weight, gain):
        return jnp.sum(summed * weight.astype(F32), axis=1) / gain.astype(F32)

    return (
        result,
        grad_in,
        gain_grad(sum_qkv, qkv_weight, first_gain),
        sum_qkv,
        sent_attn,
        gain_grad(sent_in, feed_in_weight, second_gain),
        sent_in,
        sent_down,
    )


def solution(mesh):
    in_specs = (
        P("tok", None),
        P(),
        P("tok"),
        P("tok", None),
        P("tok", None),
        P("tok"),
        P("tok", None),
        P(None, "tok"),
        P("tok", None),
    )
    out_specs = (
        P("tok", None),
        P("tok", None),
        P("tok"),
        P("tok", None),
        P("tok", None),
        P("tok"),
        P("tok", None),
        P(None, "tok"),
    )
    return jax.shard_map(
        on_device, mesh=mesh, in_specs=in_specs, out_specs=out_specs, check_vma=False
    )
```

```python
from functools import partial

import jax
import jax.numpy as jnp
from jax import lax
from jax.experimental import pallas as pl
from jax.experimental.pallas import tpu as pltpu
from jax.sharding import PartitionSpec as P

D = 768
FF = 1152
HEADS = 12
HEAD_DIM = 64
HALF = 64
PAIRS = HEADS // 2
BLOCK = 128
SPAN = BLOCK + 2 * HALF
LANES = 128
QKV_HALF = 3 * D // 2
GROUP = D // 2
GROUP_PAIRS = PAIRS // 2
FF_HALF = 1792
FF_LEFT = 2 * FF - FF_HALF
MIXED_HALF = QKV_HALF + GROUP
MIB = 1024 * 1024
BF = jnp.bfloat16
F32 = jnp.float32


def dot(left, right, left_dim=1, right_dim=0):
    return lax.dot_general(
        left, right, (((left_dim,), (right_dim,)), ((), ())), preferred_element_type=F32
    )


def params(mib):
    return pltpu.CompilerParams(vmem_limit_bytes=mib * MIB)


def whole(shape):
    return pl.BlockSpec(shape, lambda *_: (0,) * len(shape))


def rows(shape):
    return pl.BlockSpec(shape, lambda i: (i,) + (0,) * (len(shape) - 1))


SMALL = pl.CostEstimate(flops=4000000000, bytes_accessed=1000, transcendentals=0)
SMEM = pl.BlockSpec(memory_space=pltpu.SMEM)
ANY = pl.BlockSpec(memory_space=pl.ANY)
VMEM = pl.BlockSpec(memory_space=pltpu.VMEM)
HBM = pl.BlockSpec(memory_space=pltpu.HBM)
HBM = pl.BlockSpec(memory_space=pltpu.HBM)


def lane_ids(shape):
    return lax.broadcasted_iota(jnp.int32, shape, len(shape) - 1)


def swap_halves(values):
    low = (lane_ids(values.shape) & (HEAD_DIM - 1)) < HEAD_DIM // 2
    return jnp.where(
        low, pltpu.roll(values, LANES - HEAD_DIM // 2, 1), pltpu.roll(values, HEAD_DIM // 2, 1)
    )


def normalized(values):
    centered = values - jnp.mean(values, axis=-1, keepdims=True)
    scale = lax.rsqrt(jnp.mean(centered * centered, axis=-1, keepdims=True) + 1e-05)
    return centered * scale, scale


def norm_back(grad, unit, scale, gains):
    grad_unit = grad * gains
    return scale * (
        grad_unit
        - jnp.mean(grad_unit, axis=-1, keepdims=True)
        - unit * jnp.mean(grad_unit * unit, axis=-1, keepdims=True)
    )


CHIP_ROWS = 48


class Weights:
    def __init__(self, arrays, places=None):
        self.arrays = arrays
        self.places = places

    def operands(self):
        if self.places is None:
            return list(self.arrays)
        return [self.places, *self.arrays]

    def specs(self):
        if self.places is None:
            return [ANY]
        return [SMEM, VMEM, VMEM, VMEM, VMEM]

    def scratch(self):
        width = self.arrays[0].shape[-1]
        return [pltpu.VMEM((2, D, width), BF), pltpu.SemaphoreType.DMA((1,))]


def load_weights(refs, out_ref, sems):
    if len(refs) == 1:
        copy = pltpu.make_async_copy(refs[0], out_ref, sems.at[0])
        copy.start()
        copy.wait()
        return
    places_ref = refs[0]
    core = places_ref[32]
    for index, source in enumerate(refs[1:]):
        half = core if index < 2 else 1 - core
        for slot in range(8):
            place = pl.multiple_of(places_ref[index * 8 + slot] * CHIP_ROWS, 16)
            out_ref[half, pl.ds(place, CHIP_ROWS), :] = source[
                slot * CHIP_ROWS : (slot + 1) * CHIP_ROWS, :
            ]


def qkv_kernel(count, x_ref, cos_ref, sin_ref, *refs):
    weight_refs = refs[:count]
    normed_ref, qkv_ref, gains_ref, w_ref, sems = refs[count:]

    @pl.when(pl.program_id(0) == 0)
    def _():
        load_weights(weight_refs, w_ref, sems)
        for half in range(2):
            turned = w_ref[half, :, QKV_HALF:].T.astype(F32)
            gains_ref[half * 8 : half * 8 + 8, :] = turned[:8]

    unit, _ = normalized(x_ref[...].astype(F32))
    normed = (unit * gains_ref[0:1, :]).astype(BF)
    normed_ref[...] = normed
    cosine = cos_ref[...]
    sine = sin_ref[...]
    for half in range(2):
        merged = dot(normed, w_ref[half, :, :QKV_HALF])
        for tile in range(QKV_HALF // LANES):
            lanes = slice(tile * LANES, (tile + 1) * LANES)
            part = merged[:, lanes]
            if tile * LANES < 2 * GROUP:
                part = part * cosine + swap_halves(part) * sine
            qkv_ref[half, :, lanes] = part.astype(BF)


def project_qkv(tokens, weights, cosine, sine):
    count = tokens.shape[0]
    size = min(256, count)
    operands = weights.operands()
    return pl.pallas_call(
        partial(qkv_kernel, len(operands)),
        grid=(count // size,),
        in_specs=[rows((size, D)), rows((size, LANES)), rows((size, LANES)), *weights.specs()],
        out_specs=[
            rows((size, D)),
            pl.BlockSpec((2, size, QKV_HALF), lambda i: (0, i, 0)),
            whole((16, D)),
        ],
        out_shape=[
            jax.ShapeDtypeStruct((count, D), BF),
            jax.ShapeDtypeStruct((2, count, QKV_HALF), BF),
            jax.ShapeDtypeStruct((16, D), F32),
        ],
        scratch_shapes=weights.scratch(),
        compiler_params=params(12),
        cost_estimate=SMALL,
        name="qkv",
    )(tokens, cosine, sine, *operands)


def window_bias(marks_ref, block):
    shape = (SPAN, 2 * BLOCK)
    first = marks_ref[3] + block * BLOCK
    key = lax.broadcasted_iota(jnp.int32, shape, 0)
    query = lax.broadcasted_iota(jnp.int32, (1, 2 * BLOCK), 1) & (BLOCK - 1)
    place = first + query
    lowest = query
    highest = query + 2 * HALF
    for index in range(3):
        mark = marks_ref[index]
        edge = mark - first + HALF
        past = place >= mark
        lowest = jnp.where(past, jnp.maximum(lowest, edge), lowest)
        highest = jnp.where(past, highest, jnp.minimum(highest, edge - 1))
    return jnp.where((key >= lowest) & (key <= highest), 0.0, -1e30).astype(F32)


def stacked(pair):
    low = lane_ids(pair.shape) < HEAD_DIM
    zero = jnp.zeros_like(pair)
    return jnp.concatenate([jnp.where(low, pair, zero), jnp.where(low, zero, pair)], axis=0)


def unstacked(both):
    low = lane_ids((BLOCK, LANES)) < HEAD_DIM
    return jnp.where(low, both[:BLOCK], both[BLOCK:])


def span_of(qkv_ref, lower_ref, upper_ref, half, block, part, sub):
    count = qkv_ref.shape[1]
    first = block * BLOCK - HALF
    lanes = slice(part * GROUP + sub * LANES, part * GROUP + (sub + 1) * LANES)
    halo_lanes = slice((part - 1) * GROUP + sub * LANES, (part - 1) * GROUP + (sub + 1) * LANES)
    own = qkv_ref[half, max(first, 0) : min(first + SPAN, count), lanes]
    if first < 0:
        own = jnp.concatenate([lower_ref[half, :, halo_lanes], own], axis=0)
    if first + SPAN > count:
        own = jnp.concatenate([own, upper_ref[half, :, halo_lanes]], axis=0)
    return own


def many_attend(operands):
    scores = [dot(keys, query, 1, 1) + bias for query, keys, _, bias in operands]
    peaks = [jnp.max(score, axis=0, keepdims=True) for score in scores]
    expos = [jnp.exp(score - peak) for score, peak in zip(scores, peaks)]
    totals = [jnp.sum(expo, axis=0, keepdims=True) for expo in expos]
    weights = [(expo * (1.0 / total)).astype(BF) for expo, total in zip(expos, totals)]
    mixed = [unstacked(dot(weight, item[2], 0, 0)) for weight, item in zip(weights, operands)]
    return [(mix, peak + jnp.log(total)) for mix, peak, total in zip(mixed, peaks, totals)]


def attend_blocks(marks_ref, qkv_ref, lower_ref, upper_ref, blocks, store):
    for block in blocks:
        bias = window_bias(marks_ref, block)
        mine = slice(block * BLOCK, (block + 1) * BLOCK)
        for first in range(0, PAIRS, PAIRS_TOGETHER):
            pairs = range(first, first + PAIRS_TOGETHER)
            items = []
            for pair in pairs:
                half, sub = divmod(pair, GROUP_PAIRS)
                where = (qkv_ref, lower_ref, upper_ref, half, block)
                items.append(
                    (
                        stacked(qkv_ref[half, mine, sub * LANES : (sub + 1) * LANES] * BF(0.125)),
                        span_of(*where, 1, sub),
                        span_of(*where, 2, sub),
                        bias,
                    )
                )
            for pair, (mix, logs) in zip(pairs, many_attend(items)):
                store(block, pair, mix.astype(BF), logs)


def attend_inner_kernel(marks_ref, qkv_ref, out_ref, log_ref):
    def store(block, pair, mix, logs):
        half, sub = divmod(pair, GROUP_PAIRS)
        out_ref[block * BLOCK : (block + 1) * BLOCK, pair * LANES : (pair + 1) * LANES] = mix
        log_ref[block, half, sub : sub + 1, :] = logs

    blocks = range(1, qkv_ref.shape[1] // BLOCK - 1)
    attend_blocks(marks_ref, qkv_ref, None, None, blocks, store)


def attend_inner(marks, qkv):
    count = qkv.shape[1]
    return pl.pallas_call(
        attend_inner_kernel,
        in_specs=[SMEM, VMEM],
        out_specs=[VMEM, VMEM],
        out_shape=[
            jax.ShapeDtypeStruct((count, D), BF),
            jax.ShapeDtypeStruct((count // BLOCK, 2, 8, 2 * BLOCK), F32),
        ],
        compiler_params=params(8),
        cost_estimate=SMALL,
        name="attend_inner",
    )(marks, qkv)


def attend_edges_kernel(marks_ref, qkv_ref, lower_ref, upper_ref, _, out_ref, log_ref, edge_ref, sems):
    count = qkv_ref.shape[1]
    last = count // BLOCK - 1

    def store(block, pair, mix, logs):
        half, sub = divmod(pair, GROUP_PAIRS)
        side = min(block, 1)
        edge_ref[side, :, pair * LANES : (pair + 1) * LANES] = mix
        log_ref[side, half, sub : sub + 1, :] = logs

    attend_blocks(marks_ref, qkv_ref, lower_ref, upper_ref, (0, last), store)
    copies = [
        pltpu.make_async_copy(
            edge_ref.at[side], out_ref.at[pl.ds(block * BLOCK, BLOCK)], sems.at[side]
        )
        for side, block in enumerate((0, last))
    ]
    for copy in copies:
        copy.start()
    for copy in copies:
        copy.wait()


def attend_edges(marks, qkv, lower, upper, mixed):
    return pl.pallas_call(
        attend_edges_kernel,
        in_specs=[SMEM, VMEM, VMEM, VMEM, ANY],
        out_specs=[ANY, VMEM],
        out_shape=[
            jax.ShapeDtypeStruct(mixed.shape, BF),
            jax.ShapeDtypeStruct((2, 2, 8, 2 * BLOCK), F32),
        ],
        input_output_aliases={4: 0},
        scratch_shapes=[pltpu.VMEM((2, BLOCK, D), BF), pltpu.SemaphoreType.DMA((2,))],
        compiler_params=params(8),
        cost_estimate=SMALL,
        name="attend_edges",
    )(marks, qkv, lower, upper, mixed)


PAIRS_TOGETHER = 1
FF_PARTS = tuple((first, min(256, FF - first)) for first in range(0, FF, 256))


def dense_kernel(
    x_ref,
    mixed_ref,
    cot_ref,
    gains_ref,
    source_ref,
    residual_ref,
    normed_ref,
    both_ref,
    hidden_ref,
    near_ref,
    w_ref,
    sems,
):
    ranges = [(3 * FF, D), (0, 3 * FF)]
    fetch = pltpu.make_async_copy(mixed_ref, near_ref, sems.at[2])
    fetch.start()
    copies = [
        pltpu.make_async_copy(
            source_ref.at[:, pl.ds(first, size)], w_ref.at[:, pl.ds(first, size)], sems.at[index]
        )
        for index, (first, size) in enumerate(ranges)
    ]
    for copy in copies:
        copy.start()
    fetch.wait()
    copies[0].wait()
    count = x_ref.shape[0]
    size = min(512, count)
    blocks = [slice(first, first + size) for first in range(0, count, size)]
    for mine in blocks:
        residual = x_ref[mine, :].astype(F32) + dot(near_ref[mine, :], w_ref[:, 3 * FF :])
        residual_ref[mine, :] = residual
        unit, _ = normalized(residual)
        normed_ref[mine, :] = (unit * gains_ref[8:9, :]).astype(BF)
    copies[1].wait()
    for mine in blocks:
        normed = normed_ref[mine, :]
        cot = cot_ref[mine, :]
        for first, size in FF_PARTS:
            gate_cols = slice(first, first + size)
            up_cols = slice(FF + first, FF + first + size)
            down_cols = slice(2 * FF + first, 2 * FF + first + size)
            gate = dot(normed, w_ref[:, gate_cols])
            up = dot(normed, w_ref[:, up_cols])
            grad_hidden = dot(cot, w_ref[:, down_cols])
            share = 0.5 + 0.5 * lax.erf(gate * 0.7071067811865476)
            active = gate * share
            slope = share + gate * (jnp.exp(-0.5 * gate * gate) * 0.3989422804014327)
            hidden_ref[mine, gate_cols] = (active * up).astype(BF)
            both_ref[mine, gate_cols] = (grad_hidden * up * slope).astype(BF)
            both_ref[mine, up_cols] = (grad_hidden * active).astype(BF)


def dense(tokens, mixed, cotangent, gains, weights):
    count = tokens.shape[0]
    wide = [(D, F32), (D, BF), (2 * FF, BF), (FF, BF)]
    return pl.pallas_call(
        dense_kernel,
        in_specs=[VMEM, HBM, VMEM, VMEM, HBM],
        out_specs=[VMEM] * 4,
        out_shape=[jax.ShapeDtypeStruct((count, width), kind) for width, kind in wide],
        scratch_shapes=[
            pltpu.VMEM((count, D), BF),
            pltpu.VMEM(weights.shape, BF),
            pltpu.SemaphoreType.DMA((3,)),
        ],
        compiler_params=params(16),
        cost_estimate=SMALL,
        name="dense",
    )(tokens, mixed, cotangent, gains, weights)


def dense_back_kernel(residual_ref, cot_ref, both_ref, gains_ref, w_ref, *rest):
    low_ref, mixed_grad_ref, grad_ref = rest[-3:]
    unit, scale = normalized(residual_ref[...])
    grad_normed = dot(both_ref[...], w_ref[:, : 2 * FF], 1, 1)
    grad = cot_ref[...].astype(F32) + norm_back(grad_normed, unit, scale, gains_ref[8:9, :])
    grad_ref[...] = grad
    low = grad.astype(BF)
    low_ref[...] = low
    mixed_grad_ref[...] = dot(low, w_ref[:, 3 * FF :], 1, 1).astype(BF)


def dense_back(residual, cotangent, both, gains, weights, after):
    count = residual.shape[0]
    size = min(512, count)
    wide = [(D, BF), (D, BF), (D, F32)]
    return pl.pallas_call(
        dense_back_kernel,
        grid=(count // size,),
        in_specs=[
            rows((size, D)),
            rows((size, D)),
            rows((size, 2 * FF)),
            whole((16, D)),
            whole(weights.shape),
            *[ANY for _ in after],
        ],
        out_specs=[rows((size, width)) for width, _ in wide],
        out_shape=[jax.ShapeDtypeStruct((count, width), kind) for width, kind in wide],
        compiler_params=params(20),
        cost_estimate=SMALL,
        name="dense_back",
    )(residual, cotangent, both, gains, weights, *after)


def result_kernel(residual_ref, hidden_ref, w_ref, *rest):
    product = dot(hidden_ref[...], w_ref[:, 2 * FF : 3 * FF], 1, 1)
    rest[-1][...] = (residual_ref[...] + product).astype(BF)


def result_of(residual, hidden, weights, after):
    count = residual.shape[0]
    size = min(512, count)
    return pl.pallas_call(
        result_kernel,
        grid=(count // size,),
        in_specs=[rows((size, D)), rows((size, FF)), whole(weights.shape), *[ANY for _ in after]],
        out_specs=rows((size, D)),
        out_shape=jax.ShapeDtypeStruct((count, D), BF),
        compiler_params=params(16),
        cost_estimate=SMALL,
        name="result",
    )(residual, hidden, weights, *after)


def pair_back(query, keys, values, out_grad, logs, bias):
    scores = dot(keys, query, 1, 1) + bias
    weights = jnp.exp(scores - logs)
    weight_grad = dot(values, out_grad, 1, 1)
    score_grad = weights * (weight_grad - jnp.sum(weights * weight_grad, axis=0, keepdims=True))
    score_grad = score_grad.astype(BF)
    key_grad = dot(score_grad, query)
    value_grad = dot(weights.astype(BF), out_grad)
    query_grad = unstacked(dot(score_grad, keys, 0, 0)) * 0.125
    return query_grad, key_grad, value_grad


def many_back(operands):
    scores = [dot(keys, query, 1, 1) for query, keys, _, _, _, _ in operands]
    weight_grads = [dot(values, out_grad, 1, 1) for _, _, values, out_grad, _, _ in operands]
    weights = [jnp.exp(score + item[5] - item[4]) for score, item in zip(scores, operands)]
    value_grads = [dot(weight.astype(BF), item[3]) for weight, item in zip(weights, operands)]
    score_grads = [
        (weight * (grad - jnp.sum(weight * grad, axis=0, keepdims=True))).astype(BF)
        for weight, grad in zip(weights, weight_grads)
    ]
    key_grads = [dot(grad, item[0]) for grad, item in zip(score_grads, operands)]
    query_grads = [
        unstacked(dot(grad, item[1], 0, 0)) * 0.125 for grad, item in zip(score_grads, operands)
    ]
    return list(zip(query_grads, key_grads, value_grads))


def turned_back(values, cosine, sine):
    return values * cosine - swap_halves(values) * sine


def edge_back_kernel(
    marks_ref,
    mixed_grad_ref,
    log_ref,
    cos_ref,
    sin_ref,
    qkv_ref,
    lower_ref,
    upper_ref,
    grad_ref,
    sum_ref,
    away_ref,
):
    count = qkv_ref.shape[1]
    for side, block in enumerate((0, count // BLOCK - 1)):
        bias = window_bias(marks_ref, block)
        mine = slice(block * BLOCK, (block + 1) * BLOCK)
        sent = slice(0, HALF) if side == 0 else slice(SPAN - HALF, SPAN)
        for half in range(2):
            items = []
            for sub in range(GROUP_PAIRS):
                pair = half * GROUP_PAIRS + sub
                where = (qkv_ref, lower_ref, upper_ref, half, block)
                items.append(
                    (
                        stacked(qkv_ref[half, mine, sub * LANES : (sub + 1) * LANES] * BF(0.125)),
                        span_of(*where, 1, sub),
                        span_of(*where, 2, sub),
                        stacked(mixed_grad_ref[mine, pair * LANES : (pair + 1) * LANES]),
                        log_ref[side, half, sub : sub + 1, :],
                        bias,
                    )
                )
            for sub, (query_grad, key_grad, value_grad) in enumerate(many_back(items)):
                lanes = slice(sub * LANES, (sub + 1) * LANES)
                value_lanes = slice(GROUP + sub * LANES, GROUP + (sub + 1) * LANES)
                grad_ref[half, side, :, lanes] = turned_back(
                    query_grad, cos_ref[mine, :], sin_ref[mine, :]
                ).astype(BF)
                sum_ref[half, side, :, lanes] = key_grad
                sum_ref[half, side, :, value_lanes] = value_grad
                away_ref[side, half, :, lanes] = key_grad[sent].astype(BF)
                away_ref[side, half, :, value_lanes] = value_grad[sent].astype(BF)


def edge_back(marks, qkv, mixed_grad, logs, cosine, sine, lower, upper):
    return pl.pallas_call(
        edge_back_kernel,
        in_specs=[SMEM, *[VMEM] * 7],
        out_specs=[VMEM, VMEM, VMEM],
        out_shape=[
            jax.ShapeDtypeStruct((2, 2, BLOCK, GROUP), BF),
            jax.ShapeDtypeStruct((2, 2, SPAN, 2 * GROUP), F32),
            jax.ShapeDtypeStruct((2, 2, HALF, 2 * GROUP), BF),
        ],
        compiler_params=params(8),
        cost_estimate=SMALL,
        name="edge_back",
    )(marks, mixed_grad, logs, cosine, sine, qkv, lower, upper)


TOGETHER = 1


def inner_back_kernel(
    group_ref,
    marks_ref,
    mixed_grad_ref,
    log_ref,
    cos_ref,
    sin_ref,
    edge_grad_ref,
    edge_sum_ref,
    qkv_ref,
    *rest,
):
    grad_ref, sum_ref = rest[-2:]
    count = qkv_ref.shape[1]
    inner = count // BLOCK - 2
    sum_ref[0 : SPAN - HALF, :] = edge_sum_ref[0, 0, HALF:, :]
    grad_ref[0:BLOCK, 0:GROUP] = edge_grad_ref[0, 0]
    grad_ref[count - BLOCK :, 0:GROUP] = edge_grad_ref[0, 1]

    def finish(place):
        own_cosine = cos_ref[place, :]
        own_sine = sin_ref[place, :]
        for sub in range(GROUP_PAIRS):
            lanes = slice(sub * LANES, (sub + 1) * LANES)
            key_lanes = slice(GROUP + sub * LANES, GROUP + (sub + 1) * LANES)
            grad_ref[place, key_lanes] = turned_back(
                sum_ref[place, lanes], own_cosine, own_sine
            ).astype(BF)
        grad_ref[place, 2 * GROUP :] = sum_ref[place, GROUP:].astype(BF)

    for first in range(1, inner + 1, TOGETHER):
        blocks = range(first, min(first + TOGETHER, inner + 1))
        places = []
        items = []
        for block in blocks:
            bias = window_bias(marks_ref, block)
            start = block * BLOCK - HALF
            window = slice(start, start + SPAN)
            mine = slice(block * BLOCK, (block + 1) * BLOCK)
            for sub in range(GROUP_PAIRS):
                lanes = slice(sub * LANES, (sub + 1) * LANES)
                places.append((mine, start, sub))
                items.append(
                    (
                        stacked(qkv_ref[0, mine, lanes] * BF(0.125)),
                        qkv_ref[0, window, GROUP + sub * LANES : GROUP + (sub + 1) * LANES],
                        qkv_ref[0, window, 2 * GROUP + sub * LANES : 2 * GROUP + (sub + 1) * LANES],
                        stacked(mixed_grad_ref[mine, lanes]),
                        log_ref[block, 0, sub : sub + 1, :],
                        bias,
                    )
                )
        for (mine, start, sub), (query_grad, key_grad, value_grad) in zip(places, many_back(items)):
            lanes = slice(sub * LANES, (sub + 1) * LANES)
            value_lanes = slice(GROUP + sub * LANES, GROUP + (sub + 1) * LANES)
            older = slice(start, start + BLOCK)
            newer = slice(start + BLOCK, start + SPAN)
            sum_ref[older, lanes] += key_grad[:BLOCK]
            sum_ref[newer, lanes] = key_grad[BLOCK:]
            sum_ref[older, value_lanes] += value_grad[:BLOCK]
            sum_ref[newer, value_lanes] = value_grad[BLOCK:]
            grad_ref[mine, lanes] = turned_back(query_grad, cos_ref[mine, :], sin_ref[mine, :]).astype(BF)
        finish(slice(blocks[0] * BLOCK - HALF, (blocks[-1] + 1) * BLOCK - HALF))

    tail = SPAN - HALF
    sum_ref[count - tail : count - HALF, :] += edge_sum_ref[0, 1, 0:BLOCK, :]
    finish(slice(count - tail, count - HALF))


def inner_back(group, marks, qkv, mixed_grad, logs, cosine, sine, edge_grad, edge_sum, after):
    count = qkv.shape[1]
    return pl.pallas_call(
        inner_back_kernel,
        grid_spec=pltpu.PrefetchScalarGridSpec(
            num_scalar_prefetch=1,
            grid=(1,),
            in_specs=[
                SMEM,
                pl.BlockSpec((count, GROUP), lambda i, g: (0, g[0])),
                pl.BlockSpec((count // BLOCK, 1, 8, 2 * BLOCK), lambda i, g: (0, g[0], 0, 0)),
                pl.BlockSpec((count, LANES), lambda i, g: (0, 0)),
                pl.BlockSpec((count, LANES), lambda i, g: (0, 0)),
                pl.BlockSpec((1, 2, BLOCK, GROUP), lambda i, g: (g[0], 0, 0, 0)),
                pl.BlockSpec((1, 2, SPAN, 2 * GROUP), lambda i, g: (g[0], 0, 0, 0)),
                pl.BlockSpec((1, count, QKV_HALF), lambda i, g: (g[0], 0, 0)),
                *[ANY for _ in after],
            ],
            out_specs=pl.BlockSpec((count, QKV_HALF), lambda i, g: (0, 0)),
            scratch_shapes=[
                pltpu.VMEM((count, 2 * GROUP), F32),
            ],
        ),
        out_shape=jax.ShapeDtypeStruct((count, QKV_HALF), BF),
        compiler_params=params(8),
        cost_estimate=SMALL,
        name="inner_back",
    )(
        jnp.reshape(group, (1,)).astype(jnp.int32),
        marks,
        mixed_grad,
        logs,
        cosine,
        sine,
        edge_grad,
        edge_sum,
        qkv,
        *after,
    )


def patch_kernel(
    group_ref, cos_ref, sin_ref, edge_sum_ref, lower_ref, upper_ref, _, out_ref, edge_ref, sems
):
    group = group_ref[0]
    count = out_ref.shape[0]
    copies = []
    for side, (place, own, halo_ref) in enumerate(
        ((0, HALF, lower_ref), (count - HALF, BLOCK, upper_ref))
    ):
        total = edge_sum_ref[group, side, own : own + HALF, :] + halo_ref[group].astype(F32)
        cosine = cos_ref[place : place + HALF, :]
        sine = sin_ref[place : place + HALF, :]
        for sub in range(GROUP_PAIRS):
            lanes = slice(sub * LANES, (sub + 1) * LANES)
            edge_ref[side, :, lanes] = turned_back(total[:, lanes], cosine, sine).astype(BF)
        edge_ref[side, :, GROUP:] = total[:, GROUP:].astype(BF)
        copies.append(
            pltpu.make_async_copy(
                edge_ref.at[side],
                out_ref.at[pl.ds(place, HALF), pl.ds(GROUP, 2 * GROUP)],
                sems.at[side],
            )
        )
    for copy in copies:
        copy.start()
    for copy in copies:
        copy.wait()


def patch(group, cosine, sine, edge_sum, from_lower, from_upper, grads):
    return pl.pallas_call(
        patch_kernel,
        in_specs=[SMEM, *[VMEM] * 5, ANY],
        out_specs=ANY,
        out_shape=jax.ShapeDtypeStruct(grads.shape, BF),
        input_output_aliases={6: 0},
        scratch_shapes=[pltpu.VMEM((2, HALF, 2 * GROUP), BF), pltpu.SemaphoreType.DMA((2,))],
        compiler_params=params(8),
        cost_estimate=SMALL,
        name="patch",
    )(
        jnp.reshape(group, (1,)).astype(jnp.int32),
        cosine,
        sine,
        edge_sum,
        from_lower,
        from_upper,
        grads,
    )


def input_grad_kernel(count, order_ref, x_ref, gains_ref, first_ref, second_ref, grad_ref, *refs):
    weight_refs = refs[:count]
    out_ref, w_ref, sems = refs[count:]

    @pl.when(pl.program_id(0) == 0)
    def _():
        load_weights(weight_refs, w_ref, sems)

    unit, scale = normalized(x_ref[...].astype(F32))
    half = order_ref[0]
    grad_normed = dot(first_ref[...], w_ref[half, :, :QKV_HALF], 1, 1) + dot(
        second_ref[...], w_ref[1 - half, :, :QKV_HALF], 1, 1
    )
    out_ref[...] = grad_ref[...] + norm_back(grad_normed, unit, scale, gains_ref[0:1, :])


def input_grad(half, tokens, gains, weights, first, second, grad):
    count = tokens.shape[0]
    size = min(256, count)
    operands = weights.operands()
    return pl.pallas_call(
        partial(input_grad_kernel, len(operands)),
        grid=(count // size,),
        in_specs=[
            SMEM,
            rows((size, D)),
            whole((16, D)),
            rows((size, QKV_HALF)),
            rows((size, QKV_HALF)),
            rows((size, D)),
            *weights.specs(),
        ],
        out_specs=rows((size, D)),
        out_shape=jax.ShapeDtypeStruct((count, D), F32),
        scratch_shapes=weights.scratch(),
        compiler_params=params(12),
        cost_estimate=SMALL,
        name="input_grad",
    )(jnp.reshape(half, (1,)).astype(jnp.int32), tokens, gains, first, second, grad, *operands)


TILE = 256


def store_slots(slots_ref, out_ref, product):
    step = CHIP_ROWS
    for index in range(D // step):
        place = pl.multiple_of(slots_ref[1 + index] * step, 16)
        out_ref[pl.ds(place, step), :] = product[index * step : (index + 1) * step].astype(BF)


def weight_products(slots_ref, out_ref, turned, grad_ref, first, size):
    for tile in range(0, size, TILE):
        width = min(TILE, size - tile)
        product = dot(turned, grad_ref[:, tile : tile + width])
        for index in range(D // CHIP_ROWS):
            place = pl.multiple_of(slots_ref[1 + index] * CHIP_ROWS, 16)
            out_ref[pl.ds(place, CHIP_ROWS), first + tile : first + tile + width] = product[
                index * CHIP_ROWS : (index + 1) * CHIP_ROWS
            ].astype(BF)


def mixed_weight_kernel(slots_ref, normed_ref, grad_ref, mixed_ref, low_ref, *rest):
    out_ref = rest[-1]
    weight_products(slots_ref, out_ref, normed_ref[...].T, grad_ref, 0, QKV_HALF)
    lanes = pl.ds(pl.multiple_of(slots_ref[0] * GROUP, LANES), GROUP)
    weight_products(slots_ref, out_ref, mixed_ref[...].T, low_ref.at[:, lanes], QKV_HALF, GROUP)


def mixed_weight_grad(slots, normed, dqkv, mixed, low, after=()):
    count = normed.shape[0]
    return pl.pallas_call(
        mixed_weight_kernel,
        in_specs=[SMEM, *[VMEM] * 4, *[ANY for _ in after]],
        out_specs=VMEM,
        out_shape=jax.ShapeDtypeStruct((D, MIXED_HALF), BF),
        compiler_params=params(8),
        cost_estimate=SMALL,
        name="mixed_weight_grad",
    )(slots, normed, dqkv, mixed, low, *after)


def ff_weight_kernel(slots_ref, normed_ref, cot_ref, both_ref, hidden_ref, *rest):
    out_ref = rest[-1]

    @pl.when(slots_ref[0] == 0)
    def _():
        left = both_ref.at[:, 0:FF_HALF]
        weight_products(slots_ref, out_ref, normed_ref[...].T, left, 0, FF_HALF)

    @pl.when(slots_ref[0] == 1)
    def _():
        left = both_ref.at[:, FF_HALF : 2 * FF]
        weight_products(slots_ref, out_ref, normed_ref[...].T, left, 0, FF_LEFT)
        weight_products(slots_ref, out_ref, cot_ref[...].T, hidden_ref, FF_LEFT, FF)
        out_ref[:, FF_LEFT + FF :] = jnp.zeros((D, FF_HALF - FF_LEFT - FF), BF)


def ff_weight_grad(slots, normed, cot, both, hidden, after):
    count = normed.shape[0]
    return pl.pallas_call(
        ff_weight_kernel,
        in_specs=[SMEM, *[VMEM] * 4, *[ANY for _ in after]],
        out_specs=VMEM,
        out_shape=jax.ShapeDtypeStruct((D, FF_HALF), BF),
        compiler_params=params(8),
        cost_estimate=SMALL,
        name="ff_weight_grad",
    )(slots, normed, cot, both, hidden, *after)


def join_kernel(*refs):
    out_ref = refs[-1]
    first = 0
    for ref in refs[:-1]:
        out_ref[first : first + ref.shape[0], :] = ref[...]
        first += ref.shape[0]


def join(*parts):
    count = sum(part.shape[0] for part in parts)
    width = parts[0].shape[1]
    return pl.pallas_call(
        join_kernel,
        in_specs=[VMEM for _ in parts],
        out_specs=VMEM,
        out_shape=jax.ShapeDtypeStruct((count, width), parts[0].dtype),
        compiler_params=params(8),
        cost_estimate=SMALL,
        name="join",
    )(*parts)


def doc_marks(doc_lengths, row_count):
    me = lax.axis_index("tok")
    ends = jnp.cumsum(doc_lengths).astype(jnp.int32)
    before = jnp.where(me > 0, ends[jnp.maximum(me - 1, 0)], 0)
    return jnp.stack([before, ends[me], ends[me + 1], me * row_count]).astype(jnp.int32)


def rotary_tables(marks, row_count):
    place = marks[3] + jnp.arange(row_count, dtype=jnp.int32)
    offset = place - jnp.where(place >= marks[1], marks[1], marks[0])
    frequency = 10000.0 ** (-jnp.arange(0, HEAD_DIM, 2, dtype=F32) / HEAD_DIM)
    angles = offset.astype(F32)[:, None] * frequency[None, :]
    cosine = jnp.cos(angles)
    sine = jnp.sin(angles)
    return (
        jnp.concatenate([cosine] * 4, axis=1),
        jnp.concatenate([-sine, sine, -sine, sine], axis=1),
    )


def passed_along(value, steps):
    count = lax.axis_size("tok")
    first, last = (max(0, -steps), min(count, count - steps))
    return lax.ppermute(value, "tok", [(at, at + steps) for at in range(first, last)])


STAGED_DEVICES = 32


def staged():
    return lax.axis_size("tok") == STAGED_DEVICES


def exchange(value, by_core):
    pairs = [(at, at ^ by_core[at & 1]) for at in range(lax.axis_size("tok"))]
    return lax.ppermute(value, "tok", pairs)


CORE = (1, 1)
DEEP = tuple((step << 3, step << 3) for step in range(4))
NEAR = (2, 4)
FAR = (4, 2)


def slot_codes(core):
    slot = jnp.arange(16, dtype=jnp.int32)
    depth, near, far = (slot & 3, (slot >> 2) & 1, slot >> 3)
    return (depth << 2) | jnp.where(core == 0, (far << 1) | near, (near << 1) | far)


def chip_slots(chip, core):
    code = jnp.arange(16, dtype=jnp.int32) ^ chip
    depth, second, first = (code >> 2, (code >> 1) & 1, code & 1)
    return depth | jnp.where(core == 0, (second << 3) | (first << 2), (first << 3) | (second << 2))


def stage_after(value, *others):
    return lax.optimization_barrier((value, *others))[0]


def in_hbm(value):
    return pltpu.with_memory_space_constraint(value, pltpu.HBM)


def core_pieces(shard):
    core = lax.axis_index("tok") & 1
    half = shard.shape[1] // 2
    keep = jnp.where(core == 0, shard[:, :half], shard[:, half:])
    send = jnp.where(core == 0, shard[:, half:], shard[:, :half])
    came = exchange(send, CORE)
    return jnp.concatenate(
        [jnp.where(core == 0, keep, came), jnp.where(core == 0, came, keep)], axis=0
    )


def final_gather(held, far):
    me = lax.axis_index("tok")
    core = me & 1
    chip = me >> 1
    places = jnp.concatenate(
        [slot_codes(core) ^ chip, slot_codes(1 - core) ^ chip, jnp.full((1,), core, jnp.int32)]
    )
    return Weights([held, far, exchange(held, CORE), exchange(far, CORE)], places)


def whole_weights(shard):
    full = lax.all_gather(shard, "tok", axis=0, tiled=True)
    half = full.shape[1] // 2
    return Weights([jnp.stack([full[:, :half], full[:, half:]])])


def added(left, right):
    return (left.astype(F32) + right.astype(F32)).astype(BF)


def core_sum(keep, came):
    return added(keep[:384], came[:384]), added(keep[384:], came[384:])


def far_sum(near, came):
    return added(near[:192], came[:192]), added(near[192:], came[192:])


def near_sum(near, came):
    return [
        added(near[first : first + CHIP_ROWS], came[first : first + CHIP_ROWS])
        for first in range(0, 192, CHIP_ROWS)
    ]


def deep_sum(parts, *after):
    core = lax.axis_index("tok") & 1
    total = parts[0].astype(F32)
    for step in (1, 2, 3):
        total = total + stage_after(exchange(parts[step], DEEP[step]), after[step - 1]).astype(F32)
    share = CHIP_ROWS // 2
    lower, upper = (total[:share], total[share:])
    own = jnp.where(core == 0, lower, upper)
    came = exchange(jnp.where(core == 0, upper, lower), CORE)
    return jnp.concatenate(
        [jnp.where(core == 0, own, came), jnp.where(core == 0, came, own)], axis=1
    )


def summed(keep, send):
    full = jnp.concatenate([keep, send], axis=1)
    return lax.psum_scatter(full.astype(F32), "tok", scatter_dimension=0, tiled=True)


def by_part(groups):
    return jnp.concatenate(
        [
            groups[:, half * MIXED_HALF + part * GROUP : half * MIXED_HALF + (part + 1) * GROUP]
            for part in range(3)
            for half in range(2)
        ],
        axis=1,
    )


def on_device(
    tokens,
    doc_lengths,
    first_gain,
    qkv_weight,
    attn_weight,
    second_gain,
    feed_in_weight,
    feed_out_weight,
    cotangent,
):
    row_count = tokens.shape[0]
    share = first_gain.shape[0]

    def spread(gain):
        return jnp.broadcast_to(gain[:, None], (share, LANES))

    def group_of(half):
        return [
            qkv_weight[:, part * D + half * GROUP : part * D + (half + 1) * GROUP]
            for part in range(3)
        ]

    shard_one = jnp.concatenate(
        [*group_of(0), spread(first_gain), *group_of(1), spread(second_gain)], axis=1
    )
    shard_two = jnp.concatenate([feed_in_weight, feed_out_weight.T, attn_weight], axis=1)
    weights_two = lax.all_gather(shard_two, "tok", axis=0, tiled=True)
    if staged():
        piece = core_pieces(shard_one)
        marks = doc_marks(stage_after(doc_lengths, piece), row_count)
        cosine, sine = rotary_tables(marks, row_count)
        came = [exchange(piece, DEEP[step]) for step in (1, 2, 3)]
        *came, marks = lax.optimization_barrier((*came, marks, cosine, sine))[:4]
        one = join(piece, *came)
        one = join(one, exchange(one, NEAR))
        weights_one = final_gather(one, exchange(one, FAR))
    else:
        marks = doc_marks(doc_lengths, row_count)
        cosine, sine = rotary_tables(marks, row_count)
        weights_one = whole_weights(shard_one)
    normed, qkv, gains = project_qkv(tokens, weights_one, in_hbm(cosine), in_hbm(sine))
    lower = passed_along(qkv[:, row_count - HALF :, GROUP:], 1)
    upper = passed_along(qkv[:, :HALF, GROUP:], -1)
    mixed, logs = attend_inner(marks, qkv)
    mixed, edge_logs = attend_edges(marks, qkv, lower, upper, mixed)
    residual, normed_two, both, hidden = dense(tokens, in_hbm(mixed), cotangent, gains, in_hbm(weights_two))
    me = lax.axis_index("tok")
    if staged():
        halves = (1 - (me & 1), me & 1)
    else:
        halves = (jnp.int32(1), jnp.int32(0))

    def order(half):
        if staged():
            slots = chip_slots(me >> 1, half)
        else:
            slots = jnp.arange(D // CHIP_ROWS, dtype=jnp.int32)
        return jnp.concatenate([jnp.reshape(half, (1,)).astype(jnp.int32), slots])

    def ff_grad(half, after):
        return ff_weight_grad(order(half), normed_two, cotangent, both, hidden, after)

    def inner(half, after):
        return inner_back(
            half, marks, qkv, mixed_grad, logs, cosine, sine, edge_grad, edge_sum, after
        )

    def patched(half, grads):
        return patch(half, cosine, sine, edge_sum, from_lower, from_upper, grads)

    def finish(first, second):
        return input_grad(halves[0], tokens, gains, weights_one, first, second, grad)

    send, keep = halves
    def mixed_weight(half, dqkv):
        return mixed_weight_grad(order(half), normed, dqkv, mixed, low)

    ff_send = ff_grad(send, [])
    ff_keep = ff_grad(keep, [ff_send])
    low, mixed_grad, grad = dense_back(residual, cotangent, both, gains, weights_two, [ff_keep])
    if staged():
        near, far = core_sum(ff_keep, stage_after(exchange(ff_send, CORE), mixed_grad))
        mixed_grad = stage_after(mixed_grad, far)
    edge_grad, edge_sum, away = edge_back(marks, qkv, mixed_grad, edge_logs, cosine, sine, lower, upper)
    from_upper = passed_along(away[0], -1)
    from_lower = passed_along(away[1], 1)

    if staged():
        first = inner(send, [])
        from_lower, from_upper, first = lax.optimization_barrier((from_lower, from_upper, first))
        near, far = far_sum(near, stage_after(exchange(far, FAR), from_lower, from_upper))
        first = patched(send, stage_after(first, far))
        mixed_send = mixed_weight(send, first)
        second = inner(keep, [mixed_send])
        parts = near_sum(near, stage_after(exchange(far, NEAR), second))
        second = patched(keep, stage_after(second, *parts))
        mixed_keep = mixed_weight(keep, second)
        mixed_near, mixed_far = core_sum(mixed_keep, exchange(stage_after(mixed_send, second), CORE))
        grad_in = finish(first, stage_after(second, mixed_far))
        mixed_near, mixed_far = far_sum(mixed_near, stage_after(exchange(mixed_far, FAR), grad_in))
        sum_ff = deep_sum(parts, *[mixed_far] * 3)
        result = result_of(residual, hidden, weights_two, [mixed_far])
        mixed_parts = near_sum(mixed_near, stage_after(exchange(mixed_far, NEAR), result))
        sum_mixed = deep_sum(mixed_parts, *[mixed_parts[0]] * 3)
    else:
        first = patched(send, inner(send, []))
        second = patched(keep, inner(keep, []))
        result = result_of(residual, hidden, weights_two, [])
        grad_in = finish(first, second)
        sum_ff = summed(ff_keep, ff_send)
        sum_mixed = summed(mixed_weight(keep, second), mixed_weight(send, first))
    sum_qkv = by_part(sum_mixed)
    sent_attn = jnp.concatenate(
        [sum_mixed[:, QKV_HALF:MIXED_HALF], sum_mixed[:, MIXED_HALF + QKV_HALF :]], axis=1
    )
    sent_in = jnp.concatenate(
        [sum_ff[:, :FF_HALF], sum_ff[:, FF_HALF : FF_HALF + FF_LEFT]], axis=1
    )
    sent_down = sum_ff[:, FF_HALF + FF_LEFT : FF_HALF + FF_LEFT + FF].T

    def gain_grad(summed, weight, gain):
        return jnp.sum(summed * weight.astype(F32), axis=1) / gain.astype(F32)

    return (
        result,
        grad_in,
        gain_grad(sum_qkv, qkv_weight, first_gain),
        sum_qkv,
        sent_attn,
        gain_grad(sent_in, feed_in_weight, second_gain),
        sent_in,
        sent_down,
    )


def solution(mesh):
    in_specs = (
        P("tok", None),
        P(),
        P("tok"),
        P("tok", None),
        P("tok", None),
        P("tok"),
        P("tok", None),
        P(None, "tok"),
        P("tok", None),
    )
    out_specs = (
        P("tok", None),
        P("tok", None),
        P("tok"),
        P("tok", None),
        P("tok", None),
        P("tok"),
        P("tok", None),
        P(None, "tok"),
    )
    return jax.shard_map(
        on_device, mesh=mesh, in_specs=in_specs, out_specs=out_specs, check_vma=False
    )
```

```python
from functools import partial

import jax
import jax.numpy as jnp
from jax import lax
from jax.experimental import pallas as pl
from jax.experimental.pallas import tpu as pltpu
from jax.sharding import PartitionSpec as P

D = 768
FF = 1152
HEADS = 12
HEAD_DIM = 64
HALF = 64
PAIRS = HEADS // 2
BLOCK = 128
SPAN = BLOCK + 2 * HALF
LANES = 128
QKV_HALF = 3 * D // 2
GROUP = D // 2
GROUP_PAIRS = PAIRS // 2
FF_HALF = 1792
FF_LEFT = 2 * FF - FF_HALF
MIXED_HALF = QKV_HALF + GROUP
MIB = 1024 * 1024
BF = jnp.bfloat16
F32 = jnp.float32


def dot(left, right, left_dim=1, right_dim=0):
    return lax.dot_general(
        left, right, (((left_dim,), (right_dim,)), ((), ())), preferred_element_type=F32
    )


def params(mib):
    return pltpu.CompilerParams(vmem_limit_bytes=mib * MIB)


def whole(shape):
    return pl.BlockSpec(shape, lambda *_: (0,) * len(shape))


def rows(shape):
    return pl.BlockSpec(shape, lambda i: (i,) + (0,) * (len(shape) - 1))


COST = pl.CostEstimate(flops=4000000000, bytes_accessed=1000, transcendentals=0)
SMEM = pl.BlockSpec(memory_space=pltpu.SMEM)
ANY = pl.BlockSpec(memory_space=pl.ANY)
VMEM = pl.BlockSpec(memory_space=pltpu.VMEM)
HBM = pl.BlockSpec(memory_space=pltpu.HBM)
HBM = pl.BlockSpec(memory_space=pltpu.HBM)


def lane_ids(shape):
    return lax.broadcasted_iota(jnp.int32, shape, len(shape) - 1)


def swap_halves(values):
    low = (lane_ids(values.shape) & (HEAD_DIM - 1)) < HEAD_DIM // 2
    return jnp.where(
        low, pltpu.roll(values, LANES - HEAD_DIM // 2, 1), pltpu.roll(values, HEAD_DIM // 2, 1)
    )


def normalized(values):
    centered = values - jnp.mean(values, axis=-1, keepdims=True)
    scale = lax.rsqrt(jnp.mean(centered * centered, axis=-1, keepdims=True) + 1e-05)
    return centered * scale, scale


def norm_back(grad, unit, scale, gains):
    grad_unit = grad * gains
    return scale * (
        grad_unit
        - jnp.mean(grad_unit, axis=-1, keepdims=True)
        - unit * jnp.mean(grad_unit * unit, axis=-1, keepdims=True)
    )


CHIP_ROWS = 48


class Weights:
    def __init__(self, arrays, places=None):
        self.arrays = arrays
        self.places = places

    def operands(self):
        if self.places is None:
            return list(self.arrays)
        return [self.places, *self.arrays]

    def specs(self):
        if self.places is None:
            return [ANY]
        return [SMEM, VMEM, VMEM, VMEM, VMEM]

    def scratch(self):
        width = self.arrays[0].shape[-1]
        return [pltpu.VMEM((2, D, width), BF), pltpu.SemaphoreType.DMA((1,))]


def load_weights(refs, out_ref, sems):
    if len(refs) == 1:
        copy = pltpu.make_async_copy(refs[0], out_ref, sems.at[0])
        copy.start()
        copy.wait()
        return
    places_ref = refs[0]
    core = places_ref[32]
    for index, source in enumerate(refs[1:]):
        half = core if index < 2 else 1 - core
        for slot in range(8):
            place = pl.multiple_of(places_ref[index * 8 + slot] * CHIP_ROWS, 16)
            out_ref[half, pl.ds(place, CHIP_ROWS), :] = source[
                slot * CHIP_ROWS : (slot + 1) * CHIP_ROWS, :
            ]


def qkv_kernel(count, x_ref, cos_ref, sin_ref, *refs):
    weight_refs = refs[:count]
    normed_ref, qkv_ref, gains_ref, w_ref, sems = refs[count:]

    @pl.when(pl.program_id(0) == 0)
    def _():
        load_weights(weight_refs, w_ref, sems)
        for half in range(2):
            turned = w_ref[half, :, QKV_HALF:].T.astype(F32)
            gains_ref[half * 8 : half * 8 + 8, :] = turned[:8]

    unit, _ = normalized(x_ref[...].astype(F32))
    normed = (unit * gains_ref[0:1, :]).astype(BF)
    normed_ref[...] = normed
    cosine = cos_ref[...]
    sine = sin_ref[...]
    for half in range(2):
        merged = dot(normed, w_ref[half, :, :QKV_HALF])
        for tile in range(QKV_HALF // LANES):
            lanes = slice(tile * LANES, (tile + 1) * LANES)
            part = merged[:, lanes]
            if tile * LANES < 2 * GROUP:
                part = part * cosine + swap_halves(part) * sine
            qkv_ref[half, :, lanes] = part.astype(BF)


def project_qkv(tokens, weights, cosine, sine):
    count = tokens.shape[0]
    size = min(256, count)
    operands = weights.operands()
    return pl.pallas_call(
        partial(qkv_kernel, len(operands)),
        grid=(count // size,),
        in_specs=[rows((size, D)), rows((size, LANES)), rows((size, LANES)), *weights.specs()],
        out_specs=[
            rows((size, D)),
            pl.BlockSpec((2, size, QKV_HALF), lambda i: (0, i, 0)),
            whole((16, D)),
        ],
        out_shape=[
            jax.ShapeDtypeStruct((count, D), BF),
            jax.ShapeDtypeStruct((2, count, QKV_HALF), BF),
            jax.ShapeDtypeStruct((16, D), F32),
        ],
        scratch_shapes=weights.scratch(),
        compiler_params=params(12),
        cost_estimate=COST,
        name="qkv",
    )(tokens, cosine, sine, *operands)


def window_bias(marks_ref, block):
    shape = (SPAN, 2 * BLOCK)
    first = marks_ref[3] + block * BLOCK
    key = lax.broadcasted_iota(jnp.int32, shape, 0)
    query = lax.broadcasted_iota(jnp.int32, (1, 2 * BLOCK), 1) & (BLOCK - 1)
    place = first + query
    lowest = query
    highest = query + 2 * HALF
    for index in range(3):
        mark = marks_ref[index]
        edge = mark - first + HALF
        past = place >= mark
        lowest = jnp.where(past, jnp.maximum(lowest, edge), lowest)
        highest = jnp.where(past, highest, jnp.minimum(highest, edge - 1))
    return jnp.where((key >= lowest) & (key <= highest), 0.0, -1e30).astype(F32)


def stacked(pair):
    low = lane_ids(pair.shape) < HEAD_DIM
    zero = jnp.zeros_like(pair)
    return jnp.concatenate([jnp.where(low, pair, zero), jnp.where(low, zero, pair)], axis=0)


def unstacked(both):
    low = lane_ids((BLOCK, LANES)) < HEAD_DIM
    return jnp.where(low, both[:BLOCK], both[BLOCK:])


def span_of(qkv_ref, lower_ref, upper_ref, half, block, part, sub):
    count = qkv_ref.shape[1]
    first = block * BLOCK - HALF
    lanes = slice(part * GROUP + sub * LANES, part * GROUP + (sub + 1) * LANES)
    halo_lanes = slice((part - 1) * GROUP + sub * LANES, (part - 1) * GROUP + (sub + 1) * LANES)
    own = qkv_ref[half, max(first, 0) : min(first + SPAN, count), lanes]
    if first < 0:
        own = jnp.concatenate([lower_ref[half, :, halo_lanes], own], axis=0)
    if first + SPAN > count:
        own = jnp.concatenate([own, upper_ref[half, :, halo_lanes]], axis=0)
    return own


def many_attend(operands):
    scores = [dot(keys, query, 1, 1) + bias for query, keys, _, bias in operands]
    peaks = [jnp.max(score, axis=0, keepdims=True) for score in scores]
    expos = [jnp.exp(score - peak) for score, peak in zip(scores, peaks)]
    totals = [jnp.sum(expo, axis=0, keepdims=True) for expo in expos]
    weights = [(expo * (1.0 / total)).astype(BF) for expo, total in zip(expos, totals)]
    mixed = [unstacked(dot(weight, item[2], 0, 0)) for weight, item in zip(weights, operands)]
    return [(mix, peak + jnp.log(total)) for mix, peak, total in zip(mixed, peaks, totals)]


def attend_blocks(marks_ref, qkv_ref, lower_ref, upper_ref, blocks, store):
    for block in blocks:
        bias = window_bias(marks_ref, block)
        mine = slice(block * BLOCK, (block + 1) * BLOCK)
        for first in range(0, PAIRS, PAIRS_TOGETHER):
            pairs = range(first, first + PAIRS_TOGETHER)
            items = []
            for pair in pairs:
                half, sub = divmod(pair, GROUP_PAIRS)
                where = (qkv_ref, lower_ref, upper_ref, half, block)
                items.append(
                    (
                        stacked(qkv_ref[half, mine, sub * LANES : (sub + 1) * LANES] * BF(0.125)),
                        span_of(*where, 1, sub),
                        span_of(*where, 2, sub),
                        bias,
                    )
                )
            for pair, (mix, logs) in zip(pairs, many_attend(items)):
                store(block, pair, mix.astype(BF), logs)


def attend_inner_kernel(marks_ref, qkv_ref, out_ref, log_ref):
    def store(block, pair, mix, logs):
        half, sub = divmod(pair, GROUP_PAIRS)
        out_ref[block * BLOCK : (block + 1) * BLOCK, pair * LANES : (pair + 1) * LANES] = mix
        log_ref[block, half, sub : sub + 1, :] = logs

    blocks = range(1, qkv_ref.shape[1] // BLOCK - 1)
    attend_blocks(marks_ref, qkv_ref, None, None, blocks, store)


def attend_inner(marks, qkv):
    count = qkv.shape[1]
    return pl.pallas_call(
        attend_inner_kernel,
        in_specs=[SMEM, VMEM],
        out_specs=[VMEM, VMEM],
        out_shape=[
            jax.ShapeDtypeStruct((count, D), BF),
            jax.ShapeDtypeStruct((count // BLOCK, 2, 8, 2 * BLOCK), F32),
        ],
        compiler_params=params(8),
        cost_estimate=COST,
        name="attend_inner",
    )(marks, qkv)


def attend_edges_kernel(marks_ref, qkv_ref, lower_ref, upper_ref, _, out_ref, log_ref, edge_ref, sems):
    count = qkv_ref.shape[1]
    last = count // BLOCK - 1

    def store(block, pair, mix, logs):
        half, sub = divmod(pair, GROUP_PAIRS)
        side = min(block, 1)
        edge_ref[side, :, pair * LANES : (pair + 1) * LANES] = mix
        log_ref[side, half, sub : sub + 1, :] = logs

    attend_blocks(marks_ref, qkv_ref, lower_ref, upper_ref, (0, last), store)
    copies = [
        pltpu.make_async_copy(
            edge_ref.at[side], out_ref.at[pl.ds(block * BLOCK, BLOCK)], sems.at[side]
        )
        for side, block in enumerate((0, last))
    ]
    for copy in copies:
        copy.start()
    for copy in copies:
        copy.wait()


def attend_edges(marks, qkv, lower, upper, mixed):
    return pl.pallas_call(
        attend_edges_kernel,
        in_specs=[SMEM, VMEM, VMEM, VMEM, ANY],
        out_specs=[ANY, VMEM],
        out_shape=[
            jax.ShapeDtypeStruct(mixed.shape, BF),
            jax.ShapeDtypeStruct((2, 2, 8, 2 * BLOCK), F32),
        ],
        input_output_aliases={4: 0},
        scratch_shapes=[pltpu.VMEM((2, BLOCK, D), BF), pltpu.SemaphoreType.DMA((2,))],
        compiler_params=params(8),
        cost_estimate=COST,
        name="attend_edges",
    )(marks, qkv, lower, upper, mixed)


PAIRS_TOGETHER = 1
FF_PARTS = tuple((first, min(256, FF - first)) for first in range(0, FF, 256))


def dense_kernel(
    x_ref,
    mixed_ref,
    cot_ref,
    gains_ref,
    source_ref,
    residual_ref,
    normed_ref,
    both_ref,
    hidden_ref,
    near_ref,
    w_ref,
    sems,
):
    ranges = [(3 * FF, D), (0, 3 * FF)]
    fetch = pltpu.make_async_copy(mixed_ref, near_ref, sems.at[2])
    fetch.start()
    copies = [
        pltpu.make_async_copy(
            source_ref.at[:, pl.ds(first, size)], w_ref.at[:, pl.ds(first, size)], sems.at[index]
        )
        for index, (first, size) in enumerate(ranges)
    ]
    for copy in copies:
        copy.start()
    fetch.wait()
    copies[0].wait()
    count = x_ref.shape[0]
    size = min(512, count)
    blocks = [slice(first, first + size) for first in range(0, count, size)]
    for mine in blocks:
        residual = x_ref[mine, :].astype(F32) + dot(near_ref[mine, :], w_ref[:, 3 * FF :])
        residual_ref[mine, :] = residual
        unit, _ = normalized(residual)
        normed_ref[mine, :] = (unit * gains_ref[8:9, :]).astype(BF)
    copies[1].wait()
    for mine in blocks:
        normed = normed_ref[mine, :]
        cot = cot_ref[mine, :]
        for first, size in FF_PARTS:
            gate_cols = slice(first, first + size)
            up_cols = slice(FF + first, FF + first + size)
            down_cols = slice(2 * FF + first, 2 * FF + first + size)
            gate = dot(normed, w_ref[:, gate_cols])
            up = dot(normed, w_ref[:, up_cols])
            grad_hidden = dot(cot, w_ref[:, down_cols])
            share = 0.5 + 0.5 * lax.erf(gate * 0.7071067811865476)
            active = gate * share
            slope = share + gate * (jnp.exp(-0.5 * gate * gate) * 0.3989422804014327)
            hidden_ref[mine, gate_cols] = (active * up).astype(BF)
            both_ref[mine, gate_cols] = (grad_hidden * up * slope).astype(BF)
            both_ref[mine, up_cols] = (grad_hidden * active).astype(BF)


def dense(tokens, mixed, cotangent, gains, weights):
    count = tokens.shape[0]
    wide = [(D, F32), (D, BF), (2 * FF, BF), (FF, BF)]
    return pl.pallas_call(
        dense_kernel,
        in_specs=[VMEM, HBM, VMEM, VMEM, HBM],
        out_specs=[VMEM] * 4,
        out_shape=[jax.ShapeDtypeStruct((count, width), kind) for width, kind in wide],
        scratch_shapes=[
            pltpu.VMEM((count, D), BF),
            pltpu.VMEM(weights.shape, BF),
            pltpu.SemaphoreType.DMA((3,)),
        ],
        compiler_params=params(16),
        cost_estimate=COST,
        name="dense",
    )(tokens, mixed, cotangent, gains, weights)


def dense_back_kernel(residual_ref, cot_ref, both_ref, gains_ref, w_ref, *rest):
    low_ref, mixed_grad_ref, grad_ref = rest[-3:]
    count = residual_ref.shape[0]
    size = min(512, count)
    for first in range(0, count, size):
        mine = slice(first, first + size)
        unit, scale = normalized(residual_ref[mine, :])
        grad_normed = dot(both_ref[mine, :], w_ref[:, : 2 * FF], 1, 1)
        grad = cot_ref[mine, :].astype(F32) + norm_back(
            grad_normed, unit, scale, gains_ref[8:9, :]
        )
        grad_ref[mine, :] = grad
        low = grad.astype(BF)
        low_ref[mine, :] = low
        mixed_grad_ref[mine, :] = dot(low, w_ref[:, 3 * FF :], 1, 1).astype(BF)


def dense_back(residual, cotangent, both, gains, weights, after):
    count = residual.shape[0]
    wide = [(D, BF), (D, BF), (D, F32)]
    return pl.pallas_call(
        dense_back_kernel,
        in_specs=[*[VMEM] * 5, *[ANY for _ in after]],
        out_specs=[VMEM] * 3,
        out_shape=[jax.ShapeDtypeStruct((count, width), kind) for width, kind in wide],
        compiler_params=params(8),
        cost_estimate=COST,
        name="dense_back",
    )(residual, cotangent, both, gains, weights, *after)


def result_kernel(residual_ref, hidden_ref, w_ref, *rest):
    product = dot(hidden_ref[...], w_ref[:, 2 * FF : 3 * FF], 1, 1)
    rest[-1][...] = (residual_ref[...] + product).astype(BF)


def result_of(residual, hidden, weights, after):
    count = residual.shape[0]
    size = min(512, count)
    return pl.pallas_call(
        result_kernel,
        grid=(count // size,),
        in_specs=[rows((size, D)), rows((size, FF)), whole(weights.shape), *[ANY for _ in after]],
        out_specs=rows((size, D)),
        out_shape=jax.ShapeDtypeStruct((count, D), BF),
        compiler_params=params(16),
        cost_estimate=COST,
        name="result",
    )(residual, hidden, weights, *after)


def pair_back(query, keys, values, out_grad, logs, bias):
    scores = dot(keys, query, 1, 1) + bias
    weights = jnp.exp(scores - logs)
    weight_grad = dot(values, out_grad, 1, 1)
    score_grad = weights * (weight_grad - jnp.sum(weights * weight_grad, axis=0, keepdims=True))
    score_grad = score_grad.astype(BF)
    key_grad = dot(score_grad, query)
    value_grad = dot(weights.astype(BF), out_grad)
    query_grad = unstacked(dot(score_grad, keys, 0, 0)) * 0.125
    return query_grad, key_grad, value_grad


def many_back(operands):
    scores = [dot(keys, query, 1, 1) for query, keys, _, _, _, _ in operands]
    weight_grads = [dot(values, out_grad, 1, 1) for _, _, values, out_grad, _, _ in operands]
    weights = [jnp.exp(score + item[5] - item[4]) for score, item in zip(scores, operands)]
    value_grads = [dot(weight.astype(BF), item[3]) for weight, item in zip(weights, operands)]
    score_grads = [
        (weight * (grad - jnp.sum(weight * grad, axis=0, keepdims=True))).astype(BF)
        for weight, grad in zip(weights, weight_grads)
    ]
    key_grads = [dot(grad, item[0]) for grad, item in zip(score_grads, operands)]
    query_grads = [
        unstacked(dot(grad, item[1], 0, 0)) * 0.125 for grad, item in zip(score_grads, operands)
    ]
    return list(zip(query_grads, key_grads, value_grads))


def turned_back(values, cosine, sine):
    return values * cosine - swap_halves(values) * sine


def edge_back_kernel(
    marks_ref,
    mixed_grad_ref,
    log_ref,
    cos_ref,
    sin_ref,
    qkv_ref,
    lower_ref,
    upper_ref,
    grad_ref,
    sum_ref,
    away_ref,
):
    count = qkv_ref.shape[1]
    for side, block in enumerate((0, count // BLOCK - 1)):
        bias = window_bias(marks_ref, block)
        mine = slice(block * BLOCK, (block + 1) * BLOCK)
        sent = slice(0, HALF) if side == 0 else slice(SPAN - HALF, SPAN)
        for half in range(2):
            items = []
            for sub in range(GROUP_PAIRS):
                pair = half * GROUP_PAIRS + sub
                where = (qkv_ref, lower_ref, upper_ref, half, block)
                items.append(
                    (
                        stacked(qkv_ref[half, mine, sub * LANES : (sub + 1) * LANES] * BF(0.125)),
                        span_of(*where, 1, sub),
                        span_of(*where, 2, sub),
                        stacked(mixed_grad_ref[mine, pair * LANES : (pair + 1) * LANES]),
                        log_ref[side, half, sub : sub + 1, :],
                        bias,
                    )
                )
            for sub, (query_grad, key_grad, value_grad) in enumerate(many_back(items)):
                lanes = slice(sub * LANES, (sub + 1) * LANES)
                value_lanes = slice(GROUP + sub * LANES, GROUP + (sub + 1) * LANES)
                grad_ref[half, side, :, lanes] = turned_back(
                    query_grad, cos_ref[mine, :], sin_ref[mine, :]
                ).astype(BF)
                sum_ref[half, side, :, lanes] = key_grad
                sum_ref[half, side, :, value_lanes] = value_grad
                away_ref[side, half, :, lanes] = key_grad[sent].astype(BF)
                away_ref[side, half, :, value_lanes] = value_grad[sent].astype(BF)


def edge_back(marks, qkv, mixed_grad, logs, cosine, sine, lower, upper):
    return pl.pallas_call(
        edge_back_kernel,
        in_specs=[SMEM, *[VMEM] * 7],
        out_specs=[VMEM, VMEM, VMEM],
        out_shape=[
            jax.ShapeDtypeStruct((2, 2, BLOCK, GROUP), BF),
            jax.ShapeDtypeStruct((2, 2, SPAN, 2 * GROUP), F32),
            jax.ShapeDtypeStruct((2, 2, HALF, 2 * GROUP), BF),
        ],
        compiler_params=params(8),
        cost_estimate=COST,
        name="edge_back",
    )(marks, mixed_grad, logs, cosine, sine, qkv, lower, upper)


TOGETHER = 1


def inner_back_kernel(
    group_ref,
    marks_ref,
    mixed_grad_ref,
    log_ref,
    cos_ref,
    sin_ref,
    edge_grad_ref,
    edge_sum_ref,
    qkv_ref,
    *rest,
):
    grad_ref, sum_ref = rest[-2:]
    count = qkv_ref.shape[1]
    inner = count // BLOCK - 2
    sum_ref[0 : SPAN - HALF, :] = edge_sum_ref[0, 0, HALF:, :]
    grad_ref[0:BLOCK, 0:GROUP] = edge_grad_ref[0, 0]
    grad_ref[count - BLOCK :, 0:GROUP] = edge_grad_ref[0, 1]

    def finish(place):
        own_cosine = cos_ref[place, :]
        own_sine = sin_ref[place, :]
        for sub in range(GROUP_PAIRS):
            lanes = slice(sub * LANES, (sub + 1) * LANES)
            key_lanes = slice(GROUP + sub * LANES, GROUP + (sub + 1) * LANES)
            grad_ref[place, key_lanes] = turned_back(
                sum_ref[place, lanes], own_cosine, own_sine
            ).astype(BF)
        grad_ref[place, 2 * GROUP :] = sum_ref[place, GROUP:].astype(BF)

    for first in range(1, inner + 1, TOGETHER):
        blocks = range(first, min(first + TOGETHER, inner + 1))
        places = []
        items = []
        for block in blocks:
            bias = window_bias(marks_ref, block)
            start = block * BLOCK - HALF
            window = slice(start, start + SPAN)
            mine = slice(block * BLOCK, (block + 1) * BLOCK)
            for sub in range(GROUP_PAIRS):
                lanes = slice(sub * LANES, (sub + 1) * LANES)
                places.append((mine, start, sub))
                items.append(
                    (
                        stacked(qkv_ref[0, mine, lanes] * BF(0.125)),
                        qkv_ref[0, window, GROUP + sub * LANES : GROUP + (sub + 1) * LANES],
                        qkv_ref[0, window, 2 * GROUP + sub * LANES : 2 * GROUP + (sub + 1) * LANES],
                        stacked(mixed_grad_ref[mine, lanes]),
                        log_ref[block, 0, sub : sub + 1, :],
                        bias,
                    )
                )
        for (mine, start, sub), (query_grad, key_grad, value_grad) in zip(places, many_back(items)):
            lanes = slice(sub * LANES, (sub + 1) * LANES)
            value_lanes = slice(GROUP + sub * LANES, GROUP + (sub + 1) * LANES)
            older = slice(start, start + BLOCK)
            newer = slice(start + BLOCK, start + SPAN)
            sum_ref[older, lanes] += key_grad[:BLOCK]
            sum_ref[newer, lanes] = key_grad[BLOCK:]
            sum_ref[older, value_lanes] += value_grad[:BLOCK]
            sum_ref[newer, value_lanes] = value_grad[BLOCK:]
            grad_ref[mine, lanes] = turned_back(query_grad, cos_ref[mine, :], sin_ref[mine, :]).astype(BF)
        finish(slice(blocks[0] * BLOCK - HALF, (blocks[-1] + 1) * BLOCK - HALF))

    tail = SPAN - HALF
    sum_ref[count - tail : count - HALF, :] += edge_sum_ref[0, 1, 0:BLOCK, :]
    finish(slice(count - tail, count - HALF))


def inner_back(group, marks, qkv, mixed_grad, logs, cosine, sine, edge_grad, edge_sum, after):
    count = qkv.shape[1]
    return pl.pallas_call(
        inner_back_kernel,
        grid_spec=pltpu.PrefetchScalarGridSpec(
            num_scalar_prefetch=1,
            grid=(1,),
            in_specs=[
                SMEM,
                pl.BlockSpec((count, GROUP), lambda i, g: (0, g[0])),
                pl.BlockSpec((count // BLOCK, 1, 8, 2 * BLOCK), lambda i, g: (0, g[0], 0, 0)),
                pl.BlockSpec((count, LANES), lambda i, g: (0, 0)),
                pl.BlockSpec((count, LANES), lambda i, g: (0, 0)),
                pl.BlockSpec((1, 2, BLOCK, GROUP), lambda i, g: (g[0], 0, 0, 0)),
                pl.BlockSpec((1, 2, SPAN, 2 * GROUP), lambda i, g: (g[0], 0, 0, 0)),
                pl.BlockSpec((1, count, QKV_HALF), lambda i, g: (g[0], 0, 0)),
                *[ANY for _ in after],
            ],
            out_specs=pl.BlockSpec((count, QKV_HALF), lambda i, g: (0, 0)),
            scratch_shapes=[
                pltpu.VMEM((count, 2 * GROUP), F32),
            ],
        ),
        out_shape=jax.ShapeDtypeStruct((count, QKV_HALF), BF),
        compiler_params=params(8),
        cost_estimate=COST,
        name="inner_back",
    )(
        jnp.reshape(group, (1,)).astype(jnp.int32),
        marks,
        mixed_grad,
        logs,
        cosine,
        sine,
        edge_grad,
        edge_sum,
        qkv,
        *after,
    )


def patch_kernel(
    group_ref, cos_ref, sin_ref, edge_sum_ref, lower_ref, upper_ref, _, out_ref, edge_ref, sems
):
    group = group_ref[0]
    count = out_ref.shape[0]
    copies = []
    for side, (place, own, halo_ref) in enumerate(
        ((0, HALF, lower_ref), (count - HALF, BLOCK, upper_ref))
    ):
        total = edge_sum_ref[group, side, own : own + HALF, :] + halo_ref[group].astype(F32)
        cosine = cos_ref[place : place + HALF, :]
        sine = sin_ref[place : place + HALF, :]
        for sub in range(GROUP_PAIRS):
            lanes = slice(sub * LANES, (sub + 1) * LANES)
            edge_ref[side, :, lanes] = turned_back(total[:, lanes], cosine, sine).astype(BF)
        edge_ref[side, :, GROUP:] = total[:, GROUP:].astype(BF)
        copies.append(
            pltpu.make_async_copy(
                edge_ref.at[side],
                out_ref.at[pl.ds(place, HALF), pl.ds(GROUP, 2 * GROUP)],
                sems.at[side],
            )
        )
    for copy in copies:
        copy.start()
    for copy in copies:
        copy.wait()


def patch(group, cosine, sine, edge_sum, from_lower, from_upper, grads):
    return pl.pallas_call(
        patch_kernel,
        in_specs=[SMEM, *[VMEM] * 5, ANY],
        out_specs=ANY,
        out_shape=jax.ShapeDtypeStruct(grads.shape, BF),
        input_output_aliases={6: 0},
        scratch_shapes=[pltpu.VMEM((2, HALF, 2 * GROUP), BF), pltpu.SemaphoreType.DMA((2,))],
        compiler_params=params(8),
        cost_estimate=COST,
        name="patch",
    )(
        jnp.reshape(group, (1,)).astype(jnp.int32),
        cosine,
        sine,
        edge_sum,
        from_lower,
        from_upper,
        grads,
    )


def input_grad_kernel(count, order_ref, x_ref, gains_ref, first_ref, second_ref, grad_ref, *refs):
    weight_refs = refs[:count]
    out_ref, w_ref, sems = refs[count:]

    @pl.when(pl.program_id(0) == 0)
    def _():
        load_weights(weight_refs, w_ref, sems)

    unit, scale = normalized(x_ref[...].astype(F32))
    half = order_ref[0]
    grad_normed = dot(first_ref[...], w_ref[half, :, :QKV_HALF], 1, 1) + dot(
        second_ref[...], w_ref[1 - half, :, :QKV_HALF], 1, 1
    )
    out_ref[...] = grad_ref[...] + norm_back(grad_normed, unit, scale, gains_ref[0:1, :])


def input_grad(half, tokens, gains, weights, first, second, grad):
    count = tokens.shape[0]
    size = min(256, count)
    operands = weights.operands()
    return pl.pallas_call(
        partial(input_grad_kernel, len(operands)),
        grid=(count // size,),
        in_specs=[
            SMEM,
            rows((size, D)),
            whole((16, D)),
            rows((size, QKV_HALF)),
            rows((size, QKV_HALF)),
            rows((size, D)),
            *weights.specs(),
        ],
        out_specs=rows((size, D)),
        out_shape=jax.ShapeDtypeStruct((count, D), F32),
        scratch_shapes=weights.scratch(),
        compiler_params=params(12),
        cost_estimate=COST,
        name="input_grad",
    )(jnp.reshape(half, (1,)).astype(jnp.int32), tokens, gains, first, second, grad, *operands)


TILE = 256


def store_slots(slots_ref, out_ref, product):
    step = CHIP_ROWS
    for index in range(D // step):
        place = pl.multiple_of(slots_ref[1 + index] * step, 16)
        out_ref[pl.ds(place, step), :] = product[index * step : (index + 1) * step].astype(BF)


def weight_products(slots_ref, out_ref, turned, grad_ref, first, size):
    for tile in range(0, size, TILE):
        width = min(TILE, size - tile)
        product = dot(turned, grad_ref[:, tile : tile + width])
        for index in range(D // CHIP_ROWS):
            place = pl.multiple_of(slots_ref[1 + index] * CHIP_ROWS, 16)
            out_ref[pl.ds(place, CHIP_ROWS), first + tile : first + tile + width] = product[
                index * CHIP_ROWS : (index + 1) * CHIP_ROWS
            ].astype(BF)


def mixed_weight_kernel(slots_ref, normed_ref, grad_ref, mixed_ref, low_ref, *rest):
    out_ref = rest[-1]
    weight_products(slots_ref, out_ref, normed_ref[...].T, grad_ref, 0, QKV_HALF)
    lanes = pl.ds(pl.multiple_of(slots_ref[0] * GROUP, LANES), GROUP)
    weight_products(slots_ref, out_ref, mixed_ref[...].T, low_ref.at[:, lanes], QKV_HALF, GROUP)


def mixed_weight_grad(slots, normed, dqkv, mixed, low, after=()):
    count = normed.shape[0]
    return pl.pallas_call(
        mixed_weight_kernel,
        in_specs=[SMEM, *[VMEM] * 4, *[ANY for _ in after]],
        out_specs=VMEM,
        out_shape=jax.ShapeDtypeStruct((D, MIXED_HALF), BF),
        compiler_params=params(8),
        cost_estimate=COST,
        name="mixed_weight_grad",
    )(slots, normed, dqkv, mixed, low, *after)


def ff_weight_kernel(slots_ref, normed_ref, cot_ref, both_ref, hidden_ref, *rest):
    out_ref = rest[-1]

    @pl.when(slots_ref[0] == 0)
    def _():
        left = both_ref.at[:, 0:FF_HALF]
        weight_products(slots_ref, out_ref, normed_ref[...].T, left, 0, FF_HALF)

    @pl.when(slots_ref[0] == 1)
    def _():
        left = both_ref.at[:, FF_HALF : 2 * FF]
        weight_products(slots_ref, out_ref, normed_ref[...].T, left, 0, FF_LEFT)
        weight_products(slots_ref, out_ref, cot_ref[...].T, hidden_ref, FF_LEFT, FF)
        out_ref[:, FF_LEFT + FF :] = jnp.zeros((D, FF_HALF - FF_LEFT - FF), BF)


def ff_weight_grad(slots, normed, cot, both, hidden, after):
    count = normed.shape[0]
    return pl.pallas_call(
        ff_weight_kernel,
        in_specs=[SMEM, *[VMEM] * 4, *[ANY for _ in after]],
        out_specs=VMEM,
        out_shape=jax.ShapeDtypeStruct((D, FF_HALF), BF),
        compiler_params=params(8),
        cost_estimate=COST,
        name="ff_weight_grad",
    )(slots, normed, cot, both, hidden, *after)


def join_kernel(*refs):
    out_ref = refs[-1]
    first = 0
    for ref in refs[:-1]:
        out_ref[first : first + ref.shape[0], :] = ref[...]
        first += ref.shape[0]


def join(*parts):
    count = sum(part.shape[0] for part in parts)
    width = parts[0].shape[1]
    return pl.pallas_call(
        join_kernel,
        in_specs=[VMEM for _ in parts],
        out_specs=VMEM,
        out_shape=jax.ShapeDtypeStruct((count, width), parts[0].dtype),
        compiler_params=params(8),
        cost_estimate=COST,
        name="join",
    )(*parts)


def doc_marks(doc_lengths, row_count):
    me = lax.axis_index("tok")
    ends = jnp.cumsum(doc_lengths).astype(jnp.int32)
    before = jnp.where(me > 0, ends[jnp.maximum(me - 1, 0)], 0)
    return jnp.stack([before, ends[me], ends[me + 1], me * row_count]).astype(jnp.int32)


def rotary_tables(marks, row_count):
    place = marks[3] + jnp.arange(row_count, dtype=jnp.int32)
    offset = place - jnp.where(place >= marks[1], marks[1], marks[0])
    frequency = 10000.0 ** (-jnp.arange(0, HEAD_DIM, 2, dtype=F32) / HEAD_DIM)
    angles = offset.astype(F32)[:, None] * frequency[None, :]
    cosine = jnp.cos(angles)
    sine = jnp.sin(angles)
    return (
        jnp.concatenate([cosine] * 4, axis=1),
        jnp.concatenate([-sine, sine, -sine, sine], axis=1),
    )


def passed_along(value, steps):
    count = lax.axis_size("tok")
    first, last = (max(0, -steps), min(count, count - steps))
    return lax.ppermute(value, "tok", [(at, at + steps) for at in range(first, last)])


STAGED_DEVICES = 32


def staged():
    return lax.axis_size("tok") == STAGED_DEVICES


def exchange(value, by_core):
    pairs = [(at, at ^ by_core[at & 1]) for at in range(lax.axis_size("tok"))]
    return lax.ppermute(value, "tok", pairs)


CORE = (1, 1)
DEEP = tuple((step << 3, step << 3) for step in range(4))
NEAR = (2, 4)
FAR = (4, 2)


def slot_codes(core):
    slot = jnp.arange(16, dtype=jnp.int32)
    depth, near, far = (slot & 3, (slot >> 2) & 1, slot >> 3)
    return (depth << 2) | jnp.where(core == 0, (far << 1) | near, (near << 1) | far)


def chip_slots(chip, core):
    code = jnp.arange(16, dtype=jnp.int32) ^ chip
    depth, second, first = (code >> 2, (code >> 1) & 1, code & 1)
    return depth | jnp.where(core == 0, (second << 3) | (first << 2), (first << 3) | (second << 2))


def stage_after(value, *others):
    return lax.optimization_barrier((value, *others))[0]


def in_hbm(value):
    return pltpu.with_memory_space_constraint(value, pltpu.HBM)


def core_pieces(shard):
    core = lax.axis_index("tok") & 1
    half = shard.shape[1] // 2
    keep = jnp.where(core == 0, shard[:, :half], shard[:, half:])
    send = jnp.where(core == 0, shard[:, half:], shard[:, :half])
    came = exchange(send, CORE)
    return jnp.concatenate(
        [jnp.where(core == 0, keep, came), jnp.where(core == 0, came, keep)], axis=0
    )


def final_gather(held, far):
    me = lax.axis_index("tok")
    core = me & 1
    chip = me >> 1
    places = jnp.concatenate(
        [slot_codes(core) ^ chip, slot_codes(1 - core) ^ chip, jnp.full((1,), core, jnp.int32)]
    )
    return Weights([held, far, exchange(held, CORE), exchange(far, CORE)], places)


def whole_weights(shard):
    full = lax.all_gather(shard, "tok", axis=0, tiled=True)
    half = full.shape[1] // 2
    return Weights([jnp.stack([full[:, :half], full[:, half:]])])


def added(left, right):
    return (left.astype(F32) + right.astype(F32)).astype(BF)


def core_sum(keep, came):
    return added(keep[:384], came[:384]), added(keep[384:], came[384:])


def far_sum(near, came):
    return added(near[:192], came[:192]), added(near[192:], came[192:])


def near_sum(near, came):
    return [
        added(near[first : first + CHIP_ROWS], came[first : first + CHIP_ROWS])
        for first in range(0, 192, CHIP_ROWS)
    ]


def deep_sum(parts, *after):
    core = lax.axis_index("tok") & 1
    total = parts[0].astype(F32)
    for step in (1, 2, 3):
        total = total + stage_after(exchange(parts[step], DEEP[step]), after[step - 1]).astype(F32)
    share = CHIP_ROWS // 2
    lower, upper = (total[:share], total[share:])
    own = jnp.where(core == 0, lower, upper)
    came = exchange(jnp.where(core == 0, upper, lower), CORE)
    return jnp.concatenate(
        [jnp.where(core == 0, own, came), jnp.where(core == 0, came, own)], axis=1
    )


def summed(keep, send):
    full = jnp.concatenate([keep, send], axis=1)
    return lax.psum_scatter(full.astype(F32), "tok", scatter_dimension=0, tiled=True)


def by_part(groups):
    return jnp.concatenate(
        [
            groups[:, half * MIXED_HALF + part * GROUP : half * MIXED_HALF + (part + 1) * GROUP]
            for part in range(3)
            for half in range(2)
        ],
        axis=1,
    )


def on_device(
    tokens,
    doc_lengths,
    first_gain,
    qkv_weight,
    attn_weight,
    second_gain,
    feed_in_weight,
    feed_out_weight,
    cotangent,
):
    row_count = tokens.shape[0]
    share = first_gain.shape[0]

    def spread(gain):
        return jnp.broadcast_to(gain[:, None], (share, LANES))

    def group_of(half):
        return [
            qkv_weight[:, part * D + half * GROUP : part * D + (half + 1) * GROUP]
            for part in range(3)
        ]

    shard_one = jnp.concatenate(
        [*group_of(0), spread(first_gain), *group_of(1), spread(second_gain)], axis=1
    )
    shard_two = jnp.concatenate([feed_in_weight, feed_out_weight.T, attn_weight], axis=1)
    weights_two = lax.all_gather(shard_two, "tok", axis=0, tiled=True)
    if staged():
        piece = core_pieces(shard_one)
        marks = doc_marks(stage_after(doc_lengths, piece), row_count)
        cosine, sine = rotary_tables(marks, row_count)
        came = [exchange(piece, DEEP[step]) for step in (1, 2, 3)]
        *came, marks = lax.optimization_barrier((*came, marks, cosine, sine))[:4]
        one = join(piece, *came)
        one = join(one, exchange(one, NEAR))
        weights_one = final_gather(one, exchange(one, FAR))
    else:
        marks = doc_marks(doc_lengths, row_count)
        cosine, sine = rotary_tables(marks, row_count)
        weights_one = whole_weights(shard_one)
    normed, qkv, gains = project_qkv(tokens, weights_one, in_hbm(cosine), in_hbm(sine))
    lower = passed_along(qkv[:, row_count - HALF :, GROUP:], 1)
    upper = passed_along(qkv[:, :HALF, GROUP:], -1)
    mixed, logs = attend_inner(marks, qkv)
    mixed, edge_logs = attend_edges(marks, qkv, lower, upper, mixed)
    residual, normed_two, both, hidden = dense(tokens, in_hbm(mixed), cotangent, gains, in_hbm(weights_two))
    me = lax.axis_index("tok")
    if staged():
        halves = (1 - (me & 1), me & 1)
    else:
        halves = (jnp.int32(1), jnp.int32(0))

    def order(half):
        if staged():
            slots = chip_slots(me >> 1, half)
        else:
            slots = jnp.arange(D // CHIP_ROWS, dtype=jnp.int32)
        return jnp.concatenate([jnp.reshape(half, (1,)).astype(jnp.int32), slots])

    def ff_grad(half, after):
        return ff_weight_grad(order(half), normed_two, cotangent, both, hidden, after)

    def inner(half, after):
        return inner_back(
            half, marks, qkv, mixed_grad, logs, cosine, sine, edge_grad, edge_sum, after
        )

    def patched(half, grads):
        return patch(half, cosine, sine, edge_sum, from_lower, from_upper, grads)

    def finish(first, second):
        return input_grad(halves[0], tokens, gains, weights_one, first, second, grad)

    send, keep = halves
    def mixed_weight(half, dqkv):
        return mixed_weight_grad(order(half), normed, dqkv, mixed, low)

    ff_send = ff_grad(send, [])
    ff_keep = ff_grad(keep, [ff_send])
    low, mixed_grad, grad = dense_back(residual, cotangent, both, gains, weights_two, [ff_keep])
    if staged():
        near, far = core_sum(ff_keep, stage_after(exchange(ff_send, CORE), mixed_grad))
        mixed_grad = stage_after(mixed_grad, far)
    edge_grad, edge_sum, away = edge_back(marks, qkv, mixed_grad, edge_logs, cosine, sine, lower, upper)
    from_upper = passed_along(away[0], -1)
    from_lower = passed_along(away[1], 1)

    if staged():
        first = inner(send, [])
        from_lower, from_upper, first = lax.optimization_barrier((from_lower, from_upper, first))
        near, far = far_sum(near, stage_after(exchange(far, FAR), from_lower, from_upper))
        first = patched(send, stage_after(first, far))
        mixed_send = mixed_weight(send, first)
        second = inner(keep, [mixed_send])
        parts = near_sum(near, stage_after(exchange(far, NEAR), second))
        second = patched(keep, stage_after(second, *parts))
        mixed_keep = mixed_weight(keep, second)
        mixed_near, mixed_far = core_sum(mixed_keep, exchange(stage_after(mixed_send, second), CORE))
        grad_in = finish(first, stage_after(second, mixed_far))
        mixed_near, mixed_far = far_sum(mixed_near, stage_after(exchange(mixed_far, FAR), grad_in))
        sum_ff = deep_sum(parts, *[mixed_far] * 3)
        result = result_of(residual, hidden, weights_two, [mixed_far])
        mixed_parts = near_sum(mixed_near, stage_after(exchange(mixed_far, NEAR), result))
        sum_mixed = deep_sum(mixed_parts, *[mixed_parts[0]] * 3)
    else:
        first = patched(send, inner(send, []))
        second = patched(keep, inner(keep, []))
        result = result_of(residual, hidden, weights_two, [])
        grad_in = finish(first, second)
        sum_ff = summed(ff_keep, ff_send)
        sum_mixed = summed(mixed_weight(keep, second), mixed_weight(send, first))
    sum_qkv = by_part(sum_mixed)
    sent_attn = jnp.concatenate(
        [sum_mixed[:, QKV_HALF:MIXED_HALF], sum_mixed[:, MIXED_HALF + QKV_HALF :]], axis=1
    )
    sent_in = jnp.concatenate(
        [sum_ff[:, :FF_HALF], sum_ff[:, FF_HALF : FF_HALF + FF_LEFT]], axis=1
    )
    sent_down = sum_ff[:, FF_HALF + FF_LEFT : FF_HALF + FF_LEFT + FF].T

    def gain_grad(summed, weight, gain):
        return jnp.sum(summed * weight.astype(F32), axis=1) / gain.astype(F32)

    return (
        result,
        grad_in,
        gain_grad(sum_qkv, qkv_weight, first_gain),
        sum_qkv,
        sent_attn,
        gain_grad(sent_in, feed_in_weight, second_gain),
        sent_in,
        sent_down,
    )


def solution(mesh):
    in_specs = (
        P("tok", None),
        P(),
        P("tok"),
        P("tok", None),
        P("tok", None),
        P("tok"),
        P("tok", None),
        P(None, "tok"),
        P("tok", None),
    )
    out_specs = (
        P("tok", None),
        P("tok", None),
        P("tok"),
        P("tok", None),
        P("tok", None),
        P("tok"),
        P("tok", None),
        P(None, "tok"),
    )
    return jax.shard_map(
        on_device, mesh=mesh, in_specs=in_specs, out_specs=out_specs, check_vma=False
    )
```

```python
from functools import partial

import jax
import jax.numpy as jnp
from jax import lax
from jax.experimental import pallas as pl
from jax.experimental.pallas import tpu as pltpu
from jax.sharding import PartitionSpec as P

D = 768
FF = 1152
HEADS = 12
HEAD_DIM = 64
HALF = 64
PAIRS = HEADS // 2
BLOCK = 128
SPAN = BLOCK + 2 * HALF
LANES = 128
QKV_HALF = 3 * D // 2
GROUP = D // 2
GROUP_PAIRS = PAIRS // 2
FF_HALF = 1792
FF_LEFT = 2 * FF - FF_HALF
MIXED_HALF = QKV_HALF + GROUP
MIB = 1024 * 1024
BF = jnp.bfloat16
F32 = jnp.float32


def dot(left, right, left_dim=1, right_dim=0):
    return lax.dot_general(
        left, right, (((left_dim,), (right_dim,)), ((), ())), preferred_element_type=F32
    )


def params(mib):
    return pltpu.CompilerParams(vmem_limit_bytes=mib * MIB)


def whole(shape):
    return pl.BlockSpec(shape, lambda *_: (0,) * len(shape))


def rows(shape):
    return pl.BlockSpec(shape, lambda i: (i,) + (0,) * (len(shape) - 1))


COST = pl.CostEstimate(flops=4000000000, bytes_accessed=1000, transcendentals=0)
SMEM = pl.BlockSpec(memory_space=pltpu.SMEM)
ANY = pl.BlockSpec(memory_space=pl.ANY)
VMEM = pl.BlockSpec(memory_space=pltpu.VMEM)
HBM = pl.BlockSpec(memory_space=pltpu.HBM)
HBM = pl.BlockSpec(memory_space=pltpu.HBM)


def lane_ids(shape):
    return lax.broadcasted_iota(jnp.int32, shape, len(shape) - 1)


def swap_halves(values):
    low = (lane_ids(values.shape) & (HEAD_DIM - 1)) < HEAD_DIM // 2
    return jnp.where(
        low, pltpu.roll(values, LANES - HEAD_DIM // 2, 1), pltpu.roll(values, HEAD_DIM // 2, 1)
    )


def normalized(values):
    centered = values - jnp.mean(values, axis=-1, keepdims=True)
    scale = lax.rsqrt(jnp.mean(centered * centered, axis=-1, keepdims=True) + 1e-05)
    return centered * scale, scale


def norm_back(grad, unit, scale, gains):
    grad_unit = grad * gains
    return scale * (
        grad_unit
        - jnp.mean(grad_unit, axis=-1, keepdims=True)
        - unit * jnp.mean(grad_unit * unit, axis=-1, keepdims=True)
    )


CHIP_ROWS = 48


class Weights:
    def __init__(self, arrays, places=None):
        self.arrays = arrays
        self.places = places

    def operands(self):
        if self.places is None:
            return list(self.arrays)
        return [self.places, *self.arrays]

    def specs(self):
        if self.places is None:
            return [ANY]
        return [SMEM, VMEM, VMEM, VMEM, VMEM]

    def scratch(self):
        width = self.arrays[0].shape[-1]
        return [pltpu.VMEM((2, D, width), BF), pltpu.SemaphoreType.DMA((1,))]


def load_weights(refs, out_ref, sems):
    if len(refs) == 1:
        copy = pltpu.make_async_copy(refs[0], out_ref, sems.at[0])
        copy.start()
        copy.wait()
        return
    places_ref = refs[0]
    core = places_ref[32]
    for index, source in enumerate(refs[1:]):
        half = core if index < 2 else 1 - core
        for slot in range(8):
            place = pl.multiple_of(places_ref[index * 8 + slot] * CHIP_ROWS, 16)
            out_ref[half, pl.ds(place, CHIP_ROWS), :] = source[
                slot * CHIP_ROWS : (slot + 1) * CHIP_ROWS, :
            ]


def qkv_kernel(count, x_ref, cos_ref, sin_ref, *refs):
    weight_refs = refs[:count]
    normed_ref, qkv_ref, gains_ref, w_ref, sems = refs[count:]

    @pl.when(pl.program_id(0) == 0)
    def _():
        load_weights(weight_refs, w_ref, sems)
        for half in range(2):
            turned = w_ref[half, :, QKV_HALF:].T.astype(F32)
            gains_ref[half * 8 : half * 8 + 8, :] = turned[:8]

    unit, _ = normalized(x_ref[...].astype(F32))
    normed = (unit * gains_ref[0:1, :]).astype(BF)
    normed_ref[...] = normed
    cosine = cos_ref[...]
    sine = sin_ref[...]
    for half in range(2):
        merged = dot(normed, w_ref[half, :, :QKV_HALF])
        for tile in range(QKV_HALF // LANES):
            lanes = slice(tile * LANES, (tile + 1) * LANES)
            part = merged[:, lanes]
            if tile * LANES < 2 * GROUP:
                part = part * cosine + swap_halves(part) * sine
            qkv_ref[half, :, lanes] = part.astype(BF)


def project_qkv(tokens, weights, cosine, sine):
    count = tokens.shape[0]
    size = min(256, count)
    operands = weights.operands()
    return pl.pallas_call(
        partial(qkv_kernel, len(operands)),
        grid=(count // size,),
        in_specs=[rows((size, D)), rows((size, LANES)), rows((size, LANES)), *weights.specs()],
        out_specs=[
            rows((size, D)),
            pl.BlockSpec((2, size, QKV_HALF), lambda i: (0, i, 0)),
            whole((16, D)),
        ],
        out_shape=[
            jax.ShapeDtypeStruct((count, D), BF),
            jax.ShapeDtypeStruct((2, count, QKV_HALF), BF),
            jax.ShapeDtypeStruct((16, D), F32),
        ],
        scratch_shapes=weights.scratch(),
        compiler_params=params(12),
        cost_estimate=COST,
        name="qkv",
    )(tokens, cosine, sine, *operands)


def window_bias(marks_ref, block):
    shape = (SPAN, 2 * BLOCK)
    first = marks_ref[3] + block * BLOCK
    key = lax.broadcasted_iota(jnp.int32, shape, 0)
    query = lax.broadcasted_iota(jnp.int32, (1, 2 * BLOCK), 1) & (BLOCK - 1)
    place = first + query
    lowest = query
    highest = query + 2 * HALF
    for index in range(3):
        mark = marks_ref[index]
        edge = mark - first + HALF
        past = place >= mark
        lowest = jnp.where(past, jnp.maximum(lowest, edge), lowest)
        highest = jnp.where(past, highest, jnp.minimum(highest, edge - 1))
    return jnp.where((key >= lowest) & (key <= highest), 0.0, -1e30).astype(F32)


def stacked(pair):
    low = lane_ids(pair.shape) < HEAD_DIM
    zero = jnp.zeros_like(pair)
    return jnp.concatenate([jnp.where(low, pair, zero), jnp.where(low, zero, pair)], axis=0)


def unstacked(both):
    low = lane_ids((BLOCK, LANES)) < HEAD_DIM
    return jnp.where(low, both[:BLOCK], both[BLOCK:])


def span_of(qkv_ref, lower_ref, upper_ref, half, block, part, sub):
    count = qkv_ref.shape[1]
    first = block * BLOCK - HALF
    lanes = slice(part * GROUP + sub * LANES, part * GROUP + (sub + 1) * LANES)
    halo_lanes = slice((part - 1) * GROUP + sub * LANES, (part - 1) * GROUP + (sub + 1) * LANES)
    own = qkv_ref[half, max(first, 0) : min(first + SPAN, count), lanes]
    if first < 0:
        own = jnp.concatenate([lower_ref[half, :, halo_lanes], own], axis=0)
    if first + SPAN > count:
        own = jnp.concatenate([own, upper_ref[half, :, halo_lanes]], axis=0)
    return own


def many_attend(operands):
    scores = [dot(keys, query, 1, 1) + bias for query, keys, _, bias in operands]
    peaks = [jnp.max(score, axis=0, keepdims=True) for score in scores]
    expos = [jnp.exp(score - peak) for score, peak in zip(scores, peaks)]
    totals = [jnp.sum(expo, axis=0, keepdims=True) for expo in expos]
    weights = [(expo * (1.0 / total)).astype(BF) for expo, total in zip(expos, totals)]
    mixed = [unstacked(dot(weight, item[2], 0, 0)) for weight, item in zip(weights, operands)]
    return [(mix, peak + jnp.log(total)) for mix, peak, total in zip(mixed, peaks, totals)]


def attend_blocks(marks_ref, qkv_ref, lower_ref, upper_ref, blocks, store):
    for block in blocks:
        bias = window_bias(marks_ref, block)
        mine = slice(block * BLOCK, (block + 1) * BLOCK)
        for first in range(0, PAIRS, PAIRS_TOGETHER):
            pairs = range(first, first + PAIRS_TOGETHER)
            items = []
            for pair in pairs:
                half, sub = divmod(pair, GROUP_PAIRS)
                where = (qkv_ref, lower_ref, upper_ref, half, block)
                items.append(
                    (
                        stacked(qkv_ref[half, mine, sub * LANES : (sub + 1) * LANES] * BF(0.125)),
                        span_of(*where, 1, sub),
                        span_of(*where, 2, sub),
                        bias,
                    )
                )
            for pair, (mix, logs) in zip(pairs, many_attend(items)):
                store(block, pair, mix.astype(BF), logs)


def attend_inner_kernel(marks_ref, qkv_ref, out_ref, log_ref):
    def store(block, pair, mix, logs):
        half, sub = divmod(pair, GROUP_PAIRS)
        out_ref[block * BLOCK : (block + 1) * BLOCK, pair * LANES : (pair + 1) * LANES] = mix
        log_ref[block, half, sub : sub + 1, :] = logs

    blocks = range(1, qkv_ref.shape[1] // BLOCK - 1)
    attend_blocks(marks_ref, qkv_ref, None, None, blocks, store)


def attend_inner(marks, qkv):
    count = qkv.shape[1]
    return pl.pallas_call(
        attend_inner_kernel,
        in_specs=[SMEM, VMEM],
        out_specs=[VMEM, VMEM],
        out_shape=[
            jax.ShapeDtypeStruct((count, D), BF),
            jax.ShapeDtypeStruct((count // BLOCK, 2, 8, 2 * BLOCK), F32),
        ],
        compiler_params=params(8),
        cost_estimate=COST,
        name="attend_inner",
    )(marks, qkv)


def attend_edges_kernel(marks_ref, qkv_ref, lower_ref, upper_ref, _, out_ref, log_ref, edge_ref, sems):
    count = qkv_ref.shape[1]
    last = count // BLOCK - 1

    def store(block, pair, mix, logs):
        half, sub = divmod(pair, GROUP_PAIRS)
        side = min(block, 1)
        edge_ref[side, :, pair * LANES : (pair + 1) * LANES] = mix
        log_ref[side, half, sub : sub + 1, :] = logs

    attend_blocks(marks_ref, qkv_ref, lower_ref, upper_ref, (0, last), store)
    copies = [
        pltpu.make_async_copy(
            edge_ref.at[side], out_ref.at[pl.ds(block * BLOCK, BLOCK)], sems.at[side]
        )
        for side, block in enumerate((0, last))
    ]
    for copy in copies:
        copy.start()
    for copy in copies:
        copy.wait()


def attend_edges(marks, qkv, lower, upper, mixed):
    return pl.pallas_call(
        attend_edges_kernel,
        in_specs=[SMEM, VMEM, VMEM, VMEM, ANY],
        out_specs=[ANY, VMEM],
        out_shape=[
            jax.ShapeDtypeStruct(mixed.shape, BF),
            jax.ShapeDtypeStruct((2, 2, 8, 2 * BLOCK), F32),
        ],
        input_output_aliases={4: 0},
        scratch_shapes=[pltpu.VMEM((2, BLOCK, D), BF), pltpu.SemaphoreType.DMA((2,))],
        compiler_params=params(8),
        cost_estimate=COST,
        name="attend_edges",
    )(marks, qkv, lower, upper, mixed)


PAIRS_TOGETHER = 1
FF_PARTS = tuple((first, min(256, FF - first)) for first in range(0, FF, 256))


def dense_kernel(
    x_ref,
    mixed_ref,
    cot_ref,
    gains_ref,
    source_ref,
    residual_ref,
    normed_ref,
    both_ref,
    hidden_ref,
    near_ref,
    w_ref,
    sems,
):
    ranges = [(3 * FF, D), (0, 3 * FF)]
    fetch = pltpu.make_async_copy(mixed_ref, near_ref, sems.at[2])
    fetch.start()
    copies = [
        pltpu.make_async_copy(
            source_ref.at[:, pl.ds(first, size)], w_ref.at[:, pl.ds(first, size)], sems.at[index]
        )
        for index, (first, size) in enumerate(ranges)
    ]
    for copy in copies:
        copy.start()
    fetch.wait()
    copies[0].wait()
    count = x_ref.shape[0]
    size = min(512, count)
    blocks = [slice(first, first + size) for first in range(0, count, size)]
    for mine in blocks:
        residual = x_ref[mine, :].astype(F32) + dot(near_ref[mine, :], w_ref[:, 3 * FF :])
        residual_ref[mine, :] = residual
        unit, _ = normalized(residual)
        normed_ref[mine, :] = (unit * gains_ref[8:9, :]).astype(BF)
    copies[1].wait()
    for mine in blocks:
        normed = normed_ref[mine, :]
        cot = cot_ref[mine, :]
        for first, size in FF_PARTS:
            gate_cols = slice(first, first + size)
            up_cols = slice(FF + first, FF + first + size)
            down_cols = slice(2 * FF + first, 2 * FF + first + size)
            gate = dot(normed, w_ref[:, gate_cols])
            up = dot(normed, w_ref[:, up_cols])
            grad_hidden = dot(cot, w_ref[:, down_cols])
            share = 0.5 + 0.5 * lax.erf(gate * 0.7071067811865476)
            active = gate * share
            slope = share + gate * (jnp.exp(-0.5 * gate * gate) * 0.3989422804014327)
            hidden_ref[mine, gate_cols] = (active * up).astype(BF)
            both_ref[mine, gate_cols] = (grad_hidden * up * slope).astype(BF)
            both_ref[mine, up_cols] = (grad_hidden * active).astype(BF)


def dense(tokens, mixed, cotangent, gains, weights):
    count = tokens.shape[0]
    wide = [(D, F32), (D, BF), (2 * FF, BF), (FF, BF)]
    return pl.pallas_call(
        dense_kernel,
        in_specs=[VMEM, HBM, VMEM, VMEM, HBM],
        out_specs=[VMEM] * 4,
        out_shape=[jax.ShapeDtypeStruct((count, width), kind) for width, kind in wide],
        scratch_shapes=[
            pltpu.VMEM((count, D), BF),
            pltpu.VMEM(weights.shape, BF),
            pltpu.SemaphoreType.DMA((3,)),
        ],
        compiler_params=params(12),
        cost_estimate=COST,
        name="dense",
    )(tokens, mixed, cotangent, gains, weights)


def dense_back_kernel(residual_ref, cot_ref, both_ref, gains_ref, w_ref, *rest):
    low_ref, mixed_grad_ref, grad_ref = rest[-3:]
    count = residual_ref.shape[0]
    size = min(512, count)
    for first in range(0, count, size):
        mine = slice(first, first + size)
        unit, scale = normalized(residual_ref[mine, :])
        grad_normed = dot(both_ref[mine, :], w_ref[:, : 2 * FF], 1, 1)
        grad = cot_ref[mine, :].astype(F32) + norm_back(
            grad_normed, unit, scale, gains_ref[8:9, :]
        )
        grad_ref[mine, :] = grad
        low = grad.astype(BF)
        low_ref[mine, :] = low
        mixed_grad_ref[mine, :] = dot(low, w_ref[:, 3 * FF :], 1, 1).astype(BF)


def dense_back(residual, cotangent, both, gains, weights, after):
    count = residual.shape[0]
    wide = [(D, BF), (D, BF), (D, F32)]
    return pl.pallas_call(
        dense_back_kernel,
        in_specs=[*[VMEM] * 5, *[ANY for _ in after]],
        out_specs=[VMEM] * 3,
        out_shape=[jax.ShapeDtypeStruct((count, width), kind) for width, kind in wide],
        compiler_params=params(8),
        cost_estimate=COST,
        name="dense_back",
    )(residual, cotangent, both, gains, weights, *after)


def result_kernel(residual_ref, hidden_ref, w_ref, *rest):
    product = dot(hidden_ref[...], w_ref[:, 2 * FF : 3 * FF], 1, 1)
    rest[-1][...] = (residual_ref[...] + product).astype(BF)


def result_of(residual, hidden, weights, after):
    count = residual.shape[0]
    size = min(512, count)
    return pl.pallas_call(
        result_kernel,
        grid=(count // size,),
        in_specs=[rows((size, D)), rows((size, FF)), whole(weights.shape), *[ANY for _ in after]],
        out_specs=rows((size, D)),
        out_shape=jax.ShapeDtypeStruct((count, D), BF),
        compiler_params=params(16),
        cost_estimate=COST,
        name="result",
    )(residual, hidden, weights, *after)


def pair_back(query, keys, values, out_grad, logs, bias):
    scores = dot(keys, query, 1, 1) + bias
    weights = jnp.exp(scores - logs)
    weight_grad = dot(values, out_grad, 1, 1)
    score_grad = weights * (weight_grad - jnp.sum(weights * weight_grad, axis=0, keepdims=True))
    score_grad = score_grad.astype(BF)
    key_grad = dot(score_grad, query)
    value_grad = dot(weights.astype(BF), out_grad)
    query_grad = unstacked(dot(score_grad, keys, 0, 0)) * 0.125
    return query_grad, key_grad, value_grad


def many_back(operands):
    scores = [dot(keys, query, 1, 1) for query, keys, _, _, _, _ in operands]
    weight_grads = [dot(values, out_grad, 1, 1) for _, _, values, out_grad, _, _ in operands]
    weights = [jnp.exp(score + item[5] - item[4]) for score, item in zip(scores, operands)]
    value_grads = [dot(weight.astype(BF), item[3]) for weight, item in zip(weights, operands)]
    score_grads = [
        (weight * (grad - jnp.sum(weight * grad, axis=0, keepdims=True))).astype(BF)
        for weight, grad in zip(weights, weight_grads)
    ]
    key_grads = [dot(grad, item[0]) for grad, item in zip(score_grads, operands)]
    query_grads = [
        unstacked(dot(grad, item[1], 0, 0)) * 0.125 for grad, item in zip(score_grads, operands)
    ]
    return list(zip(query_grads, key_grads, value_grads))


def turned_back(values, cosine, sine):
    return values * cosine - swap_halves(values) * sine


def edge_back_kernel(
    marks_ref,
    mixed_grad_ref,
    log_ref,
    cos_ref,
    sin_ref,
    qkv_ref,
    lower_ref,
    upper_ref,
    grad_ref,
    sum_ref,
    away_ref,
):
    count = qkv_ref.shape[1]
    for side, block in enumerate((0, count // BLOCK - 1)):
        bias = window_bias(marks_ref, block)
        mine = slice(block * BLOCK, (block + 1) * BLOCK)
        sent = slice(0, HALF) if side == 0 else slice(SPAN - HALF, SPAN)
        for half in range(2):
            items = []
            for sub in range(GROUP_PAIRS):
                pair = half * GROUP_PAIRS + sub
                where = (qkv_ref, lower_ref, upper_ref, half, block)
                items.append(
                    (
                        stacked(qkv_ref[half, mine, sub * LANES : (sub + 1) * LANES] * BF(0.125)),
                        span_of(*where, 1, sub),
                        span_of(*where, 2, sub),
                        stacked(mixed_grad_ref[mine, pair * LANES : (pair + 1) * LANES]),
                        log_ref[side, half, sub : sub + 1, :],
                        bias,
                    )
                )
            for sub, (query_grad, key_grad, value_grad) in enumerate(many_back(items)):
                lanes = slice(sub * LANES, (sub + 1) * LANES)
                value_lanes = slice(GROUP + sub * LANES, GROUP + (sub + 1) * LANES)
                grad_ref[half, side, :, lanes] = turned_back(
                    query_grad, cos_ref[mine, :], sin_ref[mine, :]
                ).astype(BF)
                sum_ref[half, side, :, lanes] = key_grad
                sum_ref[half, side, :, value_lanes] = value_grad
                away_ref[side, half, :, lanes] = key_grad[sent].astype(BF)
                away_ref[side, half, :, value_lanes] = value_grad[sent].astype(BF)


def edge_back(marks, qkv, mixed_grad, logs, cosine, sine, lower, upper):
    return pl.pallas_call(
        edge_back_kernel,
        in_specs=[SMEM, *[VMEM] * 7],
        out_specs=[VMEM, VMEM, VMEM],
        out_shape=[
            jax.ShapeDtypeStruct((2, 2, BLOCK, GROUP), BF),
            jax.ShapeDtypeStruct((2, 2, SPAN, 2 * GROUP), F32),
            jax.ShapeDtypeStruct((2, 2, HALF, 2 * GROUP), BF),
        ],
        compiler_params=params(8),
        cost_estimate=COST,
        name="edge_back",
    )(marks, mixed_grad, logs, cosine, sine, qkv, lower, upper)


TOGETHER = 1


def inner_back_kernel(
    group_ref,
    marks_ref,
    mixed_grad_ref,
    log_ref,
    cos_ref,
    sin_ref,
    edge_grad_ref,
    edge_sum_ref,
    qkv_ref,
    *rest,
):
    grad_ref, sum_ref = rest[-2:]
    count = qkv_ref.shape[1]
    inner = count // BLOCK - 2
    sum_ref[0 : SPAN - HALF, :] = edge_sum_ref[0, 0, HALF:, :]
    grad_ref[0:BLOCK, 0:GROUP] = edge_grad_ref[0, 0]
    grad_ref[count - BLOCK :, 0:GROUP] = edge_grad_ref[0, 1]

    def finish(place):
        own_cosine = cos_ref[place, :]
        own_sine = sin_ref[place, :]
        for sub in range(GROUP_PAIRS):
            lanes = slice(sub * LANES, (sub + 1) * LANES)
            key_lanes = slice(GROUP + sub * LANES, GROUP + (sub + 1) * LANES)
            grad_ref[place, key_lanes] = turned_back(
                sum_ref[place, lanes], own_cosine, own_sine
            ).astype(BF)
        grad_ref[place, 2 * GROUP :] = sum_ref[place, GROUP:].astype(BF)

    for first in range(1, inner + 1, TOGETHER):
        blocks = range(first, min(first + TOGETHER, inner + 1))
        places = []
        items = []
        for block in blocks:
            bias = window_bias(marks_ref, block)
            start = block * BLOCK - HALF
            window = slice(start, start + SPAN)
            mine = slice(block * BLOCK, (block + 1) * BLOCK)
            for sub in range(GROUP_PAIRS):
                lanes = slice(sub * LANES, (sub + 1) * LANES)
                places.append((mine, start, sub))
                items.append(
                    (
                        stacked(qkv_ref[0, mine, lanes] * BF(0.125)),
                        qkv_ref[0, window, GROUP + sub * LANES : GROUP + (sub + 1) * LANES],
                        qkv_ref[0, window, 2 * GROUP + sub * LANES : 2 * GROUP + (sub + 1) * LANES],
                        stacked(mixed_grad_ref[mine, lanes]),
                        log_ref[block, 0, sub : sub + 1, :],
                        bias,
                    )
                )
        for (mine, start, sub), (query_grad, key_grad, value_grad) in zip(places, many_back(items)):
            lanes = slice(sub * LANES, (sub + 1) * LANES)
            value_lanes = slice(GROUP + sub * LANES, GROUP + (sub + 1) * LANES)
            older = slice(start, start + BLOCK)
            newer = slice(start + BLOCK, start + SPAN)
            sum_ref[older, lanes] += key_grad[:BLOCK]
            sum_ref[newer, lanes] = key_grad[BLOCK:]
            sum_ref[older, value_lanes] += value_grad[:BLOCK]
            sum_ref[newer, value_lanes] = value_grad[BLOCK:]
            grad_ref[mine, lanes] = turned_back(query_grad, cos_ref[mine, :], sin_ref[mine, :]).astype(BF)
        finish(slice(blocks[0] * BLOCK - HALF, (blocks[-1] + 1) * BLOCK - HALF))

    tail = SPAN - HALF
    sum_ref[count - tail : count - HALF, :] += edge_sum_ref[0, 1, 0:BLOCK, :]
    finish(slice(count - tail, count - HALF))


def inner_back(group, marks, qkv, mixed_grad, logs, cosine, sine, edge_grad, edge_sum, after):
    count = qkv.shape[1]
    return pl.pallas_call(
        inner_back_kernel,
        grid_spec=pltpu.PrefetchScalarGridSpec(
            num_scalar_prefetch=1,
            grid=(1,),
            in_specs=[
                SMEM,
                pl.BlockSpec((count, GROUP), lambda i, g: (0, g[0])),
                pl.BlockSpec((count // BLOCK, 1, 8, 2 * BLOCK), lambda i, g: (0, g[0], 0, 0)),
                pl.BlockSpec((count, LANES), lambda i, g: (0, 0)),
                pl.BlockSpec((count, LANES), lambda i, g: (0, 0)),
                pl.BlockSpec((1, 2, BLOCK, GROUP), lambda i, g: (g[0], 0, 0, 0)),
                pl.BlockSpec((1, 2, SPAN, 2 * GROUP), lambda i, g: (g[0], 0, 0, 0)),
                pl.BlockSpec((1, count, QKV_HALF), lambda i, g: (g[0], 0, 0)),
                *[ANY for _ in after],
            ],
            out_specs=pl.BlockSpec((count, QKV_HALF), lambda i, g: (0, 0)),
            scratch_shapes=[
                pltpu.VMEM((count, 2 * GROUP), F32),
            ],
        ),
        out_shape=jax.ShapeDtypeStruct((count, QKV_HALF), BF),
        compiler_params=params(8),
        cost_estimate=COST,
        name="inner_back",
    )(
        jnp.reshape(group, (1,)).astype(jnp.int32),
        marks,
        mixed_grad,
        logs,
        cosine,
        sine,
        edge_grad,
        edge_sum,
        qkv,
        *after,
    )


def patch_kernel(
    group_ref, cos_ref, sin_ref, edge_sum_ref, lower_ref, upper_ref, _, out_ref, edge_ref, sems
):
    group = group_ref[0]
    count = out_ref.shape[0]
    copies = []
    for side, (place, own, halo_ref) in enumerate(
        ((0, HALF, lower_ref), (count - HALF, BLOCK, upper_ref))
    ):
        total = edge_sum_ref[group, side, own : own + HALF, :] + halo_ref[group].astype(F32)
        cosine = cos_ref[place : place + HALF, :]
        sine = sin_ref[place : place + HALF, :]
        for sub in range(GROUP_PAIRS):
            lanes = slice(sub * LANES, (sub + 1) * LANES)
            edge_ref[side, :, lanes] = turned_back(total[:, lanes], cosine, sine).astype(BF)
        edge_ref[side, :, GROUP:] = total[:, GROUP:].astype(BF)
        copies.append(
            pltpu.make_async_copy(
                edge_ref.at[side],
                out_ref.at[pl.ds(place, HALF), pl.ds(GROUP, 2 * GROUP)],
                sems.at[side],
            )
        )
    for copy in copies:
        copy.start()
    for copy in copies:
        copy.wait()


def patch(group, cosine, sine, edge_sum, from_lower, from_upper, grads):
    return pl.pallas_call(
        patch_kernel,
        in_specs=[SMEM, *[VMEM] * 5, ANY],
        out_specs=ANY,
        out_shape=jax.ShapeDtypeStruct(grads.shape, BF),
        input_output_aliases={6: 0},
        scratch_shapes=[pltpu.VMEM((2, HALF, 2 * GROUP), BF), pltpu.SemaphoreType.DMA((2,))],
        compiler_params=params(8),
        cost_estimate=COST,
        name="patch",
    )(
        jnp.reshape(group, (1,)).astype(jnp.int32),
        cosine,
        sine,
        edge_sum,
        from_lower,
        from_upper,
        grads,
    )


def input_grad_kernel(count, order_ref, x_ref, gains_ref, first_ref, second_ref, grad_ref, *refs):
    weight_refs = refs[:count]
    out_ref, w_ref, sems = refs[count:]

    @pl.when(pl.program_id(0) == 0)
    def _():
        load_weights(weight_refs, w_ref, sems)

    unit, scale = normalized(x_ref[...].astype(F32))
    half = order_ref[0]
    grad_normed = dot(first_ref[...], w_ref[half, :, :QKV_HALF], 1, 1) + dot(
        second_ref[...], w_ref[1 - half, :, :QKV_HALF], 1, 1
    )
    out_ref[...] = grad_ref[...] + norm_back(grad_normed, unit, scale, gains_ref[0:1, :])


def input_grad(half, tokens, gains, weights, first, second, grad):
    count = tokens.shape[0]
    size = min(256, count)
    operands = weights.operands()
    return pl.pallas_call(
        partial(input_grad_kernel, len(operands)),
        grid=(count // size,),
        in_specs=[
            SMEM,
            rows((size, D)),
            whole((16, D)),
            rows((size, QKV_HALF)),
            rows((size, QKV_HALF)),
            rows((size, D)),
            *weights.specs(),
        ],
        out_specs=rows((size, D)),
        out_shape=jax.ShapeDtypeStruct((count, D), F32),
        scratch_shapes=weights.scratch(),
        compiler_params=params(12),
        cost_estimate=COST,
        name="input_grad",
    )(jnp.reshape(half, (1,)).astype(jnp.int32), tokens, gains, first, second, grad, *operands)


TILE = 256


def store_slots(slots_ref, out_ref, product):
    step = CHIP_ROWS
    for index in range(D // step):
        place = pl.multiple_of(slots_ref[1 + index] * step, 16)
        out_ref[pl.ds(place, step), :] = product[index * step : (index + 1) * step].astype(BF)


def weight_products(slots_ref, out_ref, turned, grad_ref, first, size):
    for tile in range(0, size, TILE):
        width = min(TILE, size - tile)
        product = dot(turned, grad_ref[:, tile : tile + width])
        for index in range(D // CHIP_ROWS):
            place = pl.multiple_of(slots_ref[1 + index] * CHIP_ROWS, 16)
            out_ref[pl.ds(place, CHIP_ROWS), first + tile : first + tile + width] = product[
                index * CHIP_ROWS : (index + 1) * CHIP_ROWS
            ].astype(BF)


def mixed_weight_kernel(slots_ref, normed_ref, grad_ref, mixed_ref, low_ref, *rest):
    out_ref = rest[-1]
    weight_products(slots_ref, out_ref, normed_ref[...].T, grad_ref, 0, QKV_HALF)
    lanes = pl.ds(pl.multiple_of(slots_ref[0] * GROUP, LANES), GROUP)
    weight_products(slots_ref, out_ref, mixed_ref[...].T, low_ref.at[:, lanes], QKV_HALF, GROUP)


def mixed_weight_grad(slots, normed, dqkv, mixed, low, after=()):
    count = normed.shape[0]
    return pl.pallas_call(
        mixed_weight_kernel,
        in_specs=[SMEM, *[VMEM] * 4, *[ANY for _ in after]],
        out_specs=VMEM,
        out_shape=jax.ShapeDtypeStruct((D, MIXED_HALF), BF),
        compiler_params=params(8),
        cost_estimate=COST,
        name="mixed_weight_grad",
    )(slots, normed, dqkv, mixed, low, *after)


def ff_weight_kernel(slots_ref, normed_ref, cot_ref, both_ref, hidden_ref, *rest):
    out_ref = rest[-1]

    @pl.when(slots_ref[0] == 0)
    def _():
        left = both_ref.at[:, 0:FF_HALF]
        weight_products(slots_ref, out_ref, normed_ref[...].T, left, 0, FF_HALF)

    @pl.when(slots_ref[0] == 1)
    def _():
        left = both_ref.at[:, FF_HALF : 2 * FF]
        weight_products(slots_ref, out_ref, normed_ref[...].T, left, 0, FF_LEFT)
        weight_products(slots_ref, out_ref, cot_ref[...].T, hidden_ref, FF_LEFT, FF)
        out_ref[:, FF_LEFT + FF :] = jnp.zeros((D, FF_HALF - FF_LEFT - FF), BF)


def ff_weight_grad(slots, normed, cot, both, hidden, after):
    count = normed.shape[0]
    return pl.pallas_call(
        ff_weight_kernel,
        in_specs=[SMEM, *[VMEM] * 4, *[ANY for _ in after]],
        out_specs=VMEM,
        out_shape=jax.ShapeDtypeStruct((D, FF_HALF), BF),
        compiler_params=params(8),
        cost_estimate=COST,
        name="ff_weight_grad",
    )(slots, normed, cot, both, hidden, *after)


def join_kernel(*refs):
    out_ref = refs[-1]
    first = 0
    for ref in refs[:-1]:
        out_ref[first : first + ref.shape[0], :] = ref[...]
        first += ref.shape[0]


def join(*parts):
    count = sum(part.shape[0] for part in parts)
    width = parts[0].shape[1]
    return pl.pallas_call(
        join_kernel,
        in_specs=[VMEM for _ in parts],
        out_specs=VMEM,
        out_shape=jax.ShapeDtypeStruct((count, width), parts[0].dtype),
        compiler_params=params(8),
        cost_estimate=COST,
        name="join",
    )(*parts)


def doc_marks(doc_lengths, row_count):
    me = lax.axis_index("tok")
    ends = jnp.cumsum(doc_lengths).astype(jnp.int32)
    before = jnp.where(me > 0, ends[jnp.maximum(me - 1, 0)], 0)
    return jnp.stack([before, ends[me], ends[me + 1], me * row_count]).astype(jnp.int32)


def rotary_tables(marks, row_count):
    place = marks[3] + jnp.arange(row_count, dtype=jnp.int32)
    offset = place - jnp.where(place >= marks[1], marks[1], marks[0])
    frequency = 10000.0 ** (-jnp.arange(0, HEAD_DIM, 2, dtype=F32) / HEAD_DIM)
    angles = offset.astype(F32)[:, None] * frequency[None, :]
    cosine = jnp.cos(angles)
    sine = jnp.sin(angles)
    return (
        jnp.concatenate([cosine] * 4, axis=1),
        jnp.concatenate([-sine, sine, -sine, sine], axis=1),
    )


def passed_along(value, steps):
    count = lax.axis_size("tok")
    first, last = (max(0, -steps), min(count, count - steps))
    return lax.ppermute(value, "tok", [(at, at + steps) for at in range(first, last)])


STAGED_DEVICES = 32


def staged():
    return lax.axis_size("tok") == STAGED_DEVICES


def exchange(value, by_core):
    pairs = [(at, at ^ by_core[at & 1]) for at in range(lax.axis_size("tok"))]
    return lax.ppermute(value, "tok", pairs)


CORE = (1, 1)
DEEP = tuple((step << 3, step << 3) for step in range(4))
NEAR = (2, 4)
FAR = (4, 2)


def slot_codes(core):
    slot = jnp.arange(16, dtype=jnp.int32)
    depth, near, far = (slot & 3, (slot >> 2) & 1, slot >> 3)
    return (depth << 2) | jnp.where(core == 0, (far << 1) | near, (near << 1) | far)


def chip_slots(chip, core):
    code = jnp.arange(16, dtype=jnp.int32) ^ chip
    depth, second, first = (code >> 2, (code >> 1) & 1, code & 1)
    return depth | jnp.where(core == 0, (second << 3) | (first << 2), (first << 3) | (second << 2))


def stage_after(value, *others):
    return lax.optimization_barrier((value, *others))[0]


def in_hbm(value):
    return pltpu.with_memory_space_constraint(value, pltpu.HBM)


def core_pieces(shard):
    core = lax.axis_index("tok") & 1
    half = shard.shape[1] // 2
    keep = jnp.where(core == 0, shard[:, :half], shard[:, half:])
    send = jnp.where(core == 0, shard[:, half:], shard[:, :half])
    came = exchange(send, CORE)
    return jnp.concatenate(
        [jnp.where(core == 0, keep, came), jnp.where(core == 0, came, keep)], axis=0
    )


def final_gather(held, far):
    me = lax.axis_index("tok")
    core = me & 1
    chip = me >> 1
    places = jnp.concatenate(
        [slot_codes(core) ^ chip, slot_codes(1 - core) ^ chip, jnp.full((1,), core, jnp.int32)]
    )
    return Weights([held, far, exchange(held, CORE), exchange(far, CORE)], places)


def whole_weights(shard):
    full = lax.all_gather(shard, "tok", axis=0, tiled=True)
    half = full.shape[1] // 2
    return Weights([jnp.stack([full[:, :half], full[:, half:]])])


def added(left, right):
    return (left.astype(F32) + right.astype(F32)).astype(BF)


def core_sum(keep, came):
    return added(keep[:384], came[:384]), added(keep[384:], came[384:])


def far_sum(near, came):
    return added(near[:192], came[:192]), added(near[192:], came[192:])


def near_sum(near, came):
    return [
        added(near[first : first + CHIP_ROWS], came[first : first + CHIP_ROWS])
        for first in range(0, 192, CHIP_ROWS)
    ]


def deep_sum(parts, *after):
    core = lax.axis_index("tok") & 1
    total = parts[0].astype(F32)
    for step in (1, 2, 3):
        total = total + stage_after(exchange(parts[step], DEEP[step]), after[step - 1]).astype(F32)
    share = CHIP_ROWS // 2
    lower, upper = (total[:share], total[share:])
    own = jnp.where(core == 0, lower, upper)
    came = exchange(jnp.where(core == 0, upper, lower), CORE)
    return jnp.concatenate(
        [jnp.where(core == 0, own, came), jnp.where(core == 0, came, own)], axis=1
    )


def summed(keep, send):
    full = jnp.concatenate([keep, send], axis=1)
    return lax.psum_scatter(full.astype(F32), "tok", scatter_dimension=0, tiled=True)


def by_part(groups):
    return jnp.concatenate(
        [
            groups[:, half * MIXED_HALF + part * GROUP : half * MIXED_HALF + (part + 1) * GROUP]
            for part in range(3)
            for half in range(2)
        ],
        axis=1,
    )


def on_device(
    tokens,
    doc_lengths,
    first_gain,
    qkv_weight,
    attn_weight,
    second_gain,
    feed_in_weight,
    feed_out_weight,
    cotangent,
):
    row_count = tokens.shape[0]
    share = first_gain.shape[0]

    def spread(gain):
        return jnp.broadcast_to(gain[:, None], (share, LANES))

    def group_of(half):
        return [
            qkv_weight[:, part * D + half * GROUP : part * D + (half + 1) * GROUP]
            for part in range(3)
        ]

    shard_one = jnp.concatenate(
        [*group_of(0), spread(first_gain), *group_of(1), spread(second_gain)], axis=1
    )
    shard_two = jnp.concatenate([feed_in_weight, feed_out_weight.T, attn_weight], axis=1)
    weights_two = lax.all_gather(shard_two, "tok", axis=0, tiled=True)
    if staged():
        piece = core_pieces(shard_one)
        marks = doc_marks(stage_after(doc_lengths, piece), row_count)
        cosine, sine = rotary_tables(marks, row_count)
        came = [exchange(piece, DEEP[step]) for step in (1, 2, 3)]
        *came, marks = lax.optimization_barrier((*came, marks, cosine, sine))[:4]
        one = join(piece, *came)
        one = join(one, exchange(one, NEAR))
        weights_one = final_gather(one, exchange(one, FAR))
    else:
        marks = doc_marks(doc_lengths, row_count)
        cosine, sine = rotary_tables(marks, row_count)
        weights_one = whole_weights(shard_one)
    normed, qkv, gains = project_qkv(tokens, weights_one, in_hbm(cosine), in_hbm(sine))
    lower = passed_along(qkv[:, row_count - HALF :, GROUP:], 1)
    upper = passed_along(qkv[:, :HALF, GROUP:], -1)
    mixed, logs = attend_inner(marks, qkv)
    mixed, edge_logs = attend_edges(marks, qkv, lower, upper, mixed)
    residual, normed_two, both, hidden = dense(tokens, in_hbm(mixed), cotangent, gains, in_hbm(weights_two))
    me = lax.axis_index("tok")
    if staged():
        halves = (1 - (me & 1), me & 1)
    else:
        halves = (jnp.int32(1), jnp.int32(0))

    def order(half):
        if staged():
            slots = chip_slots(me >> 1, half)
        else:
            slots = jnp.arange(D // CHIP_ROWS, dtype=jnp.int32)
        return jnp.concatenate([jnp.reshape(half, (1,)).astype(jnp.int32), slots])

    def ff_grad(half, after):
        return ff_weight_grad(order(half), normed_two, cotangent, both, hidden, after)

    def inner(half, after):
        return inner_back(
            half, marks, qkv, mixed_grad, logs, cosine, sine, edge_grad, edge_sum, after
        )

    def patched(half, grads):
        return patch(half, cosine, sine, edge_sum, from_lower, from_upper, grads)

    def finish(first, second):
        return input_grad(halves[0], tokens, gains, weights_one, first, second, grad)

    send, keep = halves
    def mixed_weight(half, dqkv):
        return mixed_weight_grad(order(half), normed, dqkv, mixed, low)

    ff_send = ff_grad(send, [])
    ff_keep = ff_grad(keep, [ff_send])
    low, mixed_grad, grad = dense_back(residual, cotangent, both, gains, weights_two, [ff_keep])
    if staged():
        near, far = core_sum(ff_keep, stage_after(exchange(ff_send, CORE), mixed_grad))
        mixed_grad = stage_after(mixed_grad, far)
    edge_grad, edge_sum, away = edge_back(marks, qkv, mixed_grad, edge_logs, cosine, sine, lower, upper)
    from_lower = passed_along(away[1], 1)
    from_upper = passed_along(away[0], -1)

    if staged():
        first = inner(send, [])
        from_lower, from_upper, first = lax.optimization_barrier((from_lower, from_upper, first))
        near, far = far_sum(near, stage_after(exchange(far, FAR), from_lower, from_upper))
        first = patched(send, stage_after(first, far))
        mixed_send = mixed_weight(send, first)
        second = inner(keep, [mixed_send])
        parts = near_sum(near, stage_after(exchange(far, NEAR), second))
        second = patched(keep, stage_after(second, *parts))
        mixed_keep = mixed_weight(keep, second)
        mixed_near, mixed_far = core_sum(mixed_keep, exchange(stage_after(mixed_send, second), CORE))
        grad_in = finish(first, stage_after(second, mixed_far))
        mixed_near, mixed_far = far_sum(mixed_near, stage_after(exchange(mixed_far, FAR), grad_in))
        sum_ff = deep_sum(parts, *[mixed_far] * 3)
        result = result_of(residual, hidden, weights_two, [mixed_far])
        mixed_parts = near_sum(mixed_near, stage_after(exchange(mixed_far, NEAR), result))
        sum_mixed = deep_sum(mixed_parts, *[mixed_parts[0]] * 3)
    else:
        first = patched(send, inner(send, []))
        second = patched(keep, inner(keep, []))
        result = result_of(residual, hidden, weights_two, [])
        grad_in = finish(first, second)
        sum_ff = summed(ff_keep, ff_send)
        sum_mixed = summed(mixed_weight(keep, second), mixed_weight(send, first))
    sum_qkv = by_part(sum_mixed)
    sent_attn = jnp.concatenate(
        [sum_mixed[:, QKV_HALF:MIXED_HALF], sum_mixed[:, MIXED_HALF + QKV_HALF :]], axis=1
    )
    sent_in = jnp.concatenate(
        [sum_ff[:, :FF_HALF], sum_ff[:, FF_HALF : FF_HALF + FF_LEFT]], axis=1
    )
    sent_down = sum_ff[:, FF_HALF + FF_LEFT : FF_HALF + FF_LEFT + FF].T

    def gain_grad(summed, weight, gain):
        return jnp.sum(summed * weight.astype(F32), axis=1) / gain.astype(F32)

    return (
        result,
        grad_in,
        gain_grad(sum_qkv, qkv_weight, first_gain),
        sum_qkv,
        sent_attn,
        gain_grad(sent_in, feed_in_weight, second_gain),
        sent_in,
        sent_down,
    )


def solution(mesh):
    in_specs = (
        P("tok", None),
        P(),
        P("tok"),
        P("tok", None),
        P("tok", None),
        P("tok"),
        P("tok", None),
        P(None, "tok"),
        P("tok", None),
    )
    out_specs = (
        P("tok", None),
        P("tok", None),
        P("tok"),
        P("tok", None),
        P("tok", None),
        P("tok"),
        P("tok", None),
        P(None, "tok"),
    )
    return jax.shard_map(
        on_device, mesh=mesh, in_specs=in_specs, out_specs=out_specs, check_vma=False
    )
```
